32 devices in a mesh: pipe: 2 (over core), dp: 4 (over y, x), seq: 4 (over z).
Axes of the slice: x: 2, y: 2, z: 4, core: 2. Of those that a mesh axis runs over, the one named last changes fastest.
Arguments:
- inputs: bfloat16 [8, 4096, 768], P('dp', 'seq'), may hold values from -6 to 6
- cotangent: bfloat16 [8, 4096, 768], P('dp', 'seq'), may hold values from -6 to 6
- in_weight: bfloat16 [2, 768, 3072], P('pipe'), may hold values from -0.21875 to 0.21875
- in_bias: float32 [2, 3072], P('pipe'), may hold values from -1.5 to 1.5
- out_weight: bfloat16 [2, 3072, 768], P('pipe'), may hold values from -0.109375 to 0.109375
- out_bias: float32 [2, 768], P('pipe'), may hold values from -1.5 to 1.5
- mix_gain: float32 [2, 768], P('pipe'), may hold values from 0.25 to 1.75
- mix_shift: float32 [2, 768], P('pipe'), may hold values from -1.5 to 1.5
- out_gain: float32 [2, 768], P('pipe'), may hold values from 0.25 to 1.75
- out_shift: float32 [2, 768], P('pipe'), may hold values from -1.5 to 1.5
Outputs:
- output: bfloat16 [8, 4096, 768], P('dp', 'seq', 'pipe')
- input_grad: bfloat16 [8, 4096, 768], P('dp', 'seq', 'pipe')
- in_weight_grad: float32 [2, 768, 3072], P('pipe')
- in_bias_grad: float32 [2, 3072], P('pipe')
- out_weight_grad: float32 [2, 3072, 768], P('pipe')
- out_bias_grad: float32 [2, 768], P('pipe')
- mix_gain_grad: float32 [2, 768], P('pipe')
- mix_shift_grad: float32 [2, 768], P('pipe')
- out_gain_grad: float32 [2, 768], P('pipe')
- out_shift_grad: float32 [2, 768], P('pipe')
The draws below stay inside these ranges and needn't reach their ends.
All inputs are finite; a program needn't handle non-finite values.
Results may differ from the reference program's by a relative error of at most 0.014.
Values may be sent and summed in bfloat16 or wider, within the bound.
No kernel may reach another device: no remote copies, remote signals or barrier semaphores. Data moves between devices by JAX's collectives and lax.ppermute only.
A program may use at most 448 MiB of HBM per device.

```python
import math
import jax
import jax.numpy as jnp
from jax import lax

D = 768
FF = 3072
L = 4096
LAYERS = 2
ITEMS = 8


def level_of(stream_key, dims, split, smallest, top_value):
    factor_of = 1.0
    for axis_at, shards_of in split:
        draws = jax.random.uniform(jax.random.fold_in(jax.random.fold_in(stream_key, 6), axis_at), (shards_of,), jnp.float32, smallest / len(split), top_value / len(split))
        factor_of = factor_of * jnp.repeat(jnp.exp(draws), dims[axis_at] // shards_of).reshape((-1,) + (1,) * (len(dims) - 1 - axis_at))
    return factor_of


def normal_values(key, shape, deviation, bound, split=(), kind=jnp.bfloat16):
    level = level_of(key, shape, split, -0.22, 0.18) if split else 1.0
    values = jax.random.normal(key, shape, jnp.float32) * deviation * level
    return jnp.minimum(jnp.maximum(values, -bound), bound).astype(kind)


def setup_inputs(seed: int = 0) -> dict:
    seeds = jax.random.split(jax.random.key(seed), 11)
    return {
        "inputs": normal_values(seeds[0], (ITEMS, L, D), 1.0, 6.0, ((0, 4), (1, 4))),
        "cotangent": normal_values(seeds[1], (ITEMS, L, D), 1.0, 6.0, ((0, 4), (1, 4))),
        "in_weight": normal_values(seeds[2], (LAYERS, D, FF), D ** -0.5, 0.21875, ((0, 2),)),
        "in_bias": normal_values(seeds[3], (LAYERS, FF), 0.3, 1.5, ((0, 2),), jnp.float32),
        "out_weight": normal_values(seeds[4], (LAYERS, FF, D), FF ** -0.5, 0.109375, ((0, 2),)),
        "out_bias": normal_values(seeds[5], (LAYERS, D), 0.3, 1.5, ((0, 2),), jnp.float32),
        "mix_gain": jnp.clip(1.0 + 0.15 * jax.random.normal(seeds[6], (LAYERS, D), jnp.float32), 0.25, 1.75),
        "mix_shift": normal_values(seeds[7], (LAYERS, D), 0.3, 1.5, ((0, 2),), jnp.float32),
        "out_gain": jnp.clip(1.0 + 0.15 * jax.random.normal(seeds[8], (LAYERS, D), jnp.float32), 0.25, 1.75),
        "out_shift": normal_values(seeds[9], (LAYERS, D), 0.3, 1.5, ((0, 2),), jnp.float32),
    }


@jax.custom_vjp
def low(v):
    return lax.optimization_barrier(v.astype(jnp.bfloat16)).astype(jnp.float32)

@jax.custom_vjp
def low_back(v):
    return v

def low_keep(v):
    return (low(v), None)

def low_pass(kept, grad):
    return (grad,)

def back_keep(v):
    return (v, None)

def back_low(kept, grad):
    return (low(grad),)
low.defvjp(low_keep, low_pass)
low_back.defvjp(back_keep, back_low)

def rounded_both(value):
    return low_back(low(value))

def phase_tables(length):
    positions = jnp.arange(length, dtype=jnp.int32)
    phases = positions[:, None] * positions[None, :] % length
    angles = phases.astype(jnp.float32) * (2.0 * math.pi / length)
    return (low(jnp.cos(angles)), low(jnp.sin(angles)))

def normalize(hidden, gain, shift):
    centered = hidden - lax.optimization_barrier(jnp.mean(hidden, axis=-1, keepdims=True))
    spread = lax.optimization_barrier(jnp.mean(centered * centered, axis=-1, keepdims=True))
    return centered * lax.rsqrt(spread + 1e-05) * gain + shift

def layer(layer_in, params, hidden_table, cos_table, sin_table):
    highest = lax.Precision.HIGHEST
    width = layer_in.shape[1]
    length = layer_in.shape[0]
    layer_in = low_back(layer_in)
    spectra = rounded_both(jnp.dot(layer_in, hidden_table, precision=highest) * (1.0 / math.sqrt(width)))
    mixture = jnp.dot(cos_table, spectra[:, :width], precision=highest) + jnp.dot(sin_table, spectra[:, width:], precision=highest)
    mixture = rounded_both(mixture * (1.0 / math.sqrt(length)))
    normed = normalize(layer_in + mixture, params[4], params[5])
    pre_act = low_back(jnp.dot(low(normed), params[0], precision=highest) + params[1])
    activation = low(jax.nn.gelu(pre_act, approximate=False))
    branch = low_back(jnp.dot(activation, params[2], precision=highest) + params[3])
    return low(normalize(normed + branch, params[6], params[7]))

def reference(inputs, cotangent, in_weight, in_bias, out_weight, out_bias, mix_gain, mix_shift, out_gain, out_shift):
    hidden_cos, hidden_sin = phase_tables(D)
    hidden_table = jnp.concatenate([hidden_cos, -hidden_sin], axis=1)
    cos_table, sin_table = phase_tables(L)
    params = tuple((weight.astype(jnp.float32) for weight in (in_weight, in_bias, out_weight, out_bias, mix_gain, mix_shift, out_gain, out_shift)))

    def forward(items, weights):
        first_params = tuple((weight[0] for weight in weights))
        second_params = tuple((weight[1] for weight in weights))

        def one_item(item):
            middle = layer(item, first_params, hidden_table, cos_table, sin_table)
            return layer(middle, second_params, hidden_table, cos_table, sin_table)
        return lax.map(jax.checkpoint(one_item), items)
    result, pull = jax.vjp(forward, inputs.astype(jnp.float32), params)
    input_grad, weight_grads = pull(cotangent.astype(jnp.float32))
    return (result.astype(jnp.bfloat16), input_grad.astype(jnp.bfloat16), weight_grads[0], weight_grads[1], weight_grads[2], weight_grads[3], weight_grads[4], weight_grads[5], weight_grads[6], weight_grads[7])
```

```python
import math

import jax
import jax.numpy as jnp
from jax import lax
from jax.experimental import pallas as pl
from jax.experimental.pallas import tpu as pltpu
from jax.sharding import PartitionSpec as P

BF = jnp.bfloat16
F32 = jnp.float32
PAD = 16
ROWS = 256
CHUNK = 768


def product(left, right):
    return jnp.dot(left, right, preferred_element_type=F32)


def contract(left, right, left_dim, right_dim):
    dims = (((left_dim,), (right_dim,)), ((), ()))
    return lax.dot_general(left, right, dims, preferred_element_type=F32)


def swap_cores(value):
    return lax.ppermute(value, "pipe", [(0, 1), (1, 0)])


def turn(phase, length):
    angles = (phase % length).astype(F32) * (2.0 * math.pi / length)
    return jnp.cos(angles), jnp.sin(angles)


def column_sets(width):
    quarter, half = width // 4, width // 2
    return (
        (list(range(quarter)) + [half], list(range(1, quarter))),
        (list(range(quarter, half)), list(range(quarter, half))),
    )


def feature_tables(width, core):
    sets = column_sets(width)
    order = []
    for cos_ids, sin_ids in sets:
        order.append(([k for k in cos_ids] + [k for k in sin_ids], [0] * len(cos_ids) + [1] * len(sin_ids)))
    ids_a = jnp.array(order[0][0] + order[1][0], jnp.int32)
    ids_b = jnp.array(order[1][0] + order[0][0], jnp.int32)
    odd_a = jnp.array(order[0][1] + order[1][1], jnp.int32)
    odd_b = jnp.array(order[1][1] + order[0][1], jnp.int32)
    first = core == 0
    ids = jnp.where(first, ids_a, ids_b)
    odd = jnp.where(first, odd_a, odd_b)
    sign = jnp.where(first, 1.0, -1.0)
    rows = jnp.arange(width, dtype=jnp.int32)
    cos, sin = turn(rows[:, None] * ids[None, :], width)
    spread = jnp.where(odd[None, :] == 1, -sign * sin, cos).astype(BF)
    direct = rows[None, :] == ids[:, None]
    mirror = rows[None, :] == ((width - ids) % width)[:, None]
    even_rows = (direct | mirror).astype(F32)
    odd_rows = sign * (direct.astype(F32) - mirror.astype(F32))
    unfold = jnp.where(odd[:, None] == 1, odd_rows, even_rows).astype(BF)
    return spread, unfold


def token_tables(block, rows, blocks, length):
    tall = rows + PAD
    inner = jnp.arange(tall, dtype=jnp.int32)
    slots = jnp.arange(blocks, dtype=jnp.int32)
    columns = ((block + blocks - slots) % blocks * rows)[:, None, None] + inner
    coarse = block * rows + PAD * jnp.arange(tall // PAD, dtype=jnp.int32)
    fine = jnp.arange(PAD, dtype=jnp.int32)
    cos_c, sin_c = turn(coarse[:, None] * columns, length)
    cos_f, sin_f = turn(fine[:, None] * columns, length)
    cos_c, sin_c, cos_f, sin_f = cos_c[:, :, None], sin_c[:, :, None], cos_f[:, None], sin_f[:, None]
    cos = (cos_c * cos_f - sin_c * sin_f).astype(BF)
    sin = (sin_c * cos_f + cos_c * sin_f).astype(BF)
    return cos.reshape(blocks, tall, tall), sin.reshape(blocks, tall, tall)


def row_block(height, width):
    return pl.BlockSpec((height, width), lambda i: (i, 0))


def whole(*shape):
    return pl.BlockSpec(shape, lambda *_: (0,) * len(shape), pipeline_mode=pl.Buffered(1))


def scalar_block():
    return pl.BlockSpec(memory_space=pltpu.SMEM)


def layer_block(layer, *shape):
    return pl.BlockSpec((1, *shape), lambda i: (layer,) + (0,) * len(shape), pipeline_mode=pl.Buffered(1))


def call(body, grid, in_specs, out_specs, out_shape, flops, moved, name, vmem):
    return pl.pallas_call(
        body,
        grid=grid,
        in_specs=in_specs,
        out_specs=out_specs,
        out_shape=out_shape,
        compiler_params=pltpu.CompilerParams(vmem_limit_bytes=vmem << 20),
        cost_estimate=pl.CostEstimate(flops=flops, bytes_accessed=moved, transcendentals=0),
        name=name,
    )


def like(*shape, dtype=BF):
    return jax.ShapeDtypeStruct(shape, dtype)


def divisor(count, most):
    return max(d for d in range(1, most + 1) if count % d == 0)


def fold_spectra(core, own, recv):
    rows, half = own.shape

    def body(core_ref, own_ref, recv_ref, out_ref):
        first = core_ref[0] == 0
        out_ref[:rows] = (own_ref[...].astype(F32) + recv_ref[...].astype(F32)).astype(BF)
        mine, theirs = own_ref[:PAD], recv_ref[:PAD]
        at = lax.broadcasted_iota(jnp.int32, (PAD, half), 0)
        low = jnp.where(first, mine, theirs)
        high = jnp.where(first, theirs, mine)
        out_ref[:PAD] = jnp.where(at == 0, low, out_ref[:PAD])
        out_ref[rows:] = jnp.where(at == 0, high, jnp.zeros_like(high))

    spec = pl.BlockSpec((rows, half), lambda i: (0, 0))
    return call(
        body,
        (1,),
        [scalar_block(), spec, spec],
        pl.BlockSpec((rows + PAD, half), lambda i: (0, 0)),
        like(rows + PAD, half),
        rows * half,
        6 * rows * half,
        "fold_spectra",
        8,
    )(core, own, recv)


def transform_part(cos, sin, slot, part):
    tall, half = part.shape
    wide = -(-(half // 2 + 1) // 128) * 128
    tile = divisor(tall // PAD, 17) * PAD

    def body(cos_ref, sin_ref, part_ref, out_ref):
        out_ref[:, :wide] = product(cos_ref[0], part_ref[:, :wide])
        out_ref[:, wide:] = product(sin_ref[0], part_ref[:, half - wide :])

    table = pl.BlockSpec((1, tile, tall), lambda i: (slot, i, 0))
    return call(
        body,
        (tall // tile,),
        [table, table, whole(tall, half)],
        row_block(tile, 2 * wide),
        like(tall, 2 * wide, dtype=F32),
        4 * tall * tall * wide,
        4 * tall * (tall + 2 * wide),
        "transform_part",
        12,
    )(cos, sin, part)


def transform_rest(core, cos, sin, begun, parts, factor):
    tall, half = parts[0].shape
    wide = begun.shape[1] // 2
    tile = divisor(tall // PAD, 17) * PAD
    lead = half - wide

    def body(*refs):
        core_ref, begun_ref = refs[:2]
        tables = refs[2 : 2 + 2 * len(parts)]
        part_refs = refs[2 + 2 * len(parts) : -1]
        out_ref = refs[-1]
        even, odd = begun_ref[:, :wide], begun_ref[:, wide:]
        for at, part_ref in enumerate(part_refs):
            even = even + product(tables[2 * at][0], part_ref[:, :wide])
            odd = odd + product(tables[2 * at + 1][0], part_ref[:, lead:])
        lanes = lax.broadcasted_iota(jnp.int32, (tile, wide - lead), 1) + lead
        cos_count = half // 2 + 1 - core_ref[0]
        middle = jnp.where(lanes < cos_count, even[:, lead:], odd[:, : wide - lead])
        out_ref[:, :lead] = (even[:, :lead] * factor).astype(BF)
        out_ref[:, lead:wide] = (middle * factor).astype(BF)
        out_ref[:, wide:] = (odd[:, wide - lead :] * factor).astype(BF)

    tables, specs = [], []
    for at in range(len(parts)):
        spec = pl.BlockSpec((1, tile, tall), lambda i, at=at: (at + 1, i, 0))
        tables += [cos, sin]
        specs += [spec, spec]
    return call(
        body,
        (tall // tile,),
        [scalar_block(), row_block(tile, 2 * wide)] + specs + [whole(tall, half)] * len(parts),
        row_block(tile, half),
        like(tall, half),
        4 * tall * tall * wide * len(parts),
        4 * tall * (tall * len(parts) + 2 * wide),
        "transform_rest",
        14,
    )(core, begun, *tables, *parts)


def transform(core, own, recv, cos, sin, group_shifts, factor, beside=None):
    folded = fold_spectra(core, own, recv)
    parts = [lax.ppermute(folded, "seq", pairs) for pairs in group_shifts]
    begun = transform_part(cos, sin, 0, folded)
    mixed = transform_rest(core, cos, sin, begun, parts, factor)
    return mixed, swap_cores(mixed)


def standardize(hidden):
    centered = hidden - jnp.mean(hidden, axis=-1, keepdims=True)
    spread = jnp.mean(centered * centered, axis=-1, keepdims=True)
    scale = lax.rsqrt(spread + 1e-05)
    return centered * scale, scale


def standardize_back(grad, unit, scale):
    mean_grad = jnp.mean(grad, axis=-1, keepdims=True)
    mean_both = jnp.mean(grad * unit, axis=-1, keepdims=True)
    return (grad - mean_grad - unit * mean_both) * scale


def mixture_tile(core_ref, mine_ref, mine_top, theirs_ref, theirs_top, unfold_ref):
    tile, half = mine_ref.shape
    at = lax.broadcasted_iota(jnp.int32, (tile, half), 0)
    odd_row = (at == 0) & (core_ref[0] == 1) & (pl.program_id(0) == 0)
    mine = jnp.where(odd_row, mine_top[:1], mine_ref[...])
    theirs = jnp.where(odd_row, theirs_top[:1], theirs_ref[...])
    return product(mine, unfold_ref[:half]) + product(theirs, unfold_ref[half:])


def mixture_specs(rows, half, tile):
    block = row_block(tile, half)
    top = pl.BlockSpec((PAD, half), lambda i: (rows // PAD, 0))
    return [block, top, block, top, whole(2 * half, 2 * half)]


def spectra_call(core, x, spread):
    rows, width = x.shape
    half = width // 2
    tile = min(ROWS, rows)
    factor = 1.0 / math.sqrt(width)

    def body(x_ref, spread_ref, own_ref, other_ref):
        spectra = product(x_ref[...], spread_ref[...]) * factor
        own_ref[...] = spectra[:, :half].astype(BF)
        other_ref[...] = spectra[:, half:].astype(BF)

    return call(
        body,
        (rows // tile,),
        [row_block(tile, width), whole(width, width)],
        [row_block(tile, half)] * 2,
        [like(rows, half)] * 2,
        2 * rows * width * width,
        4 * rows * width,
        "spectra",
        12,
    )(x, spread)


def forward(core, layer, x, mixed, unfold, w1, w2, b1, vec, spread):
    rows, width = x.shape
    hidden = w1.shape[2]
    half = width // 2
    tile = min(ROWS, rows)
    chunk = min(CHUNK, hidden)
    factor = 1.0 / math.sqrt(width)

    def body(core_ref, x_ref, m0, t0, m1, t1, unfold_ref, w1_ref, w2_ref, b1_ref, vec_ref, spread_ref, *outs):
        out_ref, own_ref, other_ref, low_ref, act_ref, slope_ref, unit1_ref, scale1_ref, unit2_ref, scale2_ref = outs
        mixture = mixture_tile(core_ref, m0, t0, m1, t1, unfold_ref).astype(BF).astype(F32)
        unit, scale = standardize(x_ref[...].astype(F32) + mixture)
        b2, mg, ms, og, os = (vec_ref[0, i : i + 1] for i in range(5))
        normed = unit * mg + ms
        unit1_ref[...] = unit.astype(BF)
        scale1_ref[...] = jnp.broadcast_to(scale, scale1_ref.shape)
        low = normed.astype(BF)
        low_ref[...] = low
        total = normed + b2
        for start in range(0, hidden, chunk):
            span = slice(start, start + chunk)
            pre = product(low, w1_ref[0, :, span]) + b1_ref[0, :, span]
            cdf = 0.5 + 0.5 * lax.erf(pre * (1.0 / math.sqrt(2.0)))
            act = (pre * cdf).astype(BF)
            act_ref[:, span] = act
            slope_ref[:, span] = (cdf + pre * (jnp.exp(-0.5 * pre * pre) * (1.0 / math.sqrt(2.0 * math.pi)))).astype(BF)
            total = total + product(act, w2_ref[0, span, :])
        unit, scale = standardize(total)
        unit2_ref[...] = unit.astype(BF)
        scale2_ref[...] = jnp.broadcast_to(scale, scale2_ref.shape)
        out = (unit * og + os).astype(BF)
        out_ref[...] = out
        spectra = product(out, spread_ref[...]) * factor
        own_ref[...] = spectra[:, :half].astype(BF)
        other_ref[...] = spectra[:, half:].astype(BF)

    mine, theirs = mixed
    return call(
        body,
        (rows // tile,),
        [scalar_block(), row_block(tile, width)]
        + mixture_specs(rows, half, tile)
        + [
            layer_block(layer, width, hidden),
            layer_block(layer, hidden, width),
            layer_block(layer, 1, hidden),
            layer_block(layer, 5, width),
            whole(width, width),
        ],
        [
            row_block(tile, width),
            row_block(tile, half),
            row_block(tile, half),
            row_block(tile, width),
            row_block(tile, hidden),
            row_block(tile, hidden),
            row_block(tile, width),
            row_block(tile, 128),
            row_block(tile, width),
            row_block(tile, 128),
        ],
        [
            like(rows, width),
            like(rows, half),
            like(rows, half),
            like(rows, width),
            like(rows, hidden),
            like(rows, hidden),
            like(rows, width),
            like(rows, 128, dtype=F32),
            like(rows, width),
            like(rows, 128, dtype=F32),
        ],
        4 * rows * width * (hidden + width),
        4 * width * hidden + 4 * rows * hidden + 14 * rows * width,
        "layer_forward",
        34,
    )(core, x, mine, mine, theirs, theirs, unfold, w1, w2, b1, vec, spread)


def backward(core, layer, grad, mixed, unfold, kept, w1, w2, vec, spread):
    low, act, slope, unit1, scale1, unit2, scale2 = kept
    rows, width = grad.shape
    hidden = w1.shape[2]
    half = width // 2
    tile = min(ROWS, rows)
    chunk = min(CHUNK, hidden)
    factor = 1.0 / math.sqrt(width)
    count = 0 if mixed is None else 6

    def body(*refs):
        grad_ref = refs[0]
        slope_ref, unit1_ref, scale1_ref, unit2_ref, scale2_ref, w1_ref, w2_ref, vec_ref, spread_ref = refs[1 + count : 10 + count]
        gh_ref, gb_ref, gp_ref, own_ref, other_ref, wide_ref, sums_ref = refs[10 + count :]

        @pl.when(pl.program_id(0) == 0)
        def _():
            wide_ref[...] = jnp.zeros_like(wide_ref)
            sums_ref[...] = jnp.zeros_like(sums_ref)

        grad = grad_ref[...].astype(F32)
        if count:
            grad = (grad + mixture_tile(*refs[1 : 1 + count])).astype(BF).astype(F32)
        mg, og = vec_ref[0, 1:2], vec_ref[0, 3:4]
        unit2 = unit2_ref[...].astype(F32)
        g_branch = standardize_back(grad * og, unit2, scale2_ref[:, :1])
        gb = g_branch.astype(BF)
        gb_ref[...] = gb
        total = g_branch
        for start in range(0, hidden, chunk):
            span = slice(start, start + chunk)
            g_act = contract(gb, w2_ref[0, span, :], 1, 1)
            gp = (g_act * slope_ref[:, span].astype(F32)).astype(BF)
            gp_ref[:, span] = gp
            wide_ref[:, span] += jnp.sum(gp.astype(F32), axis=0, keepdims=True)
            total = total + contract(gp, w1_ref[0, :, span], 1, 1)
        unit1 = unit1_ref[...].astype(F32)
        g_h = standardize_back(total * mg, unit1, scale1_ref[:, :1])
        gh_ref[...] = g_h
        for at, terms in enumerate((gb.astype(F32), total * unit1, total, grad * unit2, grad)):
            sums_ref[at : at + 1] += jnp.sum(terms, axis=0, keepdims=True)
        spectra = product(g_h.astype(BF), spread_ref[...]) * factor
        own_ref[...] = spectra[:, :half].astype(BF)
        other_ref[...] = spectra[:, half:].astype(BF)

    if count:
        mine, theirs = mixed
        extra = [core, mine, mine, theirs, theirs, unfold]
        extra_specs = [scalar_block()] + mixture_specs(rows, half, tile)
    else:
        extra, extra_specs = [], []
    return call(
        body,
        (rows // tile,),
        [row_block(tile, width)]
        + extra_specs
        + [
            row_block(tile, hidden),
            row_block(tile, width),
            row_block(tile, 128),
            row_block(tile, width),
            row_block(tile, 128),
            layer_block(layer, width, hidden),
            layer_block(layer, hidden, width),
            layer_block(layer, 5, width),
            whole(width, width),
        ],
        [
            row_block(tile, width),
            row_block(tile, width),
            row_block(tile, hidden),
            row_block(tile, half),
            row_block(tile, half),
            whole(1, hidden),
            whole(8, width),
        ],
        [
            like(rows, width, dtype=F32),
            like(rows, width),
            like(rows, hidden),
            like(rows, half),
            like(rows, half),
            like(1, hidden, dtype=F32),
            like(8, width, dtype=F32),
        ],
        4 * rows * width * (hidden + width),
        4 * width * hidden + 4 * rows * hidden + 14 * rows * width,
        "layer_backward",
        34,
    )(grad, *extra, slope, unit1, scale1, unit2, scale2, w1, w2, vec, spread)


def weight_grad(scalars, low, gp, act, gb, start, count, recv=None):
    rows, width = low.shape

    def body(scalar_ref, low_ref, gp_ref, act_ref, gb_ref, *refs):
        def write(value):
            if recv is None:
                refs[0][0] = value.astype(BF)
            else:
                value = (value + refs[0][0].astype(F32)).astype(BF)
                refs[1][0] = value[: width // 2]
                refs[2][0] = value[width // 2 :]

        @pl.when(scalar_ref[0] == 0)
        def _():
            write(contract(low_ref[...], gp_ref[...], 0, 0))

        @pl.when(scalar_ref[0] != 0)
        def _():
            write(contract(act_ref[...], gb_ref[...], 0, 0))

    full = pl.BlockSpec((rows, width), lambda j, s: (0, 0))
    block = pl.BlockSpec((1, width, width), lambda j, s: (j, 0, 0))
    half = pl.BlockSpec((1, width // 2, width), lambda j, s: (j, 0, 0))
    return pl.pallas_call(
        body,
        grid_spec=pltpu.PrefetchScalarGridSpec(
            num_scalar_prefetch=1,
            grid=(count,),
            in_specs=[
                full,
                pl.BlockSpec((rows, width), lambda j, s: (0, jnp.where(s[0] == 0, (j + start) ^ s[1], 0))),
                pl.BlockSpec((rows, width), lambda j, s: (0, jnp.where(s[0] == 0, 0, (j + start) ^ s[1]))),
                full,
            ]
            + ([] if recv is None else [block]),
            out_specs=block if recv is None else [half, half],
        ),
        out_shape=like(count, width, width) if recv is None else [like(count, width // 2, width)] * 2,
        compiler_params=pltpu.CompilerParams(vmem_limit_bytes=26 << 20),
        cost_estimate=pl.CostEstimate(
            flops=2 * rows * width * width * count, bytes_accessed=2 * rows * width * (count + 2) + 2 * width * width * count, transcendentals=0
        ),
        name="weight_grad",
    )(scalars, low, gp, act, gb, *([] if recv is None else [recv]))


def write_weights(scalars, first_mine, first_far, second_far, second_mine):
    count, halves, slots, piece, width = first_mine.shape
    tall = slots * piece

    def body(s, a_ref, b_ref, c_ref, d_ref, in_ref, out_ref):
        def write(source, target):
            for slot in range(slots):
                at = pl.multiple_of((s[2] + slots - slot) % slots * piece, piece)
                target[0, pl.ds(at, piece), :] = source[0, 0, slot].astype(F32)

        @pl.when(s[0] == 0)
        def _():
            write(a_ref, in_ref)
            write(b_ref, out_ref)

        @pl.when(s[0] != 0)
        def _():
            write(c_ref, in_ref)
            write(d_ref, out_ref)

    def source(core):
        return pl.BlockSpec(
            (1, 1, slots, piece, width),
            lambda q, h, s: (jnp.where(s[0] == core, q, 0), jnp.where(s[0] == core, h, 0), 0, 0, 0),
        )

    return pl.pallas_call(
        body,
        grid_spec=pltpu.PrefetchScalarGridSpec(
            num_scalar_prefetch=1,
            grid=(count, halves),
            in_specs=[source(0), source(0), source(1), source(1)],
            out_specs=[
                pl.BlockSpec((1, tall, width), lambda q, h, s: (0, h, q ^ s[1])),
                pl.BlockSpec((1, tall, width), lambda q, h, s: (0, (q ^ s[1]) * halves + h, 0)),
            ],
        ),
        out_shape=[like(1, tall * halves, width * count, dtype=F32), like(1, tall * halves * count, width, dtype=F32)],
        compiler_params=pltpu.CompilerParams(vmem_limit_bytes=20 << 20),
        cost_estimate=pl.CostEstimate(flops=0, bytes_accessed=12 * width * width * count, transcendentals=0),
        name="write_weights",
    )(scalars, first_mine, first_far, second_far, second_mine)


def finish(core, g_h, mixed, unfold):
    rows, width = g_h.shape
    half = width // 2
    tile = min(ROWS, rows)

    def body(g_ref, *refs):
        refs[-1][...] = (g_ref[...] + mixture_tile(*refs[:-1])).astype(BF)

    mine, theirs = mixed
    return call(
        body,
        (rows // tile,),
        [row_block(tile, width), scalar_block()] + mixture_specs(rows, half, tile),
        row_block(tile, width),
        like(rows, width),
        2 * rows * width * width,
        8 * rows * width,
        "finish",
        14,
    )(g_h, core, mine, mine, theirs, theirs, unfold)


def bit_pairs(count, bit):
    return [(i, i ^ (1 << bit)) for i in range(count)]


def added(left, right):
    return (left.astype(F32) + right.astype(F32)).astype(BF)


class Line:
    def __init__(self):
        self.last = None

    def __call__(self, step, *args):
        if self.last is not None:
            args, _ = lax.optimization_barrier((args, self.last))
        out = step(*args)
        self.last = min(jax.tree.leaves(out), key=lambda leaf: leaf.size)
        return out

    def after(self, value):
        return lax.optimization_barrier((value, self.last))[0]


class ChipSum:
    def __init__(self):
        self.peers = lax.axis_size("seq")
        self.z = lax.axis_index("seq")

    def across(self, bit, value):
        return lax.ppermute(value, "dp", bit_pairs(4, bit))

    def along(self, value, by):
        return lax.ppermute(value, "seq", [(i, (i + by) % self.peers) for i in range(self.peers)])

    def start_upper(self, upper):
        self.upper = upper
        self.got = [self.across(0, upper[0][1]), self.across(1, upper[1])]

    def start_lower(self, lower):
        self.lower = lower
        self.got.append(self.across(0, lower[0][1]))

    def first_sums(self):
        args = (self.upper[0], self.lower[0], self.lower[1], *self.got)
        return (lambda u, a, b, g3, g23, g1: (added(u[0], g3), added(a[0], g1), added(b[1], g23[1]), added(b[0], g23[0]))), args

    def start_second(self, sums):
        self.kept = (sums[1], sums[3])
        self.got = (self.across(1, sums[0]), self.across(0, sums[2]))

    def second_sums(self):
        def step(a, b, g0, g1, z):
            both = jnp.stack([added(a, g0), added(b, g1)])
            both = both.reshape(2, self.peers, -1, both.shape[-1])
            return [lax.dynamic_index_in_dim(both, (z + d) % self.peers, 1, keepdims=False) for d in range(self.peers)]

        return step, (*self.kept, *self.got, self.z)

    def start_scatter(self, pieces):
        self.kept = pieces[0]
        self.got = [self.along(piece, d) for d, piece in enumerate(pieces) if d]

    def scattered(self):
        def step(kept, *got):
            return sum((g.astype(F32) for g in got), kept.astype(F32)).astype(BF)

        return step, (self.kept, *self.got)

    def start_gather(self, piece):
        self.kept = piece
        self.got = [self.along(piece, d) for d in range(1, self.peers)]

    def gathered(self):
        def step(*pieces):
            return [jnp.stack([piece[at] for piece in pieces]) for at in range(2)]

        return step, (self.kept, *self.got)

    def start_back(self, halves):
        self.own = halves
        self.near = (self.across(1, halves[0]), self.across(0, halves[1]))

    def start_last(self):
        self.far = [
            (self.across(0, self.own[0]), self.across(0, self.near[0])),
            (self.across(1, self.own[1]), self.across(1, self.near[1])),
        ]

    def pieces(self):
        def step(a, b, a2, b1, a1, a3, b2, b3):
            return jnp.stack([jnp.stack([a, b]), jnp.stack([a1, b1]), jnp.stack([a2, b2]), jnp.stack([a3, b3])])

        return step, (*self.own, *self.near, *self.far[0], *self.far[1])


def small_hops():
    hops = []
    for axis in ("pipe", "seq", "dp"):
        count = lax.axis_size(axis)
        hops += [(axis, bit_pairs(count, bit)) for bit in range(count.bit_length() - 1)]
    return hops


def on_device(
    inputs,
    cotangent,
    in_weight,
    in_bias,
    out_weight,
    out_bias,
    mix_gain,
    mix_shift,
    out_gain,
    out_shift,
):
    rows, width = inputs.shape[1:]
    hidden = in_weight.shape[2]
    peers = lax.axis_size("seq")
    blocks = peers // 2
    half = width // 2
    core = lax.axis_index("pipe")
    z = lax.axis_index("seq")
    first = core == 0
    low = z < blocks
    local = low == first
    block = jnp.minimum(z, peers - 1 - z)
    which = core.astype(jnp.int32).reshape(1)

    def place(member, is_low):
        return member if is_low else peers - 1 - member

    group_shifts = [
        [(place(b, side), place((b + d) % blocks, side)) for side in (True, False) for b in range(blocks)]
        for d in range(1, blocks)
    ]
    in_pairs = []
    out_pairs = ([], [])
    for i in range(peers):
        facing = peers - 1 - i
        source = peers + i if i < blocks else i
        in_pairs.append((source, facing if i < blocks else peers + facing))
        out_pairs[0].append((source, facing))
        out_pairs[1].append((source, peers + facing))

    row_ids = lax.broadcasted_iota(jnp.int32, (rows, rows), 0)
    col_ids = lax.broadcasted_iota(jnp.int32, (rows, rows), 1)
    order = (col_ids == jnp.where(first, row_ids, (rows - row_ids) % rows)).astype(BF)

    def send_in(items):
        sent = jnp.where(low, items[1], items[0])
        kept = jnp.where(low, items[0], items[1])
        return kept, lax.ppermute(sent, ("pipe", "seq"), in_pairs)

    def arranged(kept, moved):
        return product(order, jnp.where(local, kept, moved)).astype(BF)

    def give_start(value):
        mine = jnp.where(first, value[:, :half], value[:, half:])
        theirs = jnp.where(first, value[:, half:], value[:, :half])
        return (
            mine,
            swap_cores(theirs),
            lax.ppermute(value[:, :half], ("pipe", "seq"), out_pairs[0]),
            lax.ppermute(value[:, half:], ("pipe", "seq"), out_pairs[1]),
        )

    def give_end(moved):
        mine, beside, far0, far1 = moved
        near_part = jnp.where(local, mine, beside)
        far_part = jnp.where(first, far0, far1)
        return jnp.stack([jnp.where(low, near_part, far_part), jnp.where(low, far_part, near_part)])

    x = arranged(*send_in(inputs))
    vectors = jnp.concatenate([in_bias[0], out_bias[0], mix_gain[0], mix_shift[0], out_gain[0], out_shift[0]])
    other_vectors = swap_cores(vectors)
    vectors = jnp.where(first, jnp.stack([vectors, other_vectors]), jnp.stack([other_vectors, vectors]))
    b1 = vectors[:, :hidden].reshape(2, 1, hidden)
    vec = vectors[:, hidden:].reshape(2, 5, width)
    w1 = lax.all_gather(in_weight, "pipe", axis=0, tiled=True)
    w2 = lax.all_gather(out_weight, "pipe", axis=0, tiled=True)
    spread, unfold = feature_tables(width, core)
    cos, sin = token_tables(block, rows, blocks, rows * peers)
    factor = 1.0 / math.sqrt(rows * peers)

    line = Line()

    def fold(own, other):
        folded = line(lambda a, b: fold_spectra(which, a, b), own, swap_cores(other))
        return folded, [lax.ppermute(folded, "seq", pairs) for pairs in group_shifts]

    def part(folded):
        return line(lambda f: transform_part(cos, sin, 0, f), folded)

    def rest(begun, parts):
        mixed = line(lambda a, *b: transform_rest(which, cos, sin, a, list(b), factor), begun, *parts)
        return mixed, swap_cores(mixed)

    kept = []
    own, other = line(lambda v: spectra_call(which, v, spread), x)
    for layer in range(2):
        folded, parts = fold(own, other)
        begun = part(folded)
        if layer == 1:
            grad = line(lambda v, w: arranged(v, w), *cot)
        mixed = rest(begun, parts)
        if layer == 0:
            cot = send_in(line.after(cotangent))
        x, own, other, *saved = line(
            lambda v, m, l=layer: forward(which, l, v, m, unfold, w1, w2, b1, vec, spread), x, mixed
        )
        kept.append(saved)

    def back(layer, grad, mixed):
        return line(
            lambda g, m, k: backward(which, layer, g, m, unfold, k, w1, w2, vec, spread), grad, mixed, kept[layer]
        )

    index = lax.axis_index("dp")
    zero = jnp.zeros((), jnp.int32)
    quick = lax.axis_size("dp") == 4 and hidden == 4 * width and (width // 2) % peers == 0
    begin = index if quick else zero
    to_mine = jnp.stack([core, begin]).astype(jnp.int32)
    to_theirs = jnp.stack([1 - core, begin]).astype(jnp.int32)

    def theirs(layer, start, count, gp, gb):
        return swap_cores(
            line(lambda t, a, c, p, b: weight_grad(t, a, p, c, b, start, count), to_theirs, *kept[layer][:2], gp, gb)
        )

    def mine(layer, start, count, gp, gb, recv):
        return line(
            lambda t, a, c, p, b, r: weight_grad(t, a, p, c, b, start, count, r), to_mine, *kept[layer][:2], gp, gb, recv
        )

    def run(work):
        return line(work[0], *work[1])

    def flat_small(wide, narrow):
        return jnp.concatenate([wide.reshape(-1), narrow[:5].reshape(-1)])

    sums = [ChipSum(), ChipSum()]
    early = sums[1]
    late = sums[0]
    grad, gb1, gp1, own, other, wide1, narrow1 = back(1, grad, None)
    folded, parts = fold(own, other)
    half_count = hidden // width // 2
    upper = theirs(1, half_count, half_count, gp1, gb1)
    lower = theirs(1, 0, half_count, gp1, gb1)
    begun = part(folded)
    early.start_upper(mine(1, half_count, half_count, gp1, gb1, upper))
    early.start_lower(mine(1, 0, half_count, gp1, gb1, lower))
    out_ready = line(lambda v: product(order, v).astype(BF), x)
    mixed = rest(begun, parts)
    out_moved = give_start(line.after(out_ready))
    grad, gb0, gp0, own, other, wide0, narrow0 = back(0, grad, mixed)
    folded, parts = fold(own, other)
    early.start_second(run(early.first_sums()))
    upper = theirs(0, half_count, half_count, gp0, gb0)
    lower = theirs(0, 0, half_count, gp0, gb0)
    late.start_upper(mine(0, half_count, half_count, gp0, gb0, upper))
    late.start_lower(mine(0, 0, half_count, gp0, gb0, lower))
    begun = part(folded)
    out = line(give_end, out_moved)
    early.start_scatter(run(early.second_sums()))
    mixed = rest(begun, parts)
    in_ready = line(lambda g, m: product(order, finish(which, g, m, unfold)).astype(BF), grad, mixed)
    early.start_gather(run(early.scattered()))
    small = line(lambda *v: jnp.stack([flat_small(*v[:2]), flat_small(*v[2:])]), wide0, narrow0, wide1, narrow1)
    hops = small_hops()
    late.start_second(run(late.first_sums()))
    early.start_back(run(early.gathered()))
    in_moved = give_start(line.after(in_ready))
    for axis, pairs in hops[:2]:
        small = line(lambda a, b: a + b, small, lax.ppermute(small, axis, pairs))
    late.start_scatter(run(late.second_sums()))
    early.start_last()
    for axis, pairs in hops[2:]:
        small = line(lambda a, b: a + b, small, lax.ppermute(small, axis, pairs))
    late.start_gather(run(late.scattered()))
    in_grad = line(give_end, in_moved)
    early_sum = run(early.pieces())
    to_second = lax.ppermute(early_sum, "pipe", [(0, 1)])
    late.start_back(run(late.gathered()))
    late.start_last()
    late_sum = run(late.pieces())
    to_first = lax.ppermute(late_sum, "pipe", [(1, 0)])
    scalars = jnp.stack([core, index, z]).astype(jnp.int32)
    g_w1, g_w2 = line(write_weights, scalars, late_sum, to_first, to_second, early_sum)
    small = jnp.where(first, small[0], small[1])
    g_b1 = small[:hidden]
    g_b2, g_mg, g_ms, g_og, g_os = (small[hidden + i * width : hidden + (i + 1) * width] for i in range(5))
    return (
        out,
        in_grad,
        g_w1,
        g_b1[None],
        g_w2,
        g_b2[None],
        g_mg[None],
        g_ms[None],
        g_og[None],
        g_os[None],
    )


def solution(mesh):
    return jax.shard_map(
        on_device,
        mesh=mesh,
        in_specs=(
            P("dp", "seq", None),
            P("dp", "seq", None),
            P("pipe", None, None),
            P("pipe", None),
            P("pipe", None, None),
            P("pipe", None),
            P("pipe", None),
            P("pipe", None),
            P("pipe", None),
            P("pipe", None),
        ),
        out_specs=(
            P("dp", "seq", "pipe"),
            P("dp", "seq", "pipe"),
            P("pipe", None, None),
            P("pipe", None),
            P("pipe", None, None),
            P("pipe", None),
            P("pipe", None),
            P("pipe", None),
            P("pipe", None),
            P("pipe", None),
        ),
        check_vma=False,
    )
```

```python
import math

import jax
import jax.numpy as jnp
from jax import lax
from jax.experimental import pallas as pl
from jax.experimental.pallas import tpu as pltpu
from jax.sharding import PartitionSpec as P

BF = jnp.bfloat16
F32 = jnp.float32
PAD = 16
ROWS = 256
CHUNK = 768
COST = 64


def product(left, right):
    return jnp.dot(left, right, preferred_element_type=F32)


def contract(left, right, left_dim, right_dim):
    dims = (((left_dim,), (right_dim,)), ((), ()))
    return lax.dot_general(left, right, dims, preferred_element_type=F32)


def swap_cores(value):
    return lax.ppermute(value, "pipe", [(0, 1), (1, 0)])


def turn(phase, length):
    angles = (phase % length).astype(F32) * (2.0 * math.pi / length)
    return jnp.cos(angles), jnp.sin(angles)


def column_sets(width):
    quarter, half = width // 4, width // 2
    return (
        (list(range(quarter)) + [half], list(range(1, quarter))),
        (list(range(quarter, half)), list(range(quarter, half))),
    )


def feature_tables(width, core):
    sets = column_sets(width)
    order = []
    for cos_ids, sin_ids in sets:
        order.append(([k for k in cos_ids] + [k for k in sin_ids], [0] * len(cos_ids) + [1] * len(sin_ids)))
    ids_a = jnp.array(order[0][0] + order[1][0], jnp.int32)
    ids_b = jnp.array(order[1][0] + order[0][0], jnp.int32)
    odd_a = jnp.array(order[0][1] + order[1][1], jnp.int32)
    odd_b = jnp.array(order[1][1] + order[0][1], jnp.int32)
    first = core == 0
    ids = jnp.where(first, ids_a, ids_b)
    odd = jnp.where(first, odd_a, odd_b)
    sign = jnp.where(first, 1.0, -1.0)
    rows = jnp.arange(width, dtype=jnp.int32)
    cos, sin = turn(rows[:, None] * ids[None, :], width)
    spread = jnp.where(odd[None, :] == 1, -sign * sin, cos).astype(BF)
    direct = rows[None, :] == ids[:, None]
    mirror = rows[None, :] == ((width - ids) % width)[:, None]
    even_rows = (direct | mirror).astype(F32)
    odd_rows = sign * (direct.astype(F32) - mirror.astype(F32))
    unfold = jnp.where(odd[:, None] == 1, odd_rows, even_rows).astype(BF)
    return spread, unfold


def token_tables(block, rows, blocks, length):
    tall = rows + PAD
    inner = jnp.arange(tall, dtype=jnp.int32)
    slots = jnp.arange(blocks, dtype=jnp.int32)
    columns = ((block + blocks - slots) % blocks * rows)[:, None, None] + inner
    coarse = block * rows + PAD * jnp.arange(tall // PAD, dtype=jnp.int32)
    fine = jnp.arange(PAD, dtype=jnp.int32)
    cos_c, sin_c = turn(coarse[:, None] * columns, length)
    cos_f, sin_f = turn(fine[:, None] * columns, length)
    cos_c, sin_c, cos_f, sin_f = cos_c[:, :, None], sin_c[:, :, None], cos_f[:, None], sin_f[:, None]
    cos = (cos_c * cos_f - sin_c * sin_f).astype(BF)
    sin = (sin_c * cos_f + cos_c * sin_f).astype(BF)
    return cos.reshape(blocks, tall, tall), sin.reshape(blocks, tall, tall)


def row_block(height, width):
    return pl.BlockSpec((height, width), lambda i: (i, 0))


def whole(*shape):
    return pl.BlockSpec(shape, lambda *_: (0,) * len(shape), pipeline_mode=pl.Buffered(1))


def scalar_block():
    return pl.BlockSpec(memory_space=pltpu.SMEM)


def layer_block(layer, *shape):
    return pl.BlockSpec((1, *shape), lambda i: (layer,) + (0,) * len(shape), pipeline_mode=pl.Buffered(1))


def call(body, grid, in_specs, out_specs, out_shape, flops, moved, name, vmem, scratch=()):
    return pl.pallas_call(
        body,
        grid=grid,
        in_specs=in_specs,
        out_specs=out_specs,
        out_shape=out_shape,
        scratch_shapes=scratch,
        compiler_params=pltpu.CompilerParams(vmem_limit_bytes=vmem << 20),
        cost_estimate=pl.CostEstimate(flops=flops // COST, bytes_accessed=moved // COST, transcendentals=0),
        name=name,
    )


def like(*shape, dtype=BF):
    return jax.ShapeDtypeStruct(shape, dtype)


def divisor(count, most):
    return max(d for d in range(1, most + 1) if count % d == 0)


def fold_spectra(core, own, recv):
    rows, half = own.shape

    def body(core_ref, own_ref, recv_ref, out_ref):
        first = core_ref[0] == 0
        out_ref[:rows] = (own_ref[...].astype(F32) + recv_ref[...].astype(F32)).astype(BF)
        mine, theirs = own_ref[:PAD], recv_ref[:PAD]
        at = lax.broadcasted_iota(jnp.int32, (PAD, half), 0)
        low = jnp.where(first, mine, theirs)
        high = jnp.where(first, theirs, mine)
        out_ref[:PAD] = jnp.where(at == 0, low, out_ref[:PAD])
        out_ref[rows:] = jnp.where(at == 0, high, jnp.zeros_like(high))

    spec = pl.BlockSpec((rows, half), lambda i: (0, 0))
    return call(
        body,
        (1,),
        [scalar_block(), spec, spec],
        pl.BlockSpec((rows + PAD, half), lambda i: (0, 0)),
        like(rows + PAD, half),
        rows * half,
        6 * rows * half,
        "fold_spectra",
        8,
    )(core, own, recv)


def transform_part(cos, sin, slot, part):
    tall, half = part.shape
    wide = -(-(half // 2 + 1) // 128) * 128
    tile = divisor(tall // PAD, 17) * PAD

    def body(cos_ref, sin_ref, part_ref, out_ref):
        out_ref[:, :wide] = product(cos_ref[0], part_ref[:, :wide])
        out_ref[:, wide:] = product(sin_ref[0], part_ref[:, half - wide :])

    table = pl.BlockSpec((1, tile, tall), lambda i: (slot, i, 0))
    return call(
        body,
        (tall // tile,),
        [table, table, whole(tall, half)],
        row_block(tile, 2 * wide),
        like(tall, 2 * wide, dtype=F32),
        4 * tall * tall * wide,
        4 * tall * (tall + 2 * wide),
        "transform_part",
        12,
    )(cos, sin, part)


def transform_rest(core, cos, sin, begun, parts, factor):
    tall, half = parts[0].shape
    wide = begun.shape[1] // 2
    tile = divisor(tall // PAD, 17) * PAD
    lead = half - wide

    def body(*refs):
        core_ref, begun_ref = refs[:2]
        tables = refs[2 : 2 + 2 * len(parts)]
        part_refs = refs[2 + 2 * len(parts) : -1]
        out_ref = refs[-1]
        even, odd = begun_ref[:, :wide], begun_ref[:, wide:]
        for at, part_ref in enumerate(part_refs):
            even = even + product(tables[2 * at][0], part_ref[:, :wide])
            odd = odd + product(tables[2 * at + 1][0], part_ref[:, lead:])
        lanes = lax.broadcasted_iota(jnp.int32, (tile, wide - lead), 1) + lead
        cos_count = half // 2 + 1 - core_ref[0]
        middle = jnp.where(lanes < cos_count, even[:, lead:], odd[:, : wide - lead])
        out_ref[:, :lead] = (even[:, :lead] * factor).astype(BF)
        out_ref[:, lead:wide] = (middle * factor).astype(BF)
        out_ref[:, wide:] = (odd[:, wide - lead :] * factor).astype(BF)

    tables, specs = [], []
    for at in range(len(parts)):
        spec = pl.BlockSpec((1, tile, tall), lambda i, at=at: (at + 1, i, 0))
        tables += [cos, sin]
        specs += [spec, spec]
    return call(
        body,
        (tall // tile,),
        [scalar_block(), row_block(tile, 2 * wide)] + specs + [whole(tall, half)] * len(parts),
        row_block(tile, half),
        like(tall, half),
        4 * tall * tall * wide * len(parts),
        4 * tall * (tall * len(parts) + 2 * wide),
        "transform_rest",
        14,
    )(core, begun, *tables, *parts)


def transform(core, own, recv, cos, sin, group_shifts, factor, beside=None):
    folded = fold_spectra(core, own, recv)
    parts = [lax.ppermute(folded, "seq", pairs) for pairs in group_shifts]
    begun = transform_part(cos, sin, 0, folded)
    mixed = transform_rest(core, cos, sin, begun, parts, factor)
    return mixed, swap_cores(mixed)


def standardize(hidden):
    centered = hidden - jnp.mean(hidden, axis=-1, keepdims=True)
    spread = jnp.mean(centered * centered, axis=-1, keepdims=True)
    scale = lax.rsqrt(spread + 1e-05)
    return centered * scale, scale


def standardize_back(grad, unit, scale):
    mean_grad = jnp.mean(grad, axis=-1, keepdims=True)
    mean_both = jnp.mean(grad * unit, axis=-1, keepdims=True)
    return (grad - mean_grad - unit * mean_both) * scale


def mixture_tile(core_ref, mine_ref, mine_top, theirs_ref, theirs_top, unfold_ref):
    tile, half = mine_ref.shape
    at = lax.broadcasted_iota(jnp.int32, (tile, half), 0)
    odd_row = (at == 0) & (core_ref[0] == 1) & (pl.program_id(0) == 0)
    mine = jnp.where(odd_row, mine_top[:1], mine_ref[...])
    theirs = jnp.where(odd_row, theirs_top[:1], theirs_ref[...])
    return product(mine, unfold_ref[:half]) + product(theirs, unfold_ref[half:])


def mixture_specs(rows, half, tile):
    block = row_block(tile, half)
    top = pl.BlockSpec((PAD, half), lambda i: (rows // PAD, 0))
    return [block, top, block, top, whole(2 * half, 2 * half)]


def spectra_call(core, x, spread):
    rows, width = x.shape
    half = width // 2
    tile = min(ROWS, rows)
    factor = 1.0 / math.sqrt(width)

    def body(x_ref, spread_ref, own_ref, other_ref):
        spectra = product(x_ref[...], spread_ref[...]) * factor
        own_ref[...] = spectra[:, :half].astype(BF)
        other_ref[...] = spectra[:, half:].astype(BF)

    return call(
        body,
        (rows // tile,),
        [row_block(tile, width), whole(width, width)],
        [row_block(tile, half)] * 2,
        [like(rows, half)] * 2,
        2 * rows * width * width,
        4 * rows * width,
        "spectra",
        12,
    )(x, spread)


def forward(core, layer, x, mixed, unfold, w1, w2, b1, vec, spread, ahead):
    rows, width = x.shape
    hidden = w1.shape[2]
    half = width // 2
    tile = min(ROWS, rows)
    chunk = min(CHUNK, hidden)
    factor = 1.0 / math.sqrt(width)

    def body(core_ref, x_ref, m0, t0, m1, t1, unfold_ref, w1_ref, w2_ref, b1_ref, vec_ref, spread_ref, *outs):
        out_ref, low_ref, act_ref, slope_ref, unit1_ref, scale1_ref, unit2_ref, scale2_ref = outs[:8]
        mixture = mixture_tile(core_ref, m0, t0, m1, t1, unfold_ref).astype(BF).astype(F32)
        unit, scale = standardize(x_ref[...].astype(F32) + mixture)
        b2, mg, ms, og, os = (vec_ref[0, i : i + 1] for i in range(5))
        normed = unit * mg + ms
        unit1_ref[...] = unit.astype(BF)
        scale1_ref[...] = jnp.broadcast_to(scale, scale1_ref.shape)
        low = normed.astype(BF)
        low_ref[...] = low
        total = normed + b2
        for start in range(0, hidden, chunk):
            span = slice(start, start + chunk)
            pre = product(low, w1_ref[0, :, span]) + b1_ref[0, :, span]
            cdf = 0.5 + 0.5 * lax.erf(pre * (1.0 / math.sqrt(2.0)))
            act = (pre * cdf).astype(BF)
            act_ref[:, span] = act
            slope_ref[:, span] = (cdf + pre * (jnp.exp(-0.5 * pre * pre) * (1.0 / math.sqrt(2.0 * math.pi)))).astype(BF)
            total = total + product(act, w2_ref[0, span, :])
        unit, scale = standardize(total)
        unit2_ref[...] = unit.astype(BF)
        scale2_ref[...] = jnp.broadcast_to(scale, scale2_ref.shape)
        out = (unit * og + os).astype(BF)
        out_ref[...] = out
        if ahead:
            own_ref, other_ref = outs[8:]
            spectra = product(out, spread_ref[...]) * factor
            own_ref[...] = spectra[:, :half].astype(BF)
            other_ref[...] = spectra[:, half:].astype(BF)

    mine, theirs = mixed
    return call(
        body,
        (rows // tile,),
        [scalar_block(), row_block(tile, width)]
        + mixture_specs(rows, half, tile)
        + [
            layer_block(layer, width, hidden),
            layer_block(layer, hidden, width),
            layer_block(layer, 1, hidden),
            layer_block(layer, 5, width),
            whole(width, width),
        ],
        [
            row_block(tile, width),
            row_block(tile, width),
            row_block(tile, hidden),
            row_block(tile, hidden),
            row_block(tile, width),
            row_block(tile, 128),
            row_block(tile, width),
            row_block(tile, 128),
        ]
        + [row_block(tile, half)] * (2 if ahead else 0),
        [
            like(rows, width),
            like(rows, width),
            like(rows, hidden),
            like(rows, hidden),
            like(rows, width),
            like(rows, 128, dtype=F32),
            like(rows, width),
            like(rows, 128, dtype=F32),
        ]
        + [like(rows, half)] * (2 if ahead else 0),
        4 * rows * width * (hidden + width),
        4 * width * hidden + 4 * rows * hidden + 14 * rows * width,
        "layer_forward",
        58,
    )(core, x, mine, mine, theirs, theirs, unfold, w1, w2, b1, vec, spread)


def backward(scalars, layer, grad, mixed, unfold, kept, w1, w2, vec, spread):
    low, act, slope, unit1, scale1, unit2, scale2 = kept
    rows, width = grad.shape
    hidden = w1.shape[2]
    half = width // 2
    tile = min(ROWS, rows)
    squares = hidden // width
    factor = 1.0 / math.sqrt(width)
    count = 0 if mixed is None else 5

    def body(scalar_ref, grad_ref, *refs):
        low_ref, act_ref, slope_ref, unit1_ref, scale1_ref, unit2_ref, scale2_ref, w1_ref, w2_ref, vec_ref, spread_ref = refs[
            count : 11 + count
        ]
        gh_ref, own_ref, other_ref, wide_ref, sums_ref, *block_refs = refs[11 + count : -2]
        in_sum, out_sum = refs[-2:]

        @pl.when(pl.program_id(0) == 0)
        def _():
            for ref in (wide_ref, sums_ref, in_sum, out_sum):
                ref[...] = jnp.zeros_like(ref)

        grad = grad_ref[...].astype(F32)
        if count:
            grad = (grad + mixture_tile(scalar_ref, *refs[:count])).astype(BF).astype(F32)
        mg, og = vec_ref[0, 1:2], vec_ref[0, 3:4]
        unit2 = unit2_ref[...].astype(F32)
        g_branch = standardize_back(grad * og, unit2, scale2_ref[:, :1])
        gb = g_branch.astype(BF)
        total = g_branch
        for square in range(squares):
            span = slice(square * width, (square + 1) * width)
            g_act = contract(gb, w2_ref[0, span, :], 1, 1)
            gp = (g_act * slope_ref[:, span].astype(F32)).astype(BF)
            wide_ref[:, span] += jnp.sum(gp.astype(F32), axis=0, keepdims=True)
            total = total + contract(gp, w1_ref[0, :, span], 1, 1)
            out_sum[square] += contract(act_ref[:, span], gb, 0, 0)
            in_sum[square] += contract(low_ref[...], gp, 0, 0)
        unit1 = unit1_ref[...].astype(F32)
        g_h = standardize_back(total * mg, unit1, scale1_ref[:, :1])
        gh_ref[...] = g_h
        for at, terms in enumerate((gb.astype(F32), total * unit1, total, grad * unit2, grad)):
            sums_ref[at : at + 1] += jnp.sum(terms, axis=0, keepdims=True)
        spectra = product(g_h.astype(BF), spread_ref[...]) * factor
        own_ref[...] = spectra[:, :half].astype(BF)
        other_ref[...] = spectra[:, half:].astype(BF)

        @pl.when(pl.program_id(0) == pl.num_programs(0) - 1)
        def _():
            for owner in range(2):
                part = pl.ds(pl.multiple_of((scalar_ref[0] ^ owner) * half, half), half)
                for use in range(2):
                    for at in range(2):
                        ref = block_refs[2 * owner + use]
                        ref[0, at] = out_sum[(2 * at + 1 - use) ^ scalar_ref[1], part, :].astype(BF)
                        ref[1, at] = in_sum[(2 - 2 * use + at) ^ scalar_ref[1], part, :].astype(BF)

    if count:
        mine, theirs = mixed
        extra = [mine, mine, theirs, theirs, unfold]
        extra_specs = mixture_specs(rows, half, tile)
    else:
        extra, extra_specs = [], []
    return call(
        body,
        (rows // tile,),
        [scalar_block(), row_block(tile, width)]
        + extra_specs
        + [
            row_block(tile, width),
            row_block(tile, hidden),
            row_block(tile, hidden),
            row_block(tile, width),
            row_block(tile, 128),
            row_block(tile, width),
            row_block(tile, 128),
            layer_block(layer, width, hidden),
            layer_block(layer, hidden, width),
            layer_block(layer, 5, width),
            whole(width, width),
        ],
        [
            row_block(tile, width),
            row_block(tile, half),
            row_block(tile, half),
            whole(1, hidden),
            whole(8, width),
        ]
        + [whole(2, 2, half, width)] * 4,
        [
            like(rows, width, dtype=F32),
            like(rows, half),
            like(rows, half),
            like(1, hidden, dtype=F32),
            like(8, width, dtype=F32),
        ]
        + [like(2, 2, half, width)] * 4,
        8 * rows * width * (hidden + width),
        4 * width * hidden + 4 * rows * hidden + 14 * rows * width,
        "layer_backward",
        60,
        [pltpu.VMEM((squares, width, width), F32)] * 2,
    )(scalars, grad, *extra, low, act, slope, unit1, scale1, unit2, scale2, w1, w2, vec, spread)


def backward_last(layer, grad, kept, w1, w2, vec, spread):
    low, act, slope, unit1, scale1, unit2, scale2 = kept
    rows, width = grad.shape
    hidden = w1.shape[2]
    half = width // 2
    tile = min(ROWS, rows)
    chunk = min(CHUNK, hidden)
    factor = 1.0 / math.sqrt(width)

    def body(*refs):
        grad_ref = refs[0]
        slope_ref, unit1_ref, scale1_ref, unit2_ref, scale2_ref, w1_ref, w2_ref, vec_ref, spread_ref = refs[1:10]
        gh_ref, gb_ref, gp_ref, own_ref, other_ref, wide_ref, sums_ref = refs[10:]

        @pl.when(pl.program_id(0) == 0)
        def _():
            wide_ref[...] = jnp.zeros_like(wide_ref)
            sums_ref[...] = jnp.zeros_like(sums_ref)

        grad = grad_ref[...].astype(F32)
        mg, og = vec_ref[0, 1:2], vec_ref[0, 3:4]
        unit2 = unit2_ref[...].astype(F32)
        g_branch = standardize_back(grad * og, unit2, scale2_ref[:, :1])
        gb = g_branch.astype(BF)
        gb_ref[...] = gb
        total = g_branch
        for start in range(0, hidden, chunk):
            span = slice(start, start + chunk)
            g_act = contract(gb, w2_ref[0, span, :], 1, 1)
            gp = (g_act * slope_ref[:, span].astype(F32)).astype(BF)
            gp_ref[:, span] = gp
            wide_ref[:, span] += jnp.sum(gp.astype(F32), axis=0, keepdims=True)
            total = total + contract(gp, w1_ref[0, :, span], 1, 1)
        unit1 = unit1_ref[...].astype(F32)
        g_h = standardize_back(total * mg, unit1, scale1_ref[:, :1])
        gh_ref[...] = g_h
        for at, terms in enumerate((gb.astype(F32), total * unit1, total, grad * unit2, grad)):
            sums_ref[at : at + 1] += jnp.sum(terms, axis=0, keepdims=True)
        spectra = product(g_h.astype(BF), spread_ref[...]) * factor
        own_ref[...] = spectra[:, :half].astype(BF)
        other_ref[...] = spectra[:, half:].astype(BF)

    return call(
        body,
        (rows // tile,),
        [
            row_block(tile, width),
            row_block(tile, hidden),
            row_block(tile, width),
            row_block(tile, 128),
            row_block(tile, width),
            row_block(tile, 128),
            layer_block(layer, width, hidden),
            layer_block(layer, hidden, width),
            layer_block(layer, 5, width),
            whole(width, width),
        ],
        [
            row_block(tile, width),
            row_block(tile, width),
            row_block(tile, hidden),
            row_block(tile, half),
            row_block(tile, half),
            whole(1, hidden),
            whole(8, width),
        ],
        [
            like(rows, width, dtype=F32),
            like(rows, width),
            like(rows, hidden),
            like(rows, half),
            like(rows, half),
            like(1, hidden, dtype=F32),
            like(8, width, dtype=F32),
        ],
        4 * rows * width * (hidden + width),
        4 * width * hidden + 4 * rows * hidden + 14 * rows * width,
        "last_backward",
        58,
    )(grad, slope, unit1, scale1, unit2, scale2, w1, w2, vec, spread)


def grad_blocks(scalars, low, gp, act, gb):
    rows, width = low.shape
    half = width // 2

    def body(scalar_ref, act_ref, gb_ref, low_ref, gp_ref, sent_ref, kept_ref):
        outer = contract(act_ref[...], gb_ref[...], 0, 0).astype(BF)
        inner = contract(low_ref[...], gp_ref[...], 0, 0).astype(BF)

        @pl.when(pl.program_id(0) < 2)
        def _():
            sent_ref[0, 0] = outer
            sent_ref[1, 0] = inner

        @pl.when(pl.program_id(0) >= 2)
        def _():
            kept_ref[0, 0] = outer
            kept_ref[1, 0] = inner

    def out_square(i, s):
        return ((2 * i + 1 - i // 2) % 4) ^ s[1]

    def in_square(i, s):
        return ((i + 2) % 4) ^ s[1]

    return pl.pallas_call(
        body,
        grid_spec=pltpu.PrefetchScalarGridSpec(
            num_scalar_prefetch=1,
            grid=(4,),
            in_specs=[
                pl.BlockSpec((rows, half), lambda i, s: (0, 2 * out_square(i, s) + s[0])),
                pl.BlockSpec((rows, width), lambda i, s: (0, 0)),
                pl.BlockSpec((rows, half), lambda i, s: (0, s[0])),
                pl.BlockSpec((rows, width), lambda i, s: (0, in_square(i, s))),
            ],
            out_specs=[
                pl.BlockSpec((2, 1, half, width), lambda i, s: (0, jnp.minimum(i, 1), 0, 0)),
                pl.BlockSpec((2, 1, half, width), lambda i, s: (0, jnp.maximum(i - 2, 0), 0, 0)),
            ],
        ),
        out_shape=[like(2, 2, half, width)] * 2,
        compiler_params=pltpu.CompilerParams(vmem_limit_bytes=58 << 20),
        cost_estimate=pl.CostEstimate(flops=16 * rows * width * half // COST, bytes_accessed=20 * rows * width // COST, transcendentals=0),
        name="grad_blocks",
    )(scalars, act, gb, low, gp)


def write_weights(scalars, far, sources, begun=None):
    _, slots, piece, width = sources[0][0][0].shape
    half = slots * piece
    flat = [array for pair in sources for source in pair for array in source]

    def body(s, *refs):
        in_ref, out_ref = refs[-2:]

        def write(target, source, top):
            for slot in range(slots):
                at = pl.multiple_of((s[2] + slots - slot) % slots * piece, piece)
                target[0, pl.ds(at + top, piece), :] = source[0, slot].astype(F32)

        for core in range(2):

            @pl.when(s[0] == core)
            def _():
                for at, top in ((0, core * half), (2, (1 - core) * half)):
                    write(out_ref, refs[4 * core + at], top)
                    write(in_ref, refs[4 * core + at + 1], top)

    def source(core):
        return pl.BlockSpec((1, slots, piece, width), lambda k, s: (jnp.where(s[0] == core, k, 0), 0, 0, 0))

    extra = [] if begun is None else list(begun)
    return pl.pallas_call(
        body,
        grid_spec=pltpu.PrefetchScalarGridSpec(
            num_scalar_prefetch=1,
            grid=(2,),
            in_specs=[source(0)] * 4 + [source(1)] * 4 + [pl.BlockSpec(memory_space=pl.ANY)] * len(extra),
            out_specs=[
                pl.BlockSpec((1, width, width), lambda k, s: (0, 0, (k + 2 * far) ^ s[1])),
                pl.BlockSpec((1, width, width), lambda k, s: (0, (2 * k + far) ^ s[1], 0)),
            ],
        ),
        out_shape=[like(1, width, 4 * width, dtype=F32), like(1, 4 * width, width, dtype=F32)],
        input_output_aliases={9: 0, 10: 1} if extra else {},
        compiler_params=pltpu.CompilerParams(vmem_limit_bytes=40 << 20),
        cost_estimate=pl.CostEstimate(flops=0, bytes_accessed=24 * width * width // COST, transcendentals=0),
        name="write_weights",
    )(scalars, *flat, *extra)


def finish(core, g_h, mixed, unfold):
    rows, width = g_h.shape
    half = width // 2
    tile = min(ROWS, rows)

    def body(g_ref, *refs):
        refs[-1][...] = (g_ref[...] + mixture_tile(*refs[:-1])).astype(BF)

    mine, theirs = mixed
    return call(
        body,
        (rows // tile,),
        [row_block(tile, width), scalar_block()] + mixture_specs(rows, half, tile),
        row_block(tile, width),
        like(rows, width),
        2 * rows * width * width,
        8 * rows * width,
        "finish",
        14,
    )(g_h, core, mine, mine, theirs, theirs, unfold)


def bit_pairs(count, bit):
    return [(i, i ^ (1 << bit)) for i in range(count)]


def added(left, right):
    return (left.astype(F32) + right.astype(F32)).astype(BF)


class Line:
    def __init__(self):
        self.last = None

    def __call__(self, step, *args):
        if self.last is not None:
            args, _ = lax.optimization_barrier((args, self.last))
        out = step(*args)
        self.last = min(jax.tree.leaves(out), key=lambda leaf: leaf.size)
        return out

    def after(self, value):
        return lax.optimization_barrier((value, self.last))[0]


class ChipSum:
    def __init__(self):
        self.count = lax.axis_size("dp")
        self.peers = lax.axis_size("seq")

    def across(self, bit, value):
        return lax.ppermute(value, "dp", bit_pairs(self.count, bit))

    def sent(self, mine, theirs):
        return (lambda a, b: [added(a[stream], b[stream]) for stream in range(2)]), (mine, theirs)

    def start_first(self, sent):
        self.first = [self.across(stream, sent[stream]) for stream in range(2)]

    def first_sums(self, mine, theirs):
        def step(a, b, *got):
            sums = [(a[m].astype(F32) + b[m].astype(F32) + got[m].astype(F32)).astype(BF) for m in range(2)]
            return [(part[1], part[0]) for part in sums]

        return step, (mine, theirs, *self.first)

    def start_second(self, sums):
        self.second = [(sums[stream][1], self.across(1 - stream, sums[stream][0])) for stream in range(2)]

    def second_sums(self):
        def step(z, *pairs):
            sums = [added(*pair) for pair in pairs]
            for bit in range(2, self.count.bit_length() - 1):
                sums = [added(part, self.across(bit, part)) for part in sums]
            both = jnp.stack(sums)
            both = both.reshape(2, self.peers, -1, both.shape[-1])
            return [lax.dynamic_index_in_dim(both, (z + d) % self.peers, 1, keepdims=False) for d in range(self.peers)]

        return step, (lax.axis_index("seq"), *self.second)

    def along(self, value, by):
        return lax.ppermute(value, "seq", [(i, (i + by) % self.peers) for i in range(self.peers)])

    def start_scatter(self, pieces):
        self.kept = pieces[0]
        self.got = [self.along(piece, d) for d, piece in enumerate(pieces) if d]

    def scattered(self):
        def step(kept, *got):
            return sum((g.astype(F32) for g in got), kept.astype(F32)).astype(BF)

        return step, (self.kept, *self.got)

    def start_gather(self, piece):
        self.kept = piece
        self.got = [self.along(piece, d) for d in range(1, self.peers)]

    def gathered(self):
        def step(*pieces):
            return [jnp.stack([piece[at] for piece in pieces]) for at in range(2)]

        return step, (self.kept, *self.got)

    def start_back(self, streams):
        self.own = streams
        self.near = [self.across(1 - stream, streams[stream]) for stream in range(2)]

    def paired(self):
        def step(a, b, c, d):
            return jnp.stack([a, b]), jnp.stack([c, d])

        return step, (self.own[0], self.near[0], self.own[1], self.near[1])

    def start_last(self, pairs):
        self.pairs = pairs
        self.far = [self.across(stream, pairs[stream]) for stream in range(2)]

def small_hops():
    hops = []
    for axis in ("pipe", "seq", "dp"):
        count = lax.axis_size(axis)
        hops += [(axis, bit_pairs(count, bit)) for bit in range(count.bit_length() - 1)]
    return hops


def on_device(
    inputs,
    cotangent,
    in_weight,
    in_bias,
    out_weight,
    out_bias,
    mix_gain,
    mix_shift,
    out_gain,
    out_shift,
):
    rows, width = inputs.shape[1:]
    hidden = in_weight.shape[2]
    peers = lax.axis_size("seq")
    blocks = peers // 2
    half = width // 2
    core = lax.axis_index("pipe")
    z = lax.axis_index("seq")
    first = core == 0
    low = z < blocks
    local = low == first
    block = jnp.minimum(z, peers - 1 - z)
    which = core.astype(jnp.int32).reshape(1)

    def place(member, is_low):
        return member if is_low else peers - 1 - member

    group_shifts = [
        [(place(b, side), place((b + d) % blocks, side)) for side in (True, False) for b in range(blocks)]
        for d in range(1, blocks)
    ]
    in_pairs = []
    out_pairs = []
    for i in range(peers):
        facing = peers - 1 - i
        source = peers + i if i < blocks else i
        in_pairs.append((source, facing if i < blocks else peers + facing))
        out_pairs.append((source, peers + facing if source < peers else facing))

    row_ids = lax.broadcasted_iota(jnp.int32, (rows, rows), 0)
    col_ids = lax.broadcasted_iota(jnp.int32, (rows, rows), 1)
    order = (col_ids == jnp.where(first, row_ids, (rows - row_ids) % rows)).astype(BF)

    def picked(items):
        return jnp.where(low, items[1], items[0]), jnp.where(low, items[0], items[1])

    def arranged(kept, moved):
        return product(order, jnp.where(local, kept, moved)).astype(BF)

    turned = z >= blocks
    back_order = (col_ids == jnp.where(turned, (rows - row_ids) % rows, row_ids)).astype(BF)

    def give_start(value):
        return value, lax.ppermute(value, ("pipe", "seq"), out_pairs)

    def give_cut(value, moved):
        block = jnp.where(local, value, moved)
        return jnp.where(first, block[:, :half], block[:, half:]), jnp.where(first, block[:, half:], block[:, :half])

    def give_end(mine, beside):
        near = jnp.where(local, mine, beside)
        far = jnp.where(local, beside, mine)
        return jnp.stack(
            [product(back_order, part).astype(BF) for part in (jnp.where(low, near, far), jnp.where(low, far, near))]
        )

    sent, x = picked(inputs)
    x = arranged(x, lax.ppermute(sent, ("pipe", "seq"), in_pairs))
    vectors = jnp.concatenate([in_bias[0], out_bias[0], mix_gain[0], mix_shift[0], out_gain[0], out_shift[0]])
    other_vectors = swap_cores(vectors)
    vectors = jnp.where(first, jnp.stack([vectors, other_vectors]), jnp.stack([other_vectors, vectors]))
    b1 = vectors[:, :hidden].reshape(2, 1, hidden)
    vec = vectors[:, hidden:].reshape(2, 5, width)
    w1 = lax.all_gather(in_weight, "pipe", axis=0, tiled=True)
    w2 = lax.all_gather(out_weight, "pipe", axis=0, tiled=True)
    spread, unfold = feature_tables(width, core)
    cos, sin = token_tables(block, rows, blocks, rows * peers)
    factor = 1.0 / math.sqrt(rows * peers)

    line = Line()

    def fold(own, came):
        return line(lambda a, b: fold_spectra(which, a, b), own, came)

    def spread_out(folded):
        return [lax.ppermute(folded, "seq", pairs) for pairs in group_shifts]

    def part(folded):
        return line(lambda f: transform_part(cos, sin, 0, f), folded)

    def rest(begun, parts):
        return line(lambda a, *b: transform_rest(which, cos, sin, a, list(b), factor), begun, *parts)

    kept = []
    own, other = line(lambda v: spectra_call(which, v, spread), x)
    cot_sent, cot_kept = line.after(picked(cotangent))
    for layer in range(2):
        folded = fold(own, swap_cores(other))
        parts = spread_out(folded)
        begun = part(folded)
        if layer == 1:
            grad = line(arranged, cot_kept, cot_moved)
        mixed = rest(begun, parts)
        came = swap_cores(mixed)
        if layer == 0:
            cot_moved = lax.ppermute(line.after(cot_sent), ("pipe", "seq"), in_pairs)
        x, *saved = line(
            lambda v, m, l=layer: forward(which, l, v, m, unfold, w1, w2, b1, vec, spread, l == 0), x, (mixed, came)
        )
        kept.append(saved[:7])
        if layer == 0:
            own, other = saved[7:]

    index = lax.axis_index("dp") & 3
    scalars = jnp.stack([core, index]).astype(jnp.int32)

    def back(layer, grad, mixed):
        return line(
            lambda g, m, k: backward(scalars, layer, g, m, unfold, k, w1, w2, vec, spread), grad, mixed, kept[layer]
        )

    def run(work):
        return line(work[0], *work[1])

    def flat_small(wide, narrow):
        return jnp.concatenate([wide.reshape(-1), narrow[:5].reshape(-1)])

    late, early = ChipSum(), ChipSum()
    to_theirs = jnp.stack([1 - core, index]).astype(jnp.int32)

    def blocks_of(target, gp, gb):
        return line(grad_blocks, target, kept[1][0], gp, kept[1][1], gb)

    out_moved = give_start(x)
    grad, gb, gp, own, other, wide1, narrow1 = line(
        lambda g, k: backward_last(1, g, k, w1, w2, vec, spread), grad, kept[1]
    )

    came = swap_cores(other)
    other_sent, other_kept = blocks_of(to_theirs, gp, gb)
    folded = fold(own, came)

    parts = spread_out(line.after(folded))
    got_sent, got_kept1 = swap_cores(line.after((other_sent, other_kept)))
    my_sent, my_kept1 = blocks_of(scalars, gp, gb)
    begun = part(folded)
    mixed = rest(begun, parts)

    came = swap_cores(mixed)
    sent = run(early.sent(my_sent, got_sent))

    early.start_first(line.after(sent))
    grad, own, other, wide0, narrow0, my_sent, my_kept, other_sent, other_kept = back(0, grad, (mixed, came))

    sums = run(early.first_sums(my_kept1, got_kept1))
    out_mine, out_theirs = line(give_cut, *out_moved)

    got_sent = swap_cores(line.after(other_sent))
    came = swap_cores(line.after(other))
    early.start_second(line.after(sums))
    folded = fold(own, came)
    sent = run(late.sent(my_sent, got_sent))
    pieces = run(early.second_sums())

    hops = iter(small_hops())
    small = jnp.stack([flat_small(wide0, narrow0), flat_small(wide1, narrow1)])

    def start_hop():
        axis, pairs = next(hops)
        return lax.ppermute(line.after(small), axis, pairs)

    def end_hop(got):
        return line(lambda a, b: a + b, small, got)

    late.start_first(line.after(sent))
    parts = spread_out(line.after(folded))
    early.start_scatter(line.after(pieces))
    got_kept0 = swap_cores(line.after(other_kept))
    hop = start_hop()
    begun = part(folded)
    mixed = rest(begun, parts)
    piece = run(early.scattered())
    small = end_hop(hop)
    sums = run(late.first_sums(my_kept, got_kept0))

    late.start_second(line.after(sums))
    early.start_gather(line.after(piece))
    out_beside, came = swap_cores(line.after((out_theirs, mixed)))
    pieces = run(late.second_sums())
    in_ready = line(lambda g, m: finish(which, g, m, unfold), grad, (mixed, came))
    streams = run(early.gathered())

    late.start_scatter(line.after(pieces))
    early.start_back(line.after(streams))
    hop = start_hop()
    out = line(give_end, out_mine, out_beside)
    pairs = run(early.paired())

    early.start_last(line.after(pairs))
    piece = run(late.scattered())
    small = end_hop(hop)

    late.start_gather(line.after(piece))
    pairs_far1 = lax.ppermute(line.after(pairs), "pipe", [(0, 1)])
    hop = start_hop()
    streams = run(late.gathered())
    small = end_hop(hop)
    far1 = line.after(early.far)

    streams, far1 = lax.optimization_barrier((streams, far1))
    late.start_back(streams)
    hop = start_hop()
    far1_far = lax.ppermute(line.after(far1), "pipe", [(0, 1)])
    in_moved = give_start(line.after(in_ready))
    pairs0 = run(late.paired())
    small = end_hop(hop)

    late.start_last(line.after(pairs0))
    pairs_far0 = lax.ppermute(line.after(pairs0), "pipe", [(1, 0)])
    hop = start_hop()
    scalars = jnp.stack([core, index, z]).astype(jnp.int32)
    begun = line(lambda *v: write_weights(scalars, 0, v), (pairs0, pairs_far0), (pairs, pairs_far1))
    far0 = line.after(late.far)

    far0_far = lax.ppermute(far0, "pipe", [(1, 0)])
    small, far0_far = lax.optimization_barrier((small, far0_far))
    small = end_hop(hop)
    in_mine, in_theirs = line(give_cut, *in_moved)
    in_beside = swap_cores(line.after(in_theirs))
    g_w1, g_w2 = line(lambda b, *v: write_weights(scalars, 1, v, b), begun, (far0, far0_far), (far1, far1_far))
    in_grad = line(give_end, in_mine, in_beside)
    for axis, hop in hops:
        small = line(lambda a, b: a + b, small, lax.ppermute(small, axis, hop))
    small = jnp.where(first, small[0], small[1])
    g_b1 = small[:hidden]
    g_b2, g_mg, g_ms, g_og, g_os = (small[hidden + i * width : hidden + (i + 1) * width] for i in range(5))
    return (
        out,
        in_grad,
        g_w1,
        g_b1[None],
        g_w2,
        g_b2[None],
        g_mg[None],
        g_ms[None],
        g_og[None],
        g_os[None],
    )


def solution(mesh):
    return jax.shard_map(
        on_device,
        mesh=mesh,
        in_specs=(
            P("dp", "seq", None),
            P("dp", "seq", None),
            P("pipe", None, None),
            P("pipe", None),
            P("pipe", None, None),
            P("pipe", None),
            P("pipe", None),
            P("pipe", None),
            P("pipe", None),
            P("pipe", None),
        ),
        out_specs=(
            P("dp", "seq", "pipe"),
            P("dp", "seq", "pipe"),
            P("pipe", None, None),
            P("pipe", None),
            P("pipe", None, None),
            P("pipe", None),
            P("pipe", None),
            P("pipe", None),
            P("pipe", None),
            P("pipe", None),
        ),
        check_vma=False,
    )
```

```python
import math

import jax
import jax.numpy as jnp
from jax import lax
from jax.experimental import pallas as pl
from jax.experimental.pallas import tpu as pltpu
from jax.sharding import PartitionSpec as P

BF = jnp.bfloat16
F32 = jnp.float32
PAD = 16
ROWS = 256
CHUNK = 768
COST = 64


def product(left, right):
    return jnp.dot(left, right, preferred_element_type=F32)


def contract(left, right, left_dim, right_dim):
    dims = (((left_dim,), (right_dim,)), ((), ()))
    return lax.dot_general(left, right, dims, preferred_element_type=F32)


def swap_cores(value):
    return lax.ppermute(value, "pipe", [(0, 1), (1, 0)])


def turn(phase, length):
    angles = (phase % length).astype(F32) * (2.0 * math.pi / length)
    return jnp.cos(angles), jnp.sin(angles)


def column_sets(width):
    quarter, half = width // 4, width // 2
    return (
        (list(range(quarter)) + [half], list(range(1, quarter))),
        (list(range(quarter, half)), list(range(quarter, half))),
    )


def feature_tables(width, core):
    sets = column_sets(width)
    order = []
    for cos_ids, sin_ids in sets:
        order.append(([k for k in cos_ids] + [k for k in sin_ids], [0] * len(cos_ids) + [1] * len(sin_ids)))
    ids_a = jnp.array(order[0][0] + order[1][0], jnp.int32)
    ids_b = jnp.array(order[1][0] + order[0][0], jnp.int32)
    odd_a = jnp.array(order[0][1] + order[1][1], jnp.int32)
    odd_b = jnp.array(order[1][1] + order[0][1], jnp.int32)
    first = core == 0
    ids = jnp.where(first, ids_a, ids_b)
    odd = jnp.where(first, odd_a, odd_b)
    sign = jnp.where(first, 1.0, -1.0)
    rows = jnp.arange(width, dtype=jnp.int32)
    cos, sin = turn(rows[:, None] * ids[None, :], width)
    spread = jnp.where(odd[None, :] == 1, -sign * sin, cos).astype(BF)
    direct = rows[None, :] == ids[:, None]
    mirror = rows[None, :] == ((width - ids) % width)[:, None]
    even_rows = (direct | mirror).astype(F32)
    odd_rows = sign * (direct.astype(F32) - mirror.astype(F32))
    unfold = jnp.where(odd[:, None] == 1, odd_rows, even_rows).astype(BF)
    return spread, unfold


def token_tables(block, rows, blocks, length):
    tall = rows + PAD
    inner = jnp.arange(tall, dtype=jnp.int32)
    slots = jnp.arange(blocks, dtype=jnp.int32)
    columns = ((block + blocks - slots) % blocks * rows)[:, None, None] + inner
    coarse = block * rows + PAD * jnp.arange(tall // PAD, dtype=jnp.int32)
    fine = jnp.arange(PAD, dtype=jnp.int32)
    cos_c, sin_c = turn(coarse[:, None] * columns, length)
    cos_f, sin_f = turn(fine[:, None] * columns, length)
    cos_c, sin_c, cos_f, sin_f = cos_c[:, :, None], sin_c[:, :, None], cos_f[:, None], sin_f[:, None]
    cos = (cos_c * cos_f - sin_c * sin_f).astype(BF)
    sin = (sin_c * cos_f + cos_c * sin_f).astype(BF)
    return cos.reshape(blocks, tall, tall), sin.reshape(blocks, tall, tall)


def row_block(height, width):
    return pl.BlockSpec((height, width), lambda i: (i, 0))


def whole(*shape):
    return pl.BlockSpec(shape, lambda *_: (0,) * len(shape), pipeline_mode=pl.Buffered(1))


def scalar_block():
    return pl.BlockSpec(memory_space=pltpu.SMEM)


def layer_block(layer, *shape):
    return pl.BlockSpec((1, *shape), lambda i: (layer,) + (0,) * len(shape), pipeline_mode=pl.Buffered(1))


def call(body, grid, in_specs, out_specs, out_shape, flops, moved, name, vmem, scratch=()):
    return pl.pallas_call(
        body,
        grid=grid,
        in_specs=in_specs,
        out_specs=out_specs,
        out_shape=out_shape,
        scratch_shapes=scratch,
        compiler_params=pltpu.CompilerParams(vmem_limit_bytes=vmem << 20),
        cost_estimate=pl.CostEstimate(flops=flops // COST, bytes_accessed=moved // COST, transcendentals=0),
        name=name,
    )


def like(*shape, dtype=BF):
    return jax.ShapeDtypeStruct(shape, dtype)


def divisor(count, most):
    return max(d for d in range(1, most + 1) if count % d == 0)


def fold_spectra(core, own, recv):
    rows, half = own.shape

    def body(core_ref, own_ref, recv_ref, out_ref):
        first = core_ref[0] == 0
        out_ref[:rows] = (own_ref[...].astype(F32) + recv_ref[...].astype(F32)).astype(BF)
        mine, theirs = own_ref[:PAD], recv_ref[:PAD]
        at = lax.broadcasted_iota(jnp.int32, (PAD, half), 0)
        low = jnp.where(first, mine, theirs)
        high = jnp.where(first, theirs, mine)
        out_ref[:PAD] = jnp.where(at == 0, low, out_ref[:PAD])
        out_ref[rows:] = jnp.where(at == 0, high, jnp.zeros_like(high))

    spec = pl.BlockSpec((rows, half), lambda i: (0, 0))
    return call(
        body,
        (1,),
        [scalar_block(), spec, spec],
        pl.BlockSpec((rows + PAD, half), lambda i: (0, 0)),
        like(rows + PAD, half),
        rows * half,
        6 * rows * half,
        "fold_spectra",
        8,
    )(core, own, recv)


def transform_part(cos, sin, slot, part):
    tall, half = part.shape
    wide = -(-(half // 2 + 1) // 128) * 128
    tile = divisor(tall // PAD, 17) * PAD

    def body(cos_ref, sin_ref, part_ref, out_ref):
        out_ref[:, :wide] = product(cos_ref[0], part_ref[:, :wide])
        out_ref[:, wide:] = product(sin_ref[0], part_ref[:, half - wide :])

    table = pl.BlockSpec((1, tile, tall), lambda i: (slot, i, 0))
    return call(
        body,
        (tall // tile,),
        [table, table, whole(tall, half)],
        row_block(tile, 2 * wide),
        like(tall, 2 * wide, dtype=F32),
        4 * tall * tall * wide,
        4 * tall * (tall + 2 * wide),
        "transform_part",
        12,
    )(cos, sin, part)


def transform_rest(core, cos, sin, begun, parts, factor):
    tall, half = parts[0].shape
    wide = begun.shape[1] // 2
    tile = divisor(tall // PAD, 17) * PAD
    lead = half - wide

    def body(*refs):
        core_ref, begun_ref = refs[:2]
        tables = refs[2 : 2 + 2 * len(parts)]
        part_refs = refs[2 + 2 * len(parts) : -1]
        out_ref = refs[-1]
        even, odd = begun_ref[:, :wide], begun_ref[:, wide:]
        for at, part_ref in enumerate(part_refs):
            even = even + product(tables[2 * at][0], part_ref[:, :wide])
            odd = odd + product(tables[2 * at + 1][0], part_ref[:, lead:])
        lanes = lax.broadcasted_iota(jnp.int32, (tile, wide - lead), 1) + lead
        cos_count = half // 2 + 1 - core_ref[0]
        middle = jnp.where(lanes < cos_count, even[:, lead:], odd[:, : wide - lead])
        out_ref[:, :lead] = (even[:, :lead] * factor).astype(BF)
        out_ref[:, lead:wide] = (middle * factor).astype(BF)
        out_ref[:, wide:] = (odd[:, wide - lead :] * factor).astype(BF)

    tables, specs = [], []
    for at in range(len(parts)):
        spec = pl.BlockSpec((1, tile, tall), lambda i, at=at: (at + 1, i, 0))
        tables += [cos, sin]
        specs += [spec, spec]
    return call(
        body,
        (tall // tile,),
        [scalar_block(), row_block(tile, 2 * wide)] + specs + [whole(tall, half)] * len(parts),
        row_block(tile, half),
        like(tall, half),
        4 * tall * tall * wide * len(parts),
        4 * tall * (tall * len(parts) + 2 * wide),
        "transform_rest",
        14,
    )(core, begun, *tables, *parts)


def transform(core, own, recv, cos, sin, group_shifts, factor, beside=None):
    folded = fold_spectra(core, own, recv)
    parts = [lax.ppermute(folded, "seq", pairs) for pairs in group_shifts]
    begun = transform_part(cos, sin, 0, folded)
    mixed = transform_rest(core, cos, sin, begun, parts, factor)
    return mixed, swap_cores(mixed)


def standardize(hidden):
    centered = hidden - jnp.mean(hidden, axis=-1, keepdims=True)
    spread = jnp.mean(centered * centered, axis=-1, keepdims=True)
    scale = lax.rsqrt(spread + 1e-05)
    return centered * scale, scale


def standardize_back(grad, unit, scale):
    mean_grad = jnp.mean(grad, axis=-1, keepdims=True)
    mean_both = jnp.mean(grad * unit, axis=-1, keepdims=True)
    return (grad - mean_grad - unit * mean_both) * scale


def mixture_tile(core_ref, mine_ref, mine_top, theirs_ref, theirs_top, unfold_ref):
    tile, half = mine_ref.shape
    at = lax.broadcasted_iota(jnp.int32, (tile, half), 0)
    odd_row = (at == 0) & (core_ref[0] == 1) & (pl.program_id(0) == 0)
    mine = jnp.where(odd_row, mine_top[:1], mine_ref[...])
    theirs = jnp.where(odd_row, theirs_top[:1], theirs_ref[...])
    return product(mine, unfold_ref[:half]) + product(theirs, unfold_ref[half:])


def mixture_specs(rows, half, tile):
    block = row_block(tile, half)
    top = pl.BlockSpec((PAD, half), lambda i: (rows // PAD, 0))
    return [block, top, block, top, whole(2 * half, 2 * half)]


def spectra_call(core, x, spread):
    rows, width = x.shape
    half = width // 2
    tile = min(ROWS, rows)
    factor = 1.0 / math.sqrt(width)

    def body(x_ref, spread_ref, own_ref, other_ref):
        spectra = product(x_ref[...], spread_ref[...]) * factor
        own_ref[...] = spectra[:, :half].astype(BF)
        other_ref[...] = spectra[:, half:].astype(BF)

    return call(
        body,
        (rows // tile,),
        [row_block(tile, width), whole(width, width)],
        [row_block(tile, half)] * 2,
        [like(rows, half)] * 2,
        2 * rows * width * width,
        4 * rows * width,
        "spectra",
        12,
    )(x, spread)


def forward(core, layer, x, mixed, unfold, w1, w2, b1, vec, spread, ahead):
    rows, width = x.shape
    hidden = w1.shape[2]
    half = width // 2
    tile = min(2 * ROWS, rows)
    sub = min(ROWS, tile)
    chunk = min(CHUNK, hidden)
    factor = 1.0 / math.sqrt(width)

    def body(core_ref, x_ref, m0, t0, m1, t1, unfold_ref, w1_ref, w2_ref, b1_ref, vec_ref, spread_ref, *outs):
        out_ref, low_ref, act_ref, slope_ref, unit1_ref, scale1_ref, unit2_ref, scale2_ref = outs[:8]
        b2, mg, ms, og, os = (vec_ref[0, i : i + 1] for i in range(5))
        mixture = mixture_tile(core_ref, m0, t0, m1, t1, unfold_ref).astype(BF)
        lows, totals = [], []
        for at in range(0, tile, sub):
            part = slice(at, at + sub)
            unit, scale = standardize(x_ref[part].astype(F32) + mixture[part].astype(F32))
            normed = unit * mg + ms
            unit1_ref[part] = unit.astype(BF)
            scale1_ref[part] = jnp.broadcast_to(scale, (sub, scale1_ref.shape[1]))
            lows.append(normed.astype(BF))
            low_ref[part] = lows[-1]
            totals.append(normed + b2)
        for start in range(0, hidden, chunk):
            span = slice(start, start + chunk)
            for i, at in enumerate(range(0, tile, sub)):
                part = slice(at, at + sub)
                pre = product(lows[i], w1_ref[0, :, span]) + b1_ref[0, :, span]
                cdf = 0.5 + 0.5 * lax.erf(pre * (1.0 / math.sqrt(2.0)))
                act = (pre * cdf).astype(BF)
                act_ref[part, span] = act
                slope = cdf + pre * (jnp.exp(-0.5 * pre * pre) * (1.0 / math.sqrt(2.0 * math.pi)))
                slope_ref[part, span] = slope.astype(BF)
                totals[i] = totals[i] + product(act, w2_ref[0, span, :])
        for i, at in enumerate(range(0, tile, sub)):
            part = slice(at, at + sub)
            unit, scale = standardize(totals[i])
            unit2_ref[part] = unit.astype(BF)
            scale2_ref[part] = jnp.broadcast_to(scale, (sub, scale2_ref.shape[1]))
            out = (unit * og + os).astype(BF)
            out_ref[part] = out
            if ahead:
                own_ref, other_ref = outs[8:]
                spectra = product(out, spread_ref[...]) * factor
                own_ref[part] = spectra[:, :half].astype(BF)
                other_ref[part] = spectra[:, half:].astype(BF)

    mine, theirs = mixed
    return call(
        body,
        (rows // tile,),
        [scalar_block(), row_block(tile, width)]
        + mixture_specs(rows, half, tile)
        + [
            layer_block(layer, width, hidden),
            layer_block(layer, hidden, width),
            layer_block(layer, 1, hidden),
            layer_block(layer, 5, width),
            whole(width, width),
        ],
        [
            row_block(tile, width),
            row_block(tile, width),
            row_block(tile, hidden),
            row_block(tile, hidden),
            row_block(tile, width),
            row_block(tile, 128),
            row_block(tile, width),
            row_block(tile, 128),
        ]
        + [row_block(tile, half)] * (2 if ahead else 0),
        [
            like(rows, width),
            like(rows, width),
            like(rows, hidden),
            like(rows, hidden),
            like(rows, width),
            like(rows, 128, dtype=F32),
            like(rows, width),
            like(rows, 128, dtype=F32),
        ]
        + [like(rows, half)] * (2 if ahead else 0),
        4 * rows * width * (hidden + width),
        4 * width * hidden + 4 * rows * hidden + 14 * rows * width,
        "layer_forward",
        60,
    )(core, x, mine, mine, theirs, theirs, unfold, w1, w2, b1, vec, spread)


def backward(scalars, layer, grad, mixed, unfold, kept, w1, w2, vec, spread):
    low, act, slope, unit1, scale1, unit2, scale2 = kept
    rows, width = grad.shape
    hidden = w1.shape[2]
    half = width // 2
    tile = min(ROWS, rows)
    squares = hidden // width
    factor = 1.0 / math.sqrt(width)
    count = 0 if mixed is None else 5

    def body(scalar_ref, grad_ref, *refs):
        low_ref, act_ref, slope_ref, unit1_ref, scale1_ref, unit2_ref, scale2_ref, w1_ref, w2_ref, vec_ref, spread_ref = refs[
            count : 11 + count
        ]
        gh_ref, own_ref, other_ref, wide_ref, sums_ref, *block_refs = refs[11 + count : -2]
        in_sum, out_sum = refs[-2:]

        @pl.when(pl.program_id(0) == 0)
        def _():
            for ref in (wide_ref, sums_ref, in_sum, out_sum):
                ref[...] = jnp.zeros_like(ref)

        grad = grad_ref[...].astype(F32)
        if count:
            grad = (grad + mixture_tile(scalar_ref, *refs[:count])).astype(BF).astype(F32)
        mg, og = vec_ref[0, 1:2], vec_ref[0, 3:4]
        unit2 = unit2_ref[...].astype(F32)
        g_branch = standardize_back(grad * og, unit2, scale2_ref[:, :1])
        gb = g_branch.astype(BF)
        total = g_branch
        for square in range(squares):
            span = slice(square * width, (square + 1) * width)
            g_act = contract(gb, w2_ref[0, span, :], 1, 1)
            gp = (g_act * slope_ref[:, span].astype(F32)).astype(BF)
            wide_ref[:, span] += jnp.sum(gp.astype(F32), axis=0, keepdims=True)
            total = total + contract(gp, w1_ref[0, :, span], 1, 1)
            out_sum[square] += contract(act_ref[:, span], gb, 0, 0)
            in_sum[square] += contract(low_ref[...], gp, 0, 0)
        unit1 = unit1_ref[...].astype(F32)
        g_h = standardize_back(total * mg, unit1, scale1_ref[:, :1])
        gh_ref[...] = g_h
        for at, terms in enumerate((gb.astype(F32), total * unit1, total, grad * unit2, grad)):
            sums_ref[at : at + 1] += jnp.sum(terms, axis=0, keepdims=True)
        spectra = product(g_h.astype(BF), spread_ref[...]) * factor
        own_ref[...] = spectra[:, :half].astype(BF)
        other_ref[...] = spectra[:, half:].astype(BF)

        @pl.when(pl.program_id(0) == pl.num_programs(0) - 1)
        def _():
            for owner in range(2):
                part = pl.ds(pl.multiple_of((scalar_ref[0] ^ owner) * half, half), half)
                for use in range(2):
                    for at in range(2):
                        ref = block_refs[2 * owner + use]
                        ref[0, at] = out_sum[(2 * at + 1 - use) ^ scalar_ref[1], part, :].astype(BF)
                        ref[1, at] = in_sum[(2 - 2 * use + at) ^ scalar_ref[1], part, :].astype(BF)

    if count:
        mine, theirs = mixed
        extra = [mine, mine, theirs, theirs, unfold]
        extra_specs = mixture_specs(rows, half, tile)
    else:
        extra, extra_specs = [], []
    return call(
        body,
        (rows // tile,),
        [scalar_block(), row_block(tile, width)]
        + extra_specs
        + [
            row_block(tile, width),
            row_block(tile, hidden),
            row_block(tile, hidden),
            row_block(tile, width),
            row_block(tile, 128),
            row_block(tile, width),
            row_block(tile, 128),
            layer_block(layer, width, hidden),
            layer_block(layer, hidden, width),
            layer_block(layer, 5, width),
            whole(width, width),
        ],
        [
            row_block(tile, width),
            row_block(tile, half),
            row_block(tile, half),
            whole(1, hidden),
            whole(8, width),
        ]
        + [whole(2, 2, half, width)] * 4,
        [
            like(rows, width, dtype=F32),
            like(rows, half),
            like(rows, half),
            like(1, hidden, dtype=F32),
            like(8, width, dtype=F32),
        ]
        + [like(2, 2, half, width)] * 4,
        8 * rows * width * (hidden + width),
        4 * width * hidden + 4 * rows * hidden + 14 * rows * width,
        "layer_backward",
        60,
        [pltpu.VMEM((squares, width, width), F32)] * 2,
    )(scalars, grad, *extra, low, act, slope, unit1, scale1, unit2, scale2, w1, w2, vec, spread)


def backward_last(layer, grad, kept, w1, w2, vec, spread):
    low, act, slope, unit1, scale1, unit2, scale2 = kept
    rows, width = grad.shape
    hidden = w1.shape[2]
    half = width // 2
    tile = min(ROWS, rows)
    chunk = min(CHUNK, hidden)
    factor = 1.0 / math.sqrt(width)

    def body(*refs):
        grad_ref = refs[0]
        slope_ref, unit1_ref, scale1_ref, unit2_ref, scale2_ref, w1_ref, w2_ref, vec_ref, spread_ref = refs[1:10]
        gh_ref, gb_ref, gp_ref, own_ref, other_ref, wide_ref, sums_ref = refs[10:]

        @pl.when(pl.program_id(0) == 0)
        def _():
            wide_ref[...] = jnp.zeros_like(wide_ref)
            sums_ref[...] = jnp.zeros_like(sums_ref)

        grad = grad_ref[...].astype(F32)
        mg, og = vec_ref[0, 1:2], vec_ref[0, 3:4]
        unit2 = unit2_ref[...].astype(F32)
        g_branch = standardize_back(grad * og, unit2, scale2_ref[:, :1])
        gb = g_branch.astype(BF)
        gb_ref[...] = gb
        total = g_branch
        for start in range(0, hidden, chunk):
            span = slice(start, start + chunk)
            g_act = contract(gb, w2_ref[0, span, :], 1, 1)
            gp = (g_act * slope_ref[:, span].astype(F32)).astype(BF)
            gp_ref[:, span] = gp
            wide_ref[:, span] += jnp.sum(gp.astype(F32), axis=0, keepdims=True)
            total = total + contract(gp, w1_ref[0, :, span], 1, 1)
        unit1 = unit1_ref[...].astype(F32)
        g_h = standardize_back(total * mg, unit1, scale1_ref[:, :1])
        gh_ref[...] = g_h
        for at, terms in enumerate((gb.astype(F32), total * unit1, total, grad * unit2, grad)):
            sums_ref[at : at + 1] += jnp.sum(terms, axis=0, keepdims=True)
        spectra = product(g_h.astype(BF), spread_ref[...]) * factor
        own_ref[...] = spectra[:, :half].astype(BF)
        other_ref[...] = spectra[:, half:].astype(BF)

    return call(
        body,
        (rows // tile,),
        [
            row_block(tile, width),
            row_block(tile, hidden),
            row_block(tile, width),
            row_block(tile, 128),
            row_block(tile, width),
            row_block(tile, 128),
            layer_block(layer, width, hidden),
            layer_block(layer, hidden, width),
            layer_block(layer, 5, width),
            whole(width, width),
        ],
        [
            row_block(tile, width),
            row_block(tile, width),
            row_block(tile, hidden),
            row_block(tile, half),
            row_block(tile, half),
            whole(1, hidden),
            whole(8, width),
        ],
        [
            like(rows, width, dtype=F32),
            like(rows, width),
            like(rows, hidden),
            like(rows, half),
            like(rows, half),
            like(1, hidden, dtype=F32),
            like(8, width, dtype=F32),
        ],
        4 * rows * width * (hidden + width),
        4 * width * hidden + 4 * rows * hidden + 14 * rows * width,
        "last_backward",
        58,
    )(grad, slope, unit1, scale1, unit2, scale2, w1, w2, vec, spread)


def grad_blocks(scalars, low, gp, act, gb):
    rows, width = low.shape
    half = width // 2

    def body(scalar_ref, act_ref, gb_ref, low_ref, gp_ref, sent_ref, kept_ref):
        outer = contract(act_ref[...], gb_ref[...], 0, 0).astype(BF)
        inner = contract(low_ref[...], gp_ref[...], 0, 0).astype(BF)

        @pl.when(pl.program_id(0) < 2)
        def _():
            sent_ref[0, 0] = outer
            sent_ref[1, 0] = inner

        @pl.when(pl.program_id(0) >= 2)
        def _():
            kept_ref[0, 0] = outer
            kept_ref[1, 0] = inner

    def out_square(i, s):
        return ((2 * i + 1 - i // 2) % 4) ^ s[1]

    def in_square(i, s):
        return ((i + 2) % 4) ^ s[1]

    return pl.pallas_call(
        body,
        grid_spec=pltpu.PrefetchScalarGridSpec(
            num_scalar_prefetch=1,
            grid=(4,),
            in_specs=[
                pl.BlockSpec((rows, half), lambda i, s: (0, 2 * out_square(i, s) + s[0])),
                pl.BlockSpec((rows, width), lambda i, s: (0, 0)),
                pl.BlockSpec((rows, half), lambda i, s: (0, s[0])),
                pl.BlockSpec((rows, width), lambda i, s: (0, in_square(i, s))),
            ],
            out_specs=[
                pl.BlockSpec((2, 1, half, width), lambda i, s: (0, jnp.minimum(i, 1), 0, 0)),
                pl.BlockSpec((2, 1, half, width), lambda i, s: (0, jnp.maximum(i - 2, 0), 0, 0)),
            ],
        ),
        out_shape=[like(2, 2, half, width)] * 2,
        compiler_params=pltpu.CompilerParams(vmem_limit_bytes=58 << 20),
        cost_estimate=pl.CostEstimate(flops=16 * rows * width * half // COST, bytes_accessed=20 * rows * width // COST, transcendentals=0),
        name="grad_blocks",
    )(scalars, act, gb, low, gp)


def write_weights(scalars, far, sources, begun=None):
    _, slots, piece, width = sources[0][0][0].shape
    half = slots * piece
    flat = [array for pair in sources for source in pair for array in source]

    def body(s, *refs):
        in_ref, out_ref = refs[-2:]

        def write(target, source, top):
            for slot in range(slots):
                at = pl.multiple_of((s[2] + slots - slot) % slots * piece, piece)
                target[0, pl.ds(at + top, piece), :] = source[0, slot].astype(F32)

        for core in range(2):

            @pl.when(s[0] == core)
            def _():
                for at, top in ((0, core * half), (2, (1 - core) * half)):
                    write(out_ref, refs[4 * core + at], top)
                    write(in_ref, refs[4 * core + at + 1], top)

    def source(core):
        return pl.BlockSpec((1, slots, piece, width), lambda k, s: (jnp.where(s[0] == core, k, 0), 0, 0, 0))

    extra = [] if begun is None else list(begun)
    return pl.pallas_call(
        body,
        grid_spec=pltpu.PrefetchScalarGridSpec(
            num_scalar_prefetch=1,
            grid=(2,),
            in_specs=[source(0)] * 4 + [source(1)] * 4 + [pl.BlockSpec(memory_space=pl.ANY)] * len(extra),
            out_specs=[
                pl.BlockSpec((1, width, width), lambda k, s: (0, 0, (k + 2 * far) ^ s[1])),
                pl.BlockSpec((1, width, width), lambda k, s: (0, (2 * k + far) ^ s[1], 0)),
            ],
        ),
        out_shape=[like(1, width, 4 * width, dtype=F32), like(1, 4 * width, width, dtype=F32)],
        input_output_aliases={9: 0, 10: 1} if extra else {},
        compiler_params=pltpu.CompilerParams(vmem_limit_bytes=40 << 20),
        cost_estimate=pl.CostEstimate(flops=0, bytes_accessed=24 * width * width // COST, transcendentals=0),
        name="write_weights",
    )(scalars, *flat, *extra)


def finish(core, g_h, mixed, unfold):
    rows, width = g_h.shape
    half = width // 2
    tile = min(ROWS, rows)

    def body(g_ref, *refs):
        refs[-1][...] = (g_ref[...] + mixture_tile(*refs[:-1])).astype(BF)

    mine, theirs = mixed
    return call(
        body,
        (rows // tile,),
        [row_block(tile, width), scalar_block()] + mixture_specs(rows, half, tile),
        row_block(tile, width),
        like(rows, width),
        2 * rows * width * width,
        8 * rows * width,
        "finish",
        14,
    )(g_h, core, mine, mine, theirs, theirs, unfold)


def bit_pairs(count, bit):
    return [(i, i ^ (1 << bit)) for i in range(count)]


def added(left, right):
    return (left.astype(F32) + right.astype(F32)).astype(BF)


class Line:
    def __init__(self):
        self.last = None

    def __call__(self, step, *args):
        if self.last is not None:
            args, _ = lax.optimization_barrier((args, self.last))
        out = step(*args)
        self.last = min(jax.tree.leaves(out), key=lambda leaf: leaf.size)
        return out

    def after(self, value):
        return lax.optimization_barrier((value, self.last))[0]


class ChipSum:
    def __init__(self):
        self.count = lax.axis_size("dp")
        self.peers = lax.axis_size("seq")

    def across(self, bit, value):
        return lax.ppermute(value, "dp", bit_pairs(self.count, bit))

    def sent(self, mine, theirs):
        return (lambda a, b: [added(a[stream], b[stream]) for stream in range(2)]), (mine, theirs)

    def start_first(self, sent):
        self.first = [self.across(stream, sent[stream]) for stream in range(2)]

    def first_sums(self, mine, theirs):
        def step(a, b, *got):
            sums = [(a[m].astype(F32) + b[m].astype(F32) + got[m].astype(F32)).astype(BF) for m in range(2)]
            return [(part[1], part[0]) for part in sums]

        return step, (mine, theirs, *self.first)

    def start_second(self, sums):
        self.second = [(sums[stream][1], self.across(1 - stream, sums[stream][0])) for stream in range(2)]

    def second_sums(self):
        def step(z, *pairs):
            sums = [added(*pair) for pair in pairs]
            for bit in range(2, self.count.bit_length() - 1):
                sums = [added(part, self.across(bit, part)) for part in sums]
            both = jnp.stack(sums)
            both = both.reshape(2, self.peers, -1, both.shape[-1])
            return [lax.dynamic_index_in_dim(both, (z + d) % self.peers, 1, keepdims=False) for d in range(self.peers)]

        return step, (lax.axis_index("seq"), *self.second)

    def along(self, value, by):
        return lax.ppermute(value, "seq", [(i, (i + by) % self.peers) for i in range(self.peers)])

    def start_scatter(self, pieces):
        self.kept = pieces[0]
        self.got = [self.along(piece, d) for d, piece in enumerate(pieces) if d]

    def scattered(self):
        def step(kept, *got):
            return sum((g.astype(F32) for g in got), kept.astype(F32)).astype(BF)

        return step, (self.kept, *self.got)

    def start_gather(self, piece):
        self.kept = piece
        self.got = [self.along(piece, d) for d in range(1, self.peers)]

    def gathered(self):
        def step(*pieces):
            return [jnp.stack([piece[at] for piece in pieces]) for at in range(2)]

        return step, (self.kept, *self.got)

    def start_back(self, streams):
        self.own = streams
        self.near = [self.across(1 - stream, streams[stream]) for stream in range(2)]

    def paired(self):
        def step(a, b, c, d):
            return jnp.stack([a, b]), jnp.stack([c, d])

        return step, (self.own[0], self.near[0], self.own[1], self.near[1])

    def start_last(self, pairs):
        self.pairs = pairs
        self.far = [self.across(stream, pairs[stream]) for stream in range(2)]

def small_hops():
    hops = []
    for axis in ("pipe", "seq", "dp"):
        count = lax.axis_size(axis)
        hops += [(axis, bit_pairs(count, bit)) for bit in range(count.bit_length() - 1)]
    return hops


def on_device(
    inputs,
    cotangent,
    in_weight,
    in_bias,
    out_weight,
    out_bias,
    mix_gain,
    mix_shift,
    out_gain,
    out_shift,
):
    rows, width = inputs.shape[1:]
    hidden = in_weight.shape[2]
    peers = lax.axis_size("seq")
    blocks = peers // 2
    half = width // 2
    core = lax.axis_index("pipe")
    z = lax.axis_index("seq")
    first = core == 0
    low = z < blocks
    local = low == first
    block = jnp.minimum(z, peers - 1 - z)
    which = core.astype(jnp.int32).reshape(1)

    def place(member, is_low):
        return member if is_low else peers - 1 - member

    group_shifts = [
        [(place(b, side), place((b + d) % blocks, side)) for side in (True, False) for b in range(blocks)]
        for d in range(1, blocks)
    ]
    in_pairs = []
    out_pairs = []
    for i in range(peers):
        facing = peers - 1 - i
        source = peers + i if i < blocks else i
        in_pairs.append((source, facing if i < blocks else peers + facing))
        out_pairs.append((source, peers + facing if source < peers else facing))

    row_ids = lax.broadcasted_iota(jnp.int32, (rows, rows), 0)
    col_ids = lax.broadcasted_iota(jnp.int32, (rows, rows), 1)
    order = (col_ids == jnp.where(first, row_ids, (rows - row_ids) % rows)).astype(BF)

    def picked(items):
        return jnp.where(low, items[1], items[0]), jnp.where(low, items[0], items[1])

    def arranged(kept, moved):
        return product(order, jnp.where(local, kept, moved)).astype(BF)

    turned = z >= blocks
    back_order = (col_ids == jnp.where(turned, (rows - row_ids) % rows, row_ids)).astype(BF)

    def give_start(value):
        return value, lax.ppermute(value, ("pipe", "seq"), out_pairs)

    def give_pick(value, moved):
        return jnp.where(local, value, moved)

    def give_cut(block):
        return jnp.where(first, block[:, :half], block[:, half:]), jnp.where(first, block[:, half:], block[:, :half])

    def give_end(mine, beside):
        near = jnp.where(local, mine, beside)
        far = jnp.where(local, beside, mine)
        return jnp.stack(
            [product(back_order, part).astype(BF) for part in (jnp.where(low, near, far), jnp.where(low, far, near))]
        )

    sent, x = picked(inputs)
    x = arranged(x, lax.ppermute(sent, ("pipe", "seq"), in_pairs))
    vectors = jnp.concatenate([in_bias[0], out_bias[0], mix_gain[0], mix_shift[0], out_gain[0], out_shift[0]])
    other_vectors = swap_cores(vectors)
    vectors = jnp.where(first, jnp.stack([vectors, other_vectors]), jnp.stack([other_vectors, vectors]))
    b1 = vectors[:, :hidden].reshape(2, 1, hidden)
    vec = vectors[:, hidden:].reshape(2, 5, width)
    w1 = lax.all_gather(in_weight, "pipe", axis=0, tiled=True)
    w2 = lax.all_gather(out_weight, "pipe", axis=0, tiled=True)
    spread, unfold = feature_tables(width, core)
    cos, sin = token_tables(block, rows, blocks, rows * peers)
    factor = 1.0 / math.sqrt(rows * peers)

    line = Line()

    def fold(own, came):
        return line(lambda a, b: fold_spectra(which, a, b), own, came)

    def spread_out(folded):
        return [lax.ppermute(folded, "seq", pairs) for pairs in group_shifts]

    def part(folded):
        return line(lambda f: transform_part(cos, sin, 0, f), folded)

    def rest(begun, parts):
        return line(lambda a, *b: transform_rest(which, cos, sin, a, list(b), factor), begun, *parts)

    kept = []
    own, other = line(lambda v: spectra_call(which, v, spread), x)
    cot_sent, cot_kept = line.after(picked(cotangent))
    for layer in range(2):
        folded = fold(own, swap_cores(other))
        parts = spread_out(folded)
        begun = part(folded)
        if layer == 1:
            grad = line(arranged, cot_kept, cot_moved)
        mixed = rest(begun, parts)
        came = swap_cores(mixed)
        if layer == 0:
            cot_moved = lax.ppermute(line.after(cot_sent), ("pipe", "seq"), in_pairs)
        x, *saved = line(
            lambda v, m, l=layer: forward(which, l, v, m, unfold, w1, w2, b1, vec, spread, l == 0), x, (mixed, came)
        )
        kept.append(saved[:7])
        if layer == 0:
            own, other = saved[7:]

    index = lax.axis_index("dp") & 3
    scalars = jnp.stack([core, index]).astype(jnp.int32)

    def back(layer, grad, mixed):
        return line(
            lambda g, m, k: backward(scalars, layer, g, m, unfold, k, w1, w2, vec, spread), grad, mixed, kept[layer]
        )

    def run(work):
        return line(work[0], *work[1])

    def flat_small(wide, narrow):
        return jnp.concatenate([wide.reshape(-1), narrow[:5].reshape(-1)])

    late, early = ChipSum(), ChipSum()
    to_theirs = jnp.stack([1 - core, index]).astype(jnp.int32)

    def blocks_of(target, gp, gb):
        return line(grad_blocks, target, kept[1][0], gp, kept[1][1], gb)

    out_moved = give_start(x)
    grad, gb, gp, own, other, wide1, narrow1 = line(
        lambda g, k: backward_last(1, g, k, w1, w2, vec, spread), grad, kept[1]
    )

    came = swap_cores(other)
    other_sent, other_kept = blocks_of(to_theirs, gp, gb)
    folded = fold(own, came)

    parts = spread_out(line.after(folded))
    got_sent, got_kept1 = swap_cores(line.after((other_sent, other_kept)))
    my_sent, my_kept1 = blocks_of(scalars, gp, gb)
    begun = part(folded)
    mixed = rest(begun, parts)

    came = swap_cores(mixed)
    sent = run(early.sent(my_sent, got_sent))

    early.start_first(line.after(sent))
    grad, own, other, wide0, narrow0, my_sent, my_kept, other_sent, other_kept = back(0, grad, (mixed, came))

    sums = run(early.first_sums(my_kept1, got_kept1))
    out_block = line(give_pick, *out_moved)

    got_sent = swap_cores(line.after(other_sent))
    came = swap_cores(line.after(other))
    early.start_second(line.after(sums))
    hops = iter(small_hops())
    small = line.after(jnp.stack([flat_small(wide0, narrow0), flat_small(wide1, narrow1)]))

    def start_hop():
        axis, pairs = next(hops)
        return lax.ppermute(line.after(small), axis, pairs)

    def end_hop(got):
        return line(lambda a, b: a + b, small, got)

    hop = start_hop()
    folded = fold(own, came)
    sent = run(late.sent(my_sent, got_sent))
    pieces = run(early.second_sums())
    small = end_hop(hop)

    late.start_first(line.after(sent))
    early.start_scatter(line.after(pieces))
    got_kept0 = swap_cores(line.after(other_kept))
    hop = start_hop()
    begun = part(folded)
    out_mine, out_theirs = line(give_cut, out_block)
    piece = run(early.scattered())
    small = end_hop(hop)
    sums = run(late.first_sums(my_kept, got_kept0))

    late.start_second(line.after(sums))
    early.start_gather(line.after(piece))
    out_beside = swap_cores(line.after(out_theirs))
    pieces = run(late.second_sums())
    streams = run(early.gathered())

    late.start_scatter(line.after(pieces))
    early.start_back(line.after(streams))
    hop = start_hop()
    out = line(give_end, out_mine, out_beside)
    pairs = run(early.paired())

    early.start_last(line.after(pairs))
    piece = run(late.scattered())
    small = end_hop(hop)

    late.start_gather(line.after(piece))
    pairs_far1 = lax.ppermute(line.after(pairs), "pipe", [(0, 1)])
    streams = run(late.gathered())
    far1 = line.after(early.far)

    streams, far1 = lax.optimization_barrier((streams, far1))
    late.start_back(streams)
    parts = spread_out(line.after(folded))
    far1_far = lax.ppermute(line.after(far1), "pipe", [(0, 1)])
    pairs0 = run(late.paired())

    late.start_last(line.after(pairs0))
    pairs_far0 = lax.ppermute(line.after(pairs0), "pipe", [(1, 0)])
    mixed = rest(begun, parts)
    came = swap_cores(mixed)
    in_ready = line(lambda g, m: finish(which, g, m, unfold), grad, (mixed, came))
    in_moved = give_start(in_ready)
    scalars = jnp.stack([core, index, z]).astype(jnp.int32)
    begun = line(lambda *v: write_weights(scalars, 0, v), (pairs0, pairs_far0), (pairs, pairs_far1))
    far0 = line.after(late.far)

    far0_far = lax.ppermute(far0, "pipe", [(1, 0)])
    hop = start_hop()
    g_w1, g_w2 = line(lambda b, *v: write_weights(scalars, 1, v, b), begun, (far0, far0_far), (far1, far1_far))
    small = end_hop(hop)
    hop = start_hop()
    in_mine, in_theirs = line(lambda *v: give_cut(give_pick(*v)), *in_moved)
    in_beside = swap_cores(line.after(in_theirs))
    small = end_hop(hop)
    in_grad = line(give_end, in_mine, in_beside)
    for axis, hop in hops:
        small = line(lambda a, b: a + b, small, lax.ppermute(small, axis, hop))
    small = jnp.where(first, small[0], small[1])
    g_b1 = small[:hidden]
    g_b2, g_mg, g_ms, g_og, g_os = (small[hidden + i * width : hidden + (i + 1) * width] for i in range(5))
    return (
        out,
        in_grad,
        g_w1,
        g_b1[None],
        g_w2,
        g_b2[None],
        g_mg[None],
        g_ms[None],
        g_og[None],
        g_os[None],
    )


def solution(mesh):
    return jax.shard_map(
        on_device,
        mesh=mesh,
        in_specs=(
            P("dp", "seq", None),
            P("dp", "seq", None),
            P("pipe", None, None),
            P("pipe", None),
            P("pipe", None, None),
            P("pipe", None),
            P("pipe", None),
            P("pipe", None),
            P("pipe", None),
            P("pipe", None),
        ),
        out_specs=(
            P("dp", "seq", "pipe"),
            P("dp", "seq", "pipe"),
            P("pipe", None, None),
            P("pipe", None),
            P("pipe", None, None),
            P("pipe", None),
            P("pipe", None),
            P("pipe", None),
            P("pipe", None),
            P("pipe", None),
        ),
        check_vma=False,
    )
```

```python
import math

import jax
import jax.numpy as jnp
from jax import lax
from jax.experimental import pallas as pl
from jax.experimental.pallas import tpu as pltpu
from jax.sharding import PartitionSpec as P

BF = jnp.bfloat16
F32 = jnp.float32
PAD = 16
ROWS = 256
CHUNK = 768
COST = 64


def product(left, right):
    return jnp.dot(left, right, preferred_element_type=F32)


def contract(left, right, left_dim, right_dim):
    dims = (((left_dim,), (right_dim,)), ((), ()))
    return lax.dot_general(left, right, dims, preferred_element_type=F32)


def swap_cores(value):
    return lax.ppermute(value, "pipe", [(0, 1), (1, 0)])


def turn(phase, length):
    angles = (phase % length).astype(F32) * (2.0 * math.pi / length)
    return jnp.cos(angles), jnp.sin(angles)


def column_sets(width):
    quarter, half = width // 4, width // 2
    return (
        (list(range(quarter)) + [half], list(range(1, quarter))),
        (list(range(quarter, half)), list(range(quarter, half))),
    )


def feature_tables(width, core):
    sets = column_sets(width)
    order = []
    for cos_ids, sin_ids in sets:
        order.append(([k for k in cos_ids] + [k for k in sin_ids], [0] * len(cos_ids) + [1] * len(sin_ids)))
    ids_a = jnp.array(order[0][0] + order[1][0], jnp.int32)
    ids_b = jnp.array(order[1][0] + order[0][0], jnp.int32)
    odd_a = jnp.array(order[0][1] + order[1][1], jnp.int32)
    odd_b = jnp.array(order[1][1] + order[0][1], jnp.int32)
    first = core == 0
    ids = jnp.where(first, ids_a, ids_b)
    odd = jnp.where(first, odd_a, odd_b)
    sign = jnp.where(first, 1.0, -1.0)
    rows = jnp.arange(width, dtype=jnp.int32)
    cos, sin = turn(rows[:, None] * ids[None, :], width)
    spread = jnp.where(odd[None, :] == 1, -sign * sin, cos).astype(BF)
    direct = rows[None, :] == ids[:, None]
    mirror = rows[None, :] == ((width - ids) % width)[:, None]
    even_rows = (direct | mirror).astype(F32)
    odd_rows = sign * (direct.astype(F32) - mirror.astype(F32))
    unfold = jnp.where(odd[:, None] == 1, odd_rows, even_rows).astype(BF)
    return spread, unfold


def token_tables(block, rows, blocks, length):
    tall = rows + PAD
    inner = jnp.arange(tall, dtype=jnp.int32)
    slots = jnp.arange(blocks, dtype=jnp.int32)
    columns = ((block + blocks - slots) % blocks * rows)[:, None, None] + inner
    coarse = block * rows + PAD * jnp.arange(tall // PAD, dtype=jnp.int32)
    fine = jnp.arange(PAD, dtype=jnp.int32)
    cos_c, sin_c = turn(coarse[:, None] * columns, length)
    cos_f, sin_f = turn(fine[:, None] * columns, length)
    cos_c, sin_c, cos_f, sin_f = cos_c[:, :, None], sin_c[:, :, None], cos_f[:, None], sin_f[:, None]
    cos = (cos_c * cos_f - sin_c * sin_f).astype(BF)
    sin = (sin_c * cos_f + cos_c * sin_f).astype(BF)
    return cos.reshape(blocks, tall, tall), sin.reshape(blocks, tall, tall)


def row_block(height, width):
    return pl.BlockSpec((height, width), lambda i: (i, 0))


def whole(*shape):
    return pl.BlockSpec(shape, lambda *_: (0,) * len(shape), pipeline_mode=pl.Buffered(1))


def scalar_block():
    return pl.BlockSpec(memory_space=pltpu.SMEM)


def layer_block(layer, *shape):
    return pl.BlockSpec((1, *shape), lambda i: (layer,) + (0,) * len(shape), pipeline_mode=pl.Buffered(1))


def call(body, grid, in_specs, out_specs, out_shape, flops, moved, name, vmem, scratch=()):
    return pl.pallas_call(
        body,
        grid=grid,
        in_specs=in_specs,
        out_specs=out_specs,
        out_shape=out_shape,
        scratch_shapes=scratch,
        compiler_params=pltpu.CompilerParams(vmem_limit_bytes=vmem << 20),
        cost_estimate=pl.CostEstimate(flops=flops // COST, bytes_accessed=moved // COST, transcendentals=0),
        name=name,
    )


def like(*shape, dtype=BF):
    return jax.ShapeDtypeStruct(shape, dtype)


def divisor(count, most):
    return max(d for d in range(1, most + 1) if count % d == 0)


def fold_spectra(core, own, recv):
    rows, half = own.shape

    def body(core_ref, own_ref, recv_ref, out_ref):
        first = core_ref[0] == 0
        out_ref[:rows] = (own_ref[...].astype(F32) + recv_ref[...].astype(F32)).astype(BF)
        mine, theirs = own_ref[:PAD], recv_ref[:PAD]
        at = lax.broadcasted_iota(jnp.int32, (PAD, half), 0)
        low = jnp.where(first, mine, theirs)
        high = jnp.where(first, theirs, mine)
        out_ref[:PAD] = jnp.where(at == 0, low, out_ref[:PAD])
        out_ref[rows:] = jnp.where(at == 0, high, jnp.zeros_like(high))

    spec = pl.BlockSpec((rows, half), lambda i: (0, 0))
    return call(
        body,
        (1,),
        [scalar_block(), spec, spec],
        pl.BlockSpec((rows + PAD, half), lambda i: (0, 0)),
        like(rows + PAD, half),
        rows * half,
        6 * rows * half,
        "fold_spectra",
        8,
    )(core, own, recv)


def transform_part(cos, sin, slot, part):
    tall, half = part.shape
    wide = -(-(half // 2 + 1) // 128) * 128
    tile = divisor(tall // PAD, 17) * PAD

    def body(cos_ref, sin_ref, part_ref, out_ref):
        out_ref[:, :wide] = product(cos_ref[0], part_ref[:, :wide])
        out_ref[:, wide:] = product(sin_ref[0], part_ref[:, half - wide :])

    table = pl.BlockSpec((1, tile, tall), lambda i: (slot, i, 0))
    return call(
        body,
        (tall // tile,),
        [table, table, whole(tall, half)],
        row_block(tile, 2 * wide),
        like(tall, 2 * wide, dtype=F32),
        4 * tall * tall * wide,
        4 * tall * (tall + 2 * wide),
        "transform_part",
        12,
    )(cos, sin, part)


def transform_rest(core, cos, sin, begun, parts, factor):
    tall, half = parts[0].shape
    wide = begun.shape[1] // 2
    tile = divisor(tall // PAD, 17) * PAD
    lead = half - wide

    def body(*refs):
        core_ref, begun_ref = refs[:2]
        tables = refs[2 : 2 + 2 * len(parts)]
        part_refs = refs[2 + 2 * len(parts) : -1]
        out_ref = refs[-1]
        even, odd = begun_ref[:, :wide], begun_ref[:, wide:]
        for at, part_ref in enumerate(part_refs):
            even = even + product(tables[2 * at][0], part_ref[:, :wide])
            odd = odd + product(tables[2 * at + 1][0], part_ref[:, lead:])
        lanes = lax.broadcasted_iota(jnp.int32, (tile, wide - lead), 1) + lead
        cos_count = half // 2 + 1 - core_ref[0]
        middle = jnp.where(lanes < cos_count, even[:, lead:], odd[:, : wide - lead])
        out_ref[:, :lead] = (even[:, :lead] * factor).astype(BF)
        out_ref[:, lead:wide] = (middle * factor).astype(BF)
        out_ref[:, wide:] = (odd[:, wide - lead :] * factor).astype(BF)

    tables, specs = [], []
    for at in range(len(parts)):
        spec = pl.BlockSpec((1, tile, tall), lambda i, at=at: (at + 1, i, 0))
        tables += [cos, sin]
        specs += [spec, spec]
    return call(
        body,
        (tall // tile,),
        [scalar_block(), row_block(tile, 2 * wide)] + specs + [whole(tall, half)] * len(parts),
        row_block(tile, half),
        like(tall, half),
        4 * tall * tall * wide * len(parts),
        4 * tall * (tall * len(parts) + 2 * wide),
        "transform_rest",
        14,
    )(core, begun, *tables, *parts)


def transform(core, own, recv, cos, sin, group_shifts, factor, beside=None):
    folded = fold_spectra(core, own, recv)
    parts = [lax.ppermute(folded, "seq", pairs) for pairs in group_shifts]
    begun = transform_part(cos, sin, 0, folded)
    mixed = transform_rest(core, cos, sin, begun, parts, factor)
    return mixed, swap_cores(mixed)


def standardize(hidden):
    centered = hidden - jnp.mean(hidden, axis=-1, keepdims=True)
    spread = jnp.mean(centered * centered, axis=-1, keepdims=True)
    scale = lax.rsqrt(spread + 1e-05)
    return centered * scale, scale


def standardize_back(grad, unit, scale):
    mean_grad = jnp.mean(grad, axis=-1, keepdims=True)
    mean_both = jnp.mean(grad * unit, axis=-1, keepdims=True)
    return (grad - mean_grad - unit * mean_both) * scale


def mixture_tile(core_ref, mine_ref, mine_top, theirs_ref, theirs_top, unfold_ref):
    tile, half = mine_ref.shape
    at = lax.broadcasted_iota(jnp.int32, (tile, half), 0)
    odd_row = (at == 0) & (core_ref[0] == 1) & (pl.program_id(0) == 0)
    mine = jnp.where(odd_row, mine_top[:1], mine_ref[...])
    theirs = jnp.where(odd_row, theirs_top[:1], theirs_ref[...])
    return product(mine, unfold_ref[:half]) + product(theirs, unfold_ref[half:])


def mixture_specs(rows, half, tile):
    block = row_block(tile, half)
    top = pl.BlockSpec((PAD, half), lambda i: (rows // PAD, 0))
    return [block, top, block, top, whole(2 * half, 2 * half)]


def spectra_call(core, x, spread):
    rows, width = x.shape
    half = width // 2
    tile = min(ROWS, rows)
    factor = 1.0 / math.sqrt(width)

    def body(x_ref, spread_ref, own_ref, other_ref):
        spectra = product(x_ref[...], spread_ref[...]) * factor
        own_ref[...] = spectra[:, :half].astype(BF)
        other_ref[...] = spectra[:, half:].astype(BF)

    return call(
        body,
        (rows // tile,),
        [row_block(tile, width), whole(width, width)],
        [row_block(tile, half)] * 2,
        [like(rows, half)] * 2,
        2 * rows * width * width,
        4 * rows * width,
        "spectra",
        12,
    )(x, spread)


def forward(core, layer, x, mixed, unfold, w1, w2, b1, vec, spread, ahead):
    rows, width = x.shape
    hidden = w1.shape[2]
    half = width // 2
    tile = min(2 * ROWS, rows)
    sub = min(ROWS, tile)
    chunk = min(CHUNK, hidden)
    factor = 1.0 / math.sqrt(width)

    def body(core_ref, x_ref, m0, t0, m1, t1, unfold_ref, w1_ref, w2_ref, b1_ref, vec_ref, spread_ref, *outs):
        out_ref, low_ref, act_ref, slope_ref, unit1_ref, scale1_ref, unit2_ref, scale2_ref = outs[:8]
        b2, mg, ms, og, os = (vec_ref[0, i : i + 1] for i in range(5))
        mixture = mixture_tile(core_ref, m0, t0, m1, t1, unfold_ref).astype(BF)
        lows, totals = [], []
        for at in range(0, tile, sub):
            part = slice(at, at + sub)
            unit, scale = standardize(x_ref[part].astype(F32) + mixture[part].astype(F32))
            normed = unit * mg + ms
            unit1_ref[part] = unit.astype(BF)
            scale1_ref[part] = jnp.broadcast_to(scale, (sub, scale1_ref.shape[1]))
            lows.append(normed.astype(BF))
            low_ref[part] = lows[-1]
            totals.append(normed + b2)
        for start in range(0, hidden, chunk):
            span = slice(start, start + chunk)
            for i, at in enumerate(range(0, tile, sub)):
                part = slice(at, at + sub)
                pre = product(lows[i], w1_ref[0, :, span]) + b1_ref[0, :, span]
                cdf = 0.5 + 0.5 * lax.erf(pre * (1.0 / math.sqrt(2.0)))
                act = (pre * cdf).astype(BF)
                act_ref[part, span] = act
                slope = cdf + pre * (jnp.exp(-0.5 * pre * pre) * (1.0 / math.sqrt(2.0 * math.pi)))
                slope_ref[part, span] = slope.astype(BF)
                totals[i] = totals[i] + product(act, w2_ref[0, span, :])
        for i, at in enumerate(range(0, tile, sub)):
            part = slice(at, at + sub)
            unit, scale = standardize(totals[i])
            unit2_ref[part] = unit.astype(BF)
            scale2_ref[part] = jnp.broadcast_to(scale, (sub, scale2_ref.shape[1]))
            out = (unit * og + os).astype(BF)
            out_ref[part] = out
            if ahead:
                own_ref, other_ref = outs[8:]
                spectra = product(out, spread_ref[...]) * factor
                own_ref[part] = spectra[:, :half].astype(BF)
                other_ref[part] = spectra[:, half:].astype(BF)

    mine, theirs = mixed
    return call(
        body,
        (rows // tile,),
        [scalar_block(), row_block(tile, width)]
        + mixture_specs(rows, half, tile)
        + [
            layer_block(layer, width, hidden),
            layer_block(layer, hidden, width),
            layer_block(layer, 1, hidden),
            layer_block(layer, 5, width),
            whole(width, width),
        ],
        [
            row_block(tile, width),
            row_block(tile, width),
            row_block(tile, hidden),
            row_block(tile, hidden),
            row_block(tile, width),
            row_block(tile, 128),
            row_block(tile, width),
            row_block(tile, 128),
        ]
        + [row_block(tile, half)] * (2 if ahead else 0),
        [
            like(rows, width),
            like(rows, width),
            like(rows, hidden),
            like(rows, hidden),
            like(rows, width),
            like(rows, 128, dtype=F32),
            like(rows, width),
            like(rows, 128, dtype=F32),
        ]
        + [like(rows, half)] * (2 if ahead else 0),
        4 * rows * width * (hidden + width),
        4 * width * hidden + 4 * rows * hidden + 14 * rows * width,
        "layer_forward",
        60,
    )(core, x, mine, mine, theirs, theirs, unfold, w1, w2, b1, vec, spread)


def backward(scalars, layer, grad, mixed, unfold, kept, w1, w2, vec, spread):
    low, act, slope, unit1, scale1, unit2, scale2 = kept
    rows, width = grad.shape
    hidden = w1.shape[2]
    half = width // 2
    tile = min(ROWS, rows)
    squares = hidden // width
    factor = 1.0 / math.sqrt(width)
    count = 0 if mixed is None else 5

    def body(scalar_ref, grad_ref, *refs):
        low_ref, act_ref, slope_ref, unit1_ref, scale1_ref, unit2_ref, scale2_ref, w1_ref, w2_ref, vec_ref, spread_ref = refs[
            count : 11 + count
        ]
        gh_ref, own_ref, other_ref, wide_ref, sums_ref, *block_refs = refs[11 + count : -2]
        in_sum, out_sum = refs[-2:]

        @pl.when(pl.program_id(0) == 0)
        def _():
            for ref in (wide_ref, sums_ref, in_sum, out_sum):
                ref[...] = jnp.zeros_like(ref)

        grad = grad_ref[...].astype(F32)
        if count:
            grad = (grad + mixture_tile(scalar_ref, *refs[:count])).astype(BF).astype(F32)
        mg, og = vec_ref[0, 1:2], vec_ref[0, 3:4]
        unit2 = unit2_ref[...].astype(F32)
        g_branch = standardize_back(grad * og, unit2, scale2_ref[:, :1])
        gb = g_branch.astype(BF)
        total = g_branch
        for square in range(squares):
            span = slice(square * width, (square + 1) * width)
            g_act = contract(gb, w2_ref[0, span, :], 1, 1)
            gp = (g_act * slope_ref[:, span].astype(F32)).astype(BF)
            wide_ref[:, span] += jnp.sum(gp.astype(F32), axis=0, keepdims=True)
            total = total + contract(gp, w1_ref[0, :, span], 1, 1)
            out_sum[square] += contract(act_ref[:, span], gb, 0, 0)
            in_sum[square] += contract(low_ref[...], gp, 0, 0)
        unit1 = unit1_ref[...].astype(F32)
        g_h = standardize_back(total * mg, unit1, scale1_ref[:, :1])
        gh_ref[...] = g_h
        for at, terms in enumerate((gb.astype(F32), total * unit1, total, grad * unit2, grad)):
            sums_ref[at : at + 1] += jnp.sum(terms, axis=0, keepdims=True)
        spectra = product(g_h.astype(BF), spread_ref[...]) * factor
        own_ref[...] = spectra[:, :half].astype(BF)
        other_ref[...] = spectra[:, half:].astype(BF)

        @pl.when(pl.program_id(0) == pl.num_programs(0) - 1)
        def _():
            for owner in range(2):
                part = pl.ds(pl.multiple_of((scalar_ref[0] ^ owner) * half, half), half)
                for use in range(2):
                    for at in range(2):
                        ref = block_refs[2 * owner + use]
                        ref[0, at] = out_sum[(2 * at + 1 - use) ^ scalar_ref[1], part, :].astype(BF)
                        ref[1, at] = in_sum[(2 - 2 * use + at) ^ scalar_ref[1], part, :].astype(BF)

    if count:
        mine, theirs = mixed
        extra = [mine, mine, theirs, theirs, unfold]
        extra_specs = mixture_specs(rows, half, tile)
    else:
        extra, extra_specs = [], []
    return call(
        body,
        (rows // tile,),
        [scalar_block(), row_block(tile, width)]
        + extra_specs
        + [
            row_block(tile, width),
            row_block(tile, hidden),
            row_block(tile, hidden),
            row_block(tile, width),
            row_block(tile, 128),
            row_block(tile, width),
            row_block(tile, 128),
            layer_block(layer, width, hidden),
            layer_block(layer, hidden, width),
            layer_block(layer, 5, width),
            whole(width, width),
        ],
        [
            row_block(tile, width),
            row_block(tile, half),
            row_block(tile, half),
            whole(1, hidden),
            whole(8, width),
        ]
        + [whole(2, 2, half, width)] * 4,
        [
            like(rows, width, dtype=F32),
            like(rows, half),
            like(rows, half),
            like(1, hidden, dtype=F32),
            like(8, width, dtype=F32),
        ]
        + [like(2, 2, half, width)] * 4,
        8 * rows * width * (hidden + width),
        4 * width * hidden + 4 * rows * hidden + 14 * rows * width,
        "layer_backward",
        60,
        [pltpu.VMEM((squares, width, width), F32)] * 2,
    )(scalars, grad, *extra, low, act, slope, unit1, scale1, unit2, scale2, w1, w2, vec, spread)


def backward_last(layer, grad, kept, w1, w2, vec, spread):
    low, act, slope, unit1, scale1, unit2, scale2 = kept
    rows, width = grad.shape
    hidden = w1.shape[2]
    half = width // 2
    tile = min(ROWS, rows)
    chunk = min(CHUNK, hidden)
    factor = 1.0 / math.sqrt(width)

    def body(*refs):
        grad_ref = refs[0]
        slope_ref, unit1_ref, scale1_ref, unit2_ref, scale2_ref, w1_ref, w2_ref, vec_ref, spread_ref = refs[1:10]
        gh_ref, gb_ref, gp_ref, own_ref, other_ref, wide_ref, sums_ref = refs[10:]

        @pl.when(pl.program_id(0) == 0)
        def _():
            wide_ref[...] = jnp.zeros_like(wide_ref)
            sums_ref[...] = jnp.zeros_like(sums_ref)

        grad = grad_ref[...].astype(F32)
        mg, og = vec_ref[0, 1:2], vec_ref[0, 3:4]
        unit2 = unit2_ref[...].astype(F32)
        g_branch = standardize_back(grad * og, unit2, scale2_ref[:, :1])
        gb = g_branch.astype(BF)
        gb_ref[...] = gb
        total = g_branch
        for start in range(0, hidden, chunk):
            span = slice(start, start + chunk)
            g_act = contract(gb, w2_ref[0, span, :], 1, 1)
            gp = (g_act * slope_ref[:, span].astype(F32)).astype(BF)
            gp_ref[:, span] = gp
            wide_ref[:, span] += jnp.sum(gp.astype(F32), axis=0, keepdims=True)
            total = total + contract(gp, w1_ref[0, :, span], 1, 1)
        unit1 = unit1_ref[...].astype(F32)
        g_h = standardize_back(total * mg, unit1, scale1_ref[:, :1])
        gh_ref[...] = g_h
        for at, terms in enumerate((gb.astype(F32), total * unit1, total, grad * unit2, grad)):
            sums_ref[at : at + 1] += jnp.sum(terms, axis=0, keepdims=True)
        spectra = product(g_h.astype(BF), spread_ref[...]) * factor
        own_ref[...] = spectra[:, :half].astype(BF)
        other_ref[...] = spectra[:, half:].astype(BF)

    return call(
        body,
        (rows // tile,),
        [
            row_block(tile, width),
            row_block(tile, hidden),
            row_block(tile, width),
            row_block(tile, 128),
            row_block(tile, width),
            row_block(tile, 128),
            layer_block(layer, width, hidden),
            layer_block(layer, hidden, width),
            layer_block(layer, 5, width),
            whole(width, width),
        ],
        [
            row_block(tile, width),
            row_block(tile, width),
            row_block(tile, hidden),
            row_block(tile, half),
            row_block(tile, half),
            whole(1, hidden),
            whole(8, width),
        ],
        [
            like(rows, width, dtype=F32),
            like(rows, width),
            like(rows, hidden),
            like(rows, half),
            like(rows, half),
            like(1, hidden, dtype=F32),
            like(8, width, dtype=F32),
        ],
        4 * rows * width * (hidden + width),
        4 * width * hidden + 4 * rows * hidden + 14 * rows * width,
        "last_backward",
        58,
    )(grad, slope, unit1, scale1, unit2, scale2, w1, w2, vec, spread)


def grad_blocks(scalars, low, gp, act, gb):
    rows, width = low.shape
    half = width // 2

    def body(scalar_ref, act_ref, gb_ref, low_ref, gp_ref, *refs):
        outer = contract(act_ref[...], gb_ref[...], 0, 0).astype(BF)
        inner = contract(low_ref[...], gp_ref[...], 0, 0).astype(BF)

        def write(mine, theirs):
            mine[0, 0], mine[1, 0] = outer[part], inner[part]
            theirs[0, 0], theirs[1, 0] = outer[rest], inner[rest]

        for core in range(2):
            part, rest = slice(core * half, (core + 1) * half), slice((1 - core) * half, (2 - core) * half)

            @pl.when((scalar_ref[0] == core) & (pl.program_id(0) < 2))
            def _():
                write(refs[0], refs[2])

            @pl.when((scalar_ref[0] == core) & (pl.program_id(0) >= 2))
            def _():
                write(refs[1], refs[3])

    def out_square(i, s):
        return ((2 * i + 1 - i // 2) % 4) ^ s[1]

    def in_square(i, s):
        return ((i + 2) % 4) ^ s[1]

    sent = pl.BlockSpec((2, 1, half, width), lambda i, s: (0, jnp.minimum(i, 1), 0, 0))
    held = pl.BlockSpec((2, 1, half, width), lambda i, s: (0, jnp.maximum(i - 2, 0), 0, 0))
    return pl.pallas_call(
        body,
        grid_spec=pltpu.PrefetchScalarGridSpec(
            num_scalar_prefetch=1,
            grid=(4,),
            in_specs=[
                pl.BlockSpec((rows, width), lambda i, s: (0, out_square(i, s))),
                pl.BlockSpec((rows, width), lambda i, s: (0, 0)),
                pl.BlockSpec((rows, width), lambda i, s: (0, 0)),
                pl.BlockSpec((rows, width), lambda i, s: (0, in_square(i, s))),
            ],
            out_specs=[sent, held, sent, held],
        ),
        out_shape=[like(2, 2, half, width)] * 4,
        compiler_params=pltpu.CompilerParams(vmem_limit_bytes=58 << 20),
        cost_estimate=pl.CostEstimate(flops=16 * rows * width * width // COST, bytes_accessed=20 * rows * width // COST, transcendentals=0),
        name="grad_blocks",
    )(scalars, act, gb, low, gp)


def write_weights(scalars, far, sources, begun=None):
    _, slots, piece, width = sources[0][0][0].shape
    half = slots * piece
    flat = [array for pair in sources for source in pair for array in source]

    def body(s, *refs):
        in_ref, out_ref = refs[-2:]

        def write(target, source, top):
            for slot in range(slots):
                at = pl.multiple_of((s[2] + slots - slot) % slots * piece, piece)
                target[0, pl.ds(at + top, piece), :] = source[0, slot].astype(F32)

        for core in range(2):

            @pl.when(s[0] == core)
            def _():
                for at, top in ((0, core * half), (2, (1 - core) * half)):
                    write(out_ref, refs[4 * core + at], top)
                    write(in_ref, refs[4 * core + at + 1], top)

    def source(core):
        return pl.BlockSpec((1, slots, piece, width), lambda k, s: (jnp.where(s[0] == core, k, 0), 0, 0, 0))

    extra = [] if begun is None else list(begun)
    return pl.pallas_call(
        body,
        grid_spec=pltpu.PrefetchScalarGridSpec(
            num_scalar_prefetch=1,
            grid=(2,),
            in_specs=[source(0)] * 4 + [source(1)] * 4 + [pl.BlockSpec(memory_space=pl.ANY)] * len(extra),
            out_specs=[
                pl.BlockSpec((1, width, width), lambda k, s: (0, 0, (k + 2 * far) ^ s[1])),
                pl.BlockSpec((1, width, width), lambda k, s: (0, (2 * k + far) ^ s[1], 0)),
            ],
        ),
        out_shape=[like(1, width, 4 * width, dtype=F32), like(1, 4 * width, width, dtype=F32)],
        input_output_aliases={9: 0, 10: 1} if extra else {},
        compiler_params=pltpu.CompilerParams(vmem_limit_bytes=40 << 20),
        cost_estimate=pl.CostEstimate(flops=0, bytes_accessed=24 * width * width // COST, transcendentals=0),
        name="write_weights",
    )(scalars, *flat, *extra)


def finish(core, g_h, mixed, unfold):
    rows, width = g_h.shape
    half = width // 2
    tile = min(ROWS, rows)

    def body(g_ref, *refs):
        refs[-1][...] = (g_ref[...] + mixture_tile(*refs[:-1])).astype(BF)

    mine, theirs = mixed
    return call(
        body,
        (rows // tile,),
        [row_block(tile, width), scalar_block()] + mixture_specs(rows, half, tile),
        row_block(tile, width),
        like(rows, width),
        2 * rows * width * width,
        8 * rows * width,
        "finish",
        14,
    )(g_h, core, mine, mine, theirs, theirs, unfold)


def bit_pairs(count, bit):
    return [(i, i ^ (1 << bit)) for i in range(count)]


def added(left, right):
    return (left.astype(F32) + right.astype(F32)).astype(BF)


class Line:
    def __init__(self):
        self.last = None

    def __call__(self, step, *args):
        if self.last is not None:
            args, _ = lax.optimization_barrier((args, self.last))
        out = step(*args)
        self.last = min(jax.tree.leaves(out), key=lambda leaf: leaf.size)
        return out

    def after(self, value):
        return lax.optimization_barrier((value, self.last))[0]


class ChipSum:
    def __init__(self):
        self.count = lax.axis_size("dp")
        self.peers = lax.axis_size("seq")

    def across(self, bit, value):
        return lax.ppermute(value, "dp", bit_pairs(self.count, bit))

    def sent(self, mine, theirs):
        return (lambda a, b: [added(a[stream], b[stream]) for stream in range(2)]), (mine, theirs)

    def start_first(self, sent):
        self.first = [self.across(stream, sent[stream]) for stream in range(2)]

    def first_sums(self, mine, theirs):
        def step(a, b, *got):
            sums = [(a[m].astype(F32) + b[m].astype(F32) + got[m].astype(F32)).astype(BF) for m in range(2)]
            return [(part[1], part[0]) for part in sums]

        return step, (mine, theirs, *self.first)

    def start_second(self, sums):
        self.second = [(sums[stream][1], self.across(1 - stream, sums[stream][0])) for stream in range(2)]

    def second_sums(self):
        def step(z, *pairs):
            sums = [added(*pair) for pair in pairs]
            for bit in range(2, self.count.bit_length() - 1):
                sums = [added(part, self.across(bit, part)) for part in sums]
            both = jnp.stack(sums)
            both = both.reshape(2, self.peers, -1, both.shape[-1])
            return [lax.dynamic_index_in_dim(both, (z + d) % self.peers, 1, keepdims=False) for d in range(self.peers)]

        return step, (lax.axis_index("seq"), *self.second)

    def along(self, value, by):
        return lax.ppermute(value, "seq", [(i, (i + by) % self.peers) for i in range(self.peers)])

    def start_scatter(self, pieces):
        self.kept = pieces[0]
        self.got = [self.along(piece, d) for d, piece in enumerate(pieces) if d]

    def scattered(self):
        def step(kept, *got):
            return sum((g.astype(F32) for g in got), kept.astype(F32)).astype(BF)

        return step, (self.kept, *self.got)

    def start_gather(self, piece):
        self.kept = piece
        self.got = [self.along(piece, d) for d in range(1, self.peers)]

    def gathered(self):
        def step(*pieces):
            return [jnp.stack([piece[at] for piece in pieces]) for at in range(2)]

        return step, (self.kept, *self.got)

    def start_back(self, streams):
        self.own = streams
        self.near = [self.across(1 - stream, streams[stream]) for stream in range(2)]

    def paired(self):
        def step(a, b, c, d):
            return jnp.stack([a, b]), jnp.stack([c, d])

        return step, (self.own[0], self.near[0], self.own[1], self.near[1])

    def start_last(self, pairs):
        self.pairs = pairs
        self.far = [self.across(stream, pairs[stream]) for stream in range(2)]

def small_hops():
    hops = []
    for axis in ("pipe", "seq", "dp"):
        count = lax.axis_size(axis)
        hops += [(axis, bit_pairs(count, bit)) for bit in range(count.bit_length() - 1)]
    return hops


def on_device(
    inputs,
    cotangent,
    in_weight,
    in_bias,
    out_weight,
    out_bias,
    mix_gain,
    mix_shift,
    out_gain,
    out_shift,
):
    rows, width = inputs.shape[1:]
    hidden = in_weight.shape[2]
    peers = lax.axis_size("seq")
    blocks = peers // 2
    half = width // 2
    core = lax.axis_index("pipe")
    z = lax.axis_index("seq")
    first = core == 0
    low = z < blocks
    local = low == first
    block = jnp.minimum(z, peers - 1 - z)
    which = core.astype(jnp.int32).reshape(1)

    def place(member, is_low):
        return member if is_low else peers - 1 - member

    group_shifts = [
        [(place(b, side), place((b + d) % blocks, side)) for side in (True, False) for b in range(blocks)]
        for d in range(1, blocks)
    ]
    in_pairs = []
    out_pairs = []
    for i in range(peers):
        facing = peers - 1 - i
        source = peers + i if i < blocks else i
        in_pairs.append((source, facing if i < blocks else peers + facing))
        out_pairs.append((source, peers + facing if source < peers else facing))

    row_ids = lax.broadcasted_iota(jnp.int32, (rows, rows), 0)
    col_ids = lax.broadcasted_iota(jnp.int32, (rows, rows), 1)
    order = (col_ids == jnp.where(first, row_ids, (rows - row_ids) % rows)).astype(BF)

    def picked(items):
        return jnp.where(low, items[1], items[0]), jnp.where(low, items[0], items[1])

    def arranged(kept, moved):
        return product(order, jnp.where(local, kept, moved)).astype(BF)

    turned = z >= blocks
    back_order = (col_ids == jnp.where(turned, (rows - row_ids) % rows, row_ids)).astype(BF)

    def give_start(value):
        return value, lax.ppermute(value, ("pipe", "seq"), out_pairs)

    def give_pick(value, moved):
        return jnp.where(local, value, moved)

    def give_cut(block):
        return jnp.where(first, block[:, :half], block[:, half:]), jnp.where(first, block[:, half:], block[:, :half])

    def give_end(mine, beside):
        near = jnp.where(local, mine, beside)
        far = jnp.where(local, beside, mine)
        return jnp.stack(
            [product(back_order, part).astype(BF) for part in (jnp.where(low, near, far), jnp.where(low, far, near))]
        )

    sent, x = picked(inputs)
    x = arranged(x, lax.ppermute(sent, ("pipe", "seq"), in_pairs))
    vectors = jnp.concatenate([in_bias[0], out_bias[0], mix_gain[0], mix_shift[0], out_gain[0], out_shift[0]])
    other_vectors = swap_cores(vectors)
    vectors = jnp.where(first, jnp.stack([vectors, other_vectors]), jnp.stack([other_vectors, vectors]))
    b1 = vectors[:, :hidden].reshape(2, 1, hidden)
    vec = vectors[:, hidden:].reshape(2, 5, width)
    w1 = lax.all_gather(in_weight, "pipe", axis=0, tiled=True)
    w2 = lax.all_gather(out_weight, "pipe", axis=0, tiled=True)
    spread, unfold = feature_tables(width, core)
    cos, sin = token_tables(block, rows, blocks, rows * peers)
    factor = 1.0 / math.sqrt(rows * peers)

    line = Line()

    def fold(own, came):
        return line(lambda a, b: fold_spectra(which, a, b), own, came)

    def spread_out(folded):
        return [lax.ppermute(folded, "seq", pairs) for pairs in group_shifts]

    def part(folded):
        return line(lambda f: transform_part(cos, sin, 0, f), folded)

    def rest(begun, parts):
        return line(lambda a, *b: transform_rest(which, cos, sin, a, list(b), factor), begun, *parts)

    kept = []
    own, other = line(lambda v: spectra_call(which, v, spread), x)
    cot_sent, cot_kept = line.after(picked(cotangent))
    for layer in range(2):
        folded = fold(own, swap_cores(other))
        parts = spread_out(folded)
        begun = part(folded)
        if layer == 1:
            grad = line(arranged, cot_kept, cot_moved)
        mixed = rest(begun, parts)
        came = swap_cores(mixed)
        if layer == 0:
            cot_moved = lax.ppermute(line.after(cot_sent), ("pipe", "seq"), in_pairs)
        x, *saved = line(
            lambda v, m, l=layer: forward(which, l, v, m, unfold, w1, w2, b1, vec, spread, l == 0), x, (mixed, came)
        )
        kept.append(saved[:7])
        if layer == 0:
            own, other = saved[7:]

    index = lax.axis_index("dp") & 3
    scalars = jnp.stack([core, index]).astype(jnp.int32)

    def back(layer, grad, mixed):
        return line(
            lambda g, m, k: backward(scalars, layer, g, m, unfold, k, w1, w2, vec, spread), grad, mixed, kept[layer]
        )

    def run(work):
        return line(work[0], *work[1])

    def flat_small(wide, narrow):
        return jnp.concatenate([wide.reshape(-1), narrow[:5].reshape(-1)])

    late, early = ChipSum(), ChipSum()

    out_moved = give_start(x)
    grad, gb, gp, own, other, wide1, narrow1 = line(
        lambda g, k: backward_last(1, g, k, w1, w2, vec, spread), grad, kept[1]
    )

    came = swap_cores(other)
    folded = fold(own, came)

    parts = spread_out(line.after(folded))
    my_sent, my_kept1, other_sent, other_kept = line(grad_blocks, scalars, kept[1][0], gp, kept[1][1], gb)
    begun = part(folded)
    mixed = rest(begun, parts)

    came = swap_cores(mixed)
    got_sent = swap_cores(line.after(other_sent))
    add_sent, parts = early.sent(my_sent, got_sent)
    sent = line(lambda a, b, _: add_sent(a, b), *parts, came)
    got_kept1 = swap_cores(line.after(other_kept))

    early.start_first(line.after(sent))
    grad, own, other, wide0, narrow0, my_sent, my_kept, other_sent, other_kept = back(0, grad, (mixed, came))

    sums = run(early.first_sums(my_kept1, got_kept1))
    out_block = line(give_pick, *out_moved)

    got_sent = swap_cores(line.after(other_sent))
    came = swap_cores(line.after(other))
    early.start_second(line.after(sums))
    hops = iter(small_hops())
    small = line.after(jnp.stack([flat_small(wide0, narrow0), flat_small(wide1, narrow1)]))

    def start_hop():
        axis, pairs = next(hops)
        return lax.ppermute(line.after(small), axis, pairs)

    def end_hop(got):
        return line(lambda a, b: a + b, small, got)

    hop = start_hop()
    folded = fold(own, came)
    sent = run(late.sent(my_sent, got_sent))
    pieces = run(early.second_sums())
    small = end_hop(hop)

    late.start_first(line.after(sent))
    early.start_scatter(line.after(pieces))
    got_kept0 = swap_cores(line.after(other_kept))
    hop = start_hop()
    begun = part(folded)
    out_mine, out_theirs = line(give_cut, out_block)
    piece = run(early.scattered())
    small = end_hop(hop)
    sums = run(late.first_sums(my_kept, got_kept0))

    late.start_second(line.after(sums))
    early.start_gather(line.after(piece))
    out_beside = swap_cores(line.after(out_theirs))
    pieces = run(late.second_sums())
    streams = run(early.gathered())

    late.start_scatter(line.after(pieces))
    early.start_back(line.after(streams))
    hop = start_hop()
    out = line(give_end, out_mine, out_beside)
    pairs = run(early.paired())

    early.start_last(line.after(pairs))
    piece = run(late.scattered())
    small = end_hop(hop)

    late.start_gather(line.after(piece))
    pairs_far1 = lax.ppermute(line.after(pairs), "pipe", [(0, 1)])
    streams = run(late.gathered())
    far1 = line.after(early.far)

    streams, far1 = lax.optimization_barrier((streams, far1))
    late.start_back(streams)
    parts = spread_out(line.after(folded))
    far1_far = lax.ppermute(line.after(far1), "pipe", [(0, 1)])
    pairs0 = run(late.paired())

    late.start_last(line.after(pairs0))
    pairs_far0 = lax.ppermute(line.after(pairs0), "pipe", [(1, 0)])
    mixed = rest(begun, parts)
    came = swap_cores(mixed)
    in_ready = line(lambda g, m: finish(which, g, m, unfold), grad, (mixed, came))
    in_moved = give_start(in_ready)
    scalars = jnp.stack([core, index, z]).astype(jnp.int32)
    begun = line(lambda *v: write_weights(scalars, 0, v), (pairs0, pairs_far0), (pairs, pairs_far1))
    far0 = line.after(late.far)

    far0_far = lax.ppermute(far0, "pipe", [(1, 0)])
    hop = start_hop()
    g_w1, g_w2 = line(lambda b, *v: write_weights(scalars, 1, v, b), begun, (far0, far0_far), (far1, far1_far))
    small = end_hop(hop)
    hop = start_hop()
    in_mine, in_theirs = line(lambda *v: give_cut(give_pick(*v)), *in_moved)
    in_beside = swap_cores(line.after(in_theirs))
    small = end_hop(hop)
    in_grad = line(give_end, in_mine, in_beside)
    for axis, hop in hops:
        small = line(lambda a, b: a + b, small, lax.ppermute(small, axis, hop))
    small = jnp.where(first, small[0], small[1])
    g_b1 = small[:hidden]
    g_b2, g_mg, g_ms, g_og, g_os = (small[hidden + i * width : hidden + (i + 1) * width] for i in range(5))
    return (
        out,
        in_grad,
        g_w1,
        g_b1[None],
        g_w2,
        g_b2[None],
        g_mg[None],
        g_ms[None],
        g_og[None],
        g_os[None],
    )


def solution(mesh):
    return jax.shard_map(
        on_device,
        mesh=mesh,
        in_specs=(
            P("dp", "seq", None),
            P("dp", "seq", None),
            P("pipe", None, None),
            P("pipe", None),
            P("pipe", None, None),
            P("pipe", None),
            P("pipe", None),
            P("pipe", None),
            P("pipe", None),
            P("pipe", None),
        ),
        out_specs=(
            P("dp", "seq", "pipe"),
            P("dp", "seq", "pipe"),
            P("pipe", None, None),
            P("pipe", None),
            P("pipe", None, None),
            P("pipe", None),
            P("pipe", None),
            P("pipe", None),
            P("pipe", None),
            P("pipe", None),
        ),
        check_vma=False,
    )
```

```python
import math

import jax
import jax.numpy as jnp
from jax import lax
from jax.experimental import pallas as pl
from jax.experimental.pallas import tpu as pltpu
from jax.sharding import PartitionSpec as P

BF = jnp.bfloat16
F32 = jnp.float32
PAD = 16
ROWS = 256
CHUNK = 768
COST = 64


def product(left, right):
    return jnp.dot(left, right, preferred_element_type=F32)


def contract(left, right, left_dim, right_dim):
    dims = (((left_dim,), (right_dim,)), ((), ()))
    return lax.dot_general(left, right, dims, preferred_element_type=F32)


def swap_cores(value):
    return lax.ppermute(value, "pipe", [(0, 1), (1, 0)])


def turn(phase, length):
    angles = (phase % length).astype(F32) * (2.0 * math.pi / length)
    return jnp.cos(angles), jnp.sin(angles)


def column_sets(width):
    quarter, half = width // 4, width // 2
    return (
        (list(range(quarter)) + [half], list(range(1, quarter))),
        (list(range(quarter, half)), list(range(quarter, half))),
    )


def feature_tables(width, core):
    sets = column_sets(width)
    order = []
    for cos_ids, sin_ids in sets:
        order.append(([k for k in cos_ids] + [k for k in sin_ids], [0] * len(cos_ids) + [1] * len(sin_ids)))
    ids_a = jnp.array(order[0][0] + order[1][0], jnp.int32)
    ids_b = jnp.array(order[1][0] + order[0][0], jnp.int32)
    odd_a = jnp.array(order[0][1] + order[1][1], jnp.int32)
    odd_b = jnp.array(order[1][1] + order[0][1], jnp.int32)
    first = core == 0
    ids = jnp.where(first, ids_a, ids_b)
    odd = jnp.where(first, odd_a, odd_b)
    sign = jnp.where(first, 1.0, -1.0)
    rows = jnp.arange(width, dtype=jnp.int32)
    cos, sin = turn(rows[:, None] * ids[None, :], width)
    spread = jnp.where(odd[None, :] == 1, -sign * sin, cos).astype(BF)
    direct = rows[None, :] == ids[:, None]
    mirror = rows[None, :] == ((width - ids) % width)[:, None]
    even_rows = (direct | mirror).astype(F32)
    odd_rows = sign * (direct.astype(F32) - mirror.astype(F32))
    unfold = jnp.where(odd[:, None] == 1, odd_rows, even_rows).astype(BF)
    return spread, unfold


def token_tables(block, rows, blocks, length):
    tall = rows + PAD
    inner = jnp.arange(tall, dtype=jnp.int32)
    slots = jnp.arange(blocks, dtype=jnp.int32)
    columns = ((block + blocks - slots) % blocks * rows)[:, None, None] + inner
    coarse = block * rows + PAD * jnp.arange(tall // PAD, dtype=jnp.int32)
    fine = jnp.arange(PAD, dtype=jnp.int32)
    cos_c, sin_c = turn(coarse[:, None] * columns, length)
    cos_f, sin_f = turn(fine[:, None] * columns, length)
    cos_c, sin_c, cos_f, sin_f = cos_c[:, :, None], sin_c[:, :, None], cos_f[:, None], sin_f[:, None]
    cos = (cos_c * cos_f - sin_c * sin_f).astype(BF)
    sin = (sin_c * cos_f + cos_c * sin_f).astype(BF)
    return cos.reshape(blocks, tall, tall), sin.reshape(blocks, tall, tall)


def row_block(height, width):
    return pl.BlockSpec((height, width), lambda i: (i, 0))


def whole(*shape):
    return pl.BlockSpec(shape, lambda *_: (0,) * len(shape), pipeline_mode=pl.Buffered(1))


def scalar_block():
    return pl.BlockSpec(memory_space=pltpu.SMEM)


def layer_block(layer, *shape):
    return pl.BlockSpec((1, *shape), lambda i: (layer,) + (0,) * len(shape), pipeline_mode=pl.Buffered(1))


def call(body, grid, in_specs, out_specs, out_shape, flops, moved, name, vmem, scratch=()):
    return pl.pallas_call(
        body,
        grid=grid,
        in_specs=in_specs,
        out_specs=out_specs,
        out_shape=out_shape,
        scratch_shapes=scratch,
        compiler_params=pltpu.CompilerParams(vmem_limit_bytes=vmem << 20),
        cost_estimate=pl.CostEstimate(flops=flops // COST, bytes_accessed=moved // COST, transcendentals=0),
        name=name,
    )


def like(*shape, dtype=BF):
    return jax.ShapeDtypeStruct(shape, dtype)


def divisor(count, most):
    return max(d for d in range(1, most + 1) if count % d == 0)


def fold_spectra(core, own, recv):
    rows, half = own.shape

    def body(core_ref, own_ref, recv_ref, out_ref):
        first = core_ref[0] == 0
        out_ref[:rows] = (own_ref[...].astype(F32) + recv_ref[...].astype(F32)).astype(BF)
        mine, theirs = own_ref[:PAD], recv_ref[:PAD]
        at = lax.broadcasted_iota(jnp.int32, (PAD, half), 0)
        low = jnp.where(first, mine, theirs)
        high = jnp.where(first, theirs, mine)
        out_ref[:PAD] = jnp.where(at == 0, low, out_ref[:PAD])
        out_ref[rows:] = jnp.where(at == 0, high, jnp.zeros_like(high))

    spec = pl.BlockSpec((rows, half), lambda i: (0, 0))
    return call(
        body,
        (1,),
        [scalar_block(), spec, spec],
        pl.BlockSpec((rows + PAD, half), lambda i: (0, 0)),
        like(rows + PAD, half),
        rows * half,
        6 * rows * half,
        "fold_spectra",
        8,
    )(core, own, recv)


def transform_part(cos, sin, slot, part):
    tall, half = part.shape
    wide = -(-(half // 2 + 1) // 128) * 128
    tile = divisor(tall // PAD, 17) * PAD

    def body(cos_ref, sin_ref, part_ref, out_ref):
        out_ref[:, :wide] = product(cos_ref[0], part_ref[:, :wide])
        out_ref[:, wide:] = product(sin_ref[0], part_ref[:, half - wide :])

    table = pl.BlockSpec((1, tile, tall), lambda i: (slot, i, 0))
    return call(
        body,
        (tall // tile,),
        [table, table, whole(tall, half)],
        row_block(tile, 2 * wide),
        like(tall, 2 * wide, dtype=F32),
        4 * tall * tall * wide,
        4 * tall * (tall + 2 * wide),
        "transform_part",
        12,
    )(cos, sin, part)


def transform_rest(core, cos, sin, begun, parts, factor):
    tall, half = parts[0].shape
    wide = begun.shape[1] // 2
    tile = divisor(tall // PAD, 17) * PAD
    lead = half - wide

    def body(*refs):
        core_ref, begun_ref = refs[:2]
        tables = refs[2 : 2 + 2 * len(parts)]
        part_refs = refs[2 + 2 * len(parts) : -1]
        out_ref = refs[-1]
        even, odd = begun_ref[:, :wide], begun_ref[:, wide:]
        for at, part_ref in enumerate(part_refs):
            even = even + product(tables[2 * at][0], part_ref[:, :wide])
            odd = odd + product(tables[2 * at + 1][0], part_ref[:, lead:])
        lanes = lax.broadcasted_iota(jnp.int32, (tile, wide - lead), 1) + lead
        cos_count = half // 2 + 1 - core_ref[0]
        middle = jnp.where(lanes < cos_count, even[:, lead:], odd[:, : wide - lead])
        out_ref[:, :lead] = (even[:, :lead] * factor).astype(BF)
        out_ref[:, lead:wide] = (middle * factor).astype(BF)
        out_ref[:, wide:] = (odd[:, wide - lead :] * factor).astype(BF)

    tables, specs = [], []
    for at in range(len(parts)):
        spec = pl.BlockSpec((1, tile, tall), lambda i, at=at: (at + 1, i, 0))
        tables += [cos, sin]
        specs += [spec, spec]
    return call(
        body,
        (tall // tile,),
        [scalar_block(), row_block(tile, 2 * wide)] + specs + [whole(tall, half)] * len(parts),
        row_block(tile, half),
        like(tall, half),
        4 * tall * tall * wide * len(parts),
        4 * tall * (tall * len(parts) + 2 * wide),
        "transform_rest",
        14,
    )(core, begun, *tables, *parts)


def transform(core, own, recv, cos, sin, group_shifts, factor, beside=None):
    folded = fold_spectra(core, own, recv)
    parts = [lax.ppermute(folded, "seq", pairs) for pairs in group_shifts]
    begun = transform_part(cos, sin, 0, folded)
    mixed = transform_rest(core, cos, sin, begun, parts, factor)
    return mixed, swap_cores(mixed)


def standardize(hidden):
    centered = hidden - jnp.mean(hidden, axis=-1, keepdims=True)
    spread = jnp.mean(centered * centered, axis=-1, keepdims=True)
    scale = lax.rsqrt(spread + 1e-05)
    return centered * scale, scale


def standardize_back(grad, unit, scale):
    mean_grad = jnp.mean(grad, axis=-1, keepdims=True)
    mean_both = jnp.mean(grad * unit, axis=-1, keepdims=True)
    return (grad - mean_grad - unit * mean_both) * scale


def mixture_tile(core_ref, mine_ref, mine_top, theirs_ref, theirs_top, unfold_ref):
    tile, half = mine_ref.shape
    at = lax.broadcasted_iota(jnp.int32, (tile, half), 0)
    odd_row = (at == 0) & (core_ref[0] == 1) & (pl.program_id(0) == 0)
    mine = jnp.where(odd_row, mine_top[:1], mine_ref[...])
    theirs = jnp.where(odd_row, theirs_top[:1], theirs_ref[...])
    return product(mine, unfold_ref[:half]) + product(theirs, unfold_ref[half:])


def mixture_specs(rows, half, tile):
    block = row_block(tile, half)
    top = pl.BlockSpec((PAD, half), lambda i: (rows // PAD, 0))
    return [block, top, block, top, whole(2 * half, 2 * half)]


def spectra_call(core, x, spread):
    rows, width = x.shape
    half = width // 2
    tile = min(ROWS, rows)
    factor = 1.0 / math.sqrt(width)

    def body(x_ref, spread_ref, own_ref, other_ref):
        spectra = product(x_ref[...], spread_ref[...]) * factor
        own_ref[...] = spectra[:, :half].astype(BF)
        other_ref[...] = spectra[:, half:].astype(BF)

    return call(
        body,
        (rows // tile,),
        [row_block(tile, width), whole(width, width)],
        [row_block(tile, half)] * 2,
        [like(rows, half)] * 2,
        2 * rows * width * width,
        4 * rows * width,
        "spectra",
        12,
    )(x, spread)


def forward(core, layer, x, mixed, unfold, w1, w2, b1, vec, spread, ahead):
    rows, width = x.shape
    hidden = w1.shape[2]
    half = width // 2
    tile = min(2 * ROWS, rows)
    sub = min(ROWS, tile)
    chunk = min(CHUNK, hidden)
    factor = 1.0 / math.sqrt(width)

    def body(core_ref, x_ref, m0, t0, m1, t1, unfold_ref, w1_ref, w2_ref, b1_ref, vec_ref, spread_ref, *outs):
        out_ref, low_ref, act_ref, slope_ref, unit1_ref, scale1_ref, unit2_ref, scale2_ref = outs[:8]
        b2, mg, ms, og, os = (vec_ref[0, i : i + 1] for i in range(5))
        mixture = mixture_tile(core_ref, m0, t0, m1, t1, unfold_ref).astype(BF)
        lows, totals = [], []
        for at in range(0, tile, sub):
            part = slice(at, at + sub)
            unit, scale = standardize(x_ref[part].astype(F32) + mixture[part].astype(F32))
            normed = unit * mg + ms
            unit1_ref[part] = unit.astype(BF)
            scale1_ref[part] = jnp.broadcast_to(scale, (sub, scale1_ref.shape[1]))
            lows.append(normed.astype(BF))
            low_ref[part] = lows[-1]
            totals.append(normed + b2)
        for start in range(0, hidden, chunk):
            span = slice(start, start + chunk)
            for i, at in enumerate(range(0, tile, sub)):
                part = slice(at, at + sub)
                pre = product(lows[i], w1_ref[0, :, span]) + b1_ref[0, :, span]
                cdf = 0.5 + 0.5 * lax.erf(pre * (1.0 / math.sqrt(2.0)))
                act = (pre * cdf).astype(BF)
                act_ref[part, span] = act
                slope = cdf + pre * (jnp.exp(-0.5 * pre * pre) * (1.0 / math.sqrt(2.0 * math.pi)))
                slope_ref[part, span] = slope.astype(BF)
                totals[i] = totals[i] + product(act, w2_ref[0, span, :])
        for i, at in enumerate(range(0, tile, sub)):
            part = slice(at, at + sub)
            unit, scale = standardize(totals[i])
            unit2_ref[part] = unit.astype(BF)
            scale2_ref[part] = jnp.broadcast_to(scale, (sub, scale2_ref.shape[1]))
            out = (unit * og + os).astype(BF)
            out_ref[part] = out
            if ahead:
                own_ref, other_ref = outs[8:]
                spectra = product(out, spread_ref[...]) * factor
                own_ref[part] = spectra[:, :half].astype(BF)
                other_ref[part] = spectra[:, half:].astype(BF)

    mine, theirs = mixed
    return call(
        body,
        (rows // tile,),
        [scalar_block(), row_block(tile, width)]
        + mixture_specs(rows, half, tile)
        + [
            layer_block(layer, width, hidden),
            layer_block(layer, hidden, width),
            layer_block(layer, 1, hidden),
            layer_block(layer, 5, width),
            whole(width, width),
        ],
        [
            row_block(tile, width),
            row_block(tile, width),
            row_block(tile, hidden),
            row_block(tile, hidden),
            row_block(tile, width),
            row_block(tile, 128),
            row_block(tile, width),
            row_block(tile, 128),
        ]
        + [row_block(tile, half)] * (2 if ahead else 0),
        [
            like(rows, width),
            like(rows, width),
            like(rows, hidden),
            like(rows, hidden),
            like(rows, width),
            like(rows, 128, dtype=F32),
            like(rows, width),
            like(rows, 128, dtype=F32),
        ]
        + [like(rows, half)] * (2 if ahead else 0),
        4 * rows * width * (hidden + width),
        4 * width * hidden + 4 * rows * hidden + 14 * rows * width,
        "layer_forward",
        60,
    )(core, x, mine, mine, theirs, theirs, unfold, w1, w2, b1, vec, spread)


def backward(scalars, layer, grad, mixed, unfold, kept, w1, w2, vec, spread):
    low, act, slope, unit1, scale1, unit2, scale2 = kept
    rows, width = grad.shape
    hidden = w1.shape[2]
    half = width // 2
    tile = min(ROWS, rows)
    squares = hidden // width
    factor = 1.0 / math.sqrt(width)
    count = 0 if mixed is None else 5

    def body(scalar_ref, grad_ref, *refs):
        low_ref, act_ref, slope_ref, unit1_ref, scale1_ref, unit2_ref, scale2_ref, w1_ref, w2_ref, vec_ref, spread_ref = refs[
            count : 11 + count
        ]
        gh_ref, own_ref, other_ref, wide_ref, sums_ref, *block_refs = refs[11 + count : -2]
        in_sum, out_sum = refs[-2:]

        @pl.when(pl.program_id(0) == 0)
        def _():
            for ref in (wide_ref, sums_ref, in_sum, out_sum):
                ref[...] = jnp.zeros_like(ref)

        grad = grad_ref[...].astype(F32)
        if count:
            grad = (grad + mixture_tile(scalar_ref, *refs[:count])).astype(BF).astype(F32)
        mg, og = vec_ref[0, 1:2], vec_ref[0, 3:4]
        unit2 = unit2_ref[...].astype(F32)
        g_branch = standardize_back(grad * og, unit2, scale2_ref[:, :1])
        gb = g_branch.astype(BF)
        total = g_branch
        for square in range(squares):
            span = slice(square * width, (square + 1) * width)
            g_act = contract(gb, w2_ref[0, span, :], 1, 1)
            gp = (g_act * slope_ref[:, span].astype(F32)).astype(BF)
            wide_ref[:, span] += jnp.sum(gp.astype(F32), axis=0, keepdims=True)
            total = total + contract(gp, w1_ref[0, :, span], 1, 1)
            out_sum[square] += contract(act_ref[:, span], gb, 0, 0)
            in_sum[square] += contract(low_ref[...], gp, 0, 0)
        unit1 = unit1_ref[...].astype(F32)
        g_h = standardize_back(total * mg, unit1, scale1_ref[:, :1])
        gh_ref[...] = g_h
        for at, terms in enumerate((gb.astype(F32), total * unit1, total, grad * unit2, grad)):
            sums_ref[at : at + 1] += jnp.sum(terms, axis=0, keepdims=True)
        spectra = product(g_h.astype(BF), spread_ref[...]) * factor
        own_ref[...] = spectra[:, :half].astype(BF)
        other_ref[...] = spectra[:, half:].astype(BF)

        @pl.when(pl.program_id(0) == pl.num_programs(0) - 1)
        def _():
            for owner in range(2):
                part = pl.ds(pl.multiple_of((scalar_ref[0] ^ owner) * half, half), half)
                for use in range(2):
                    for at in range(2):
                        ref = block_refs[2 * owner + use]
                        ref[0, at] = out_sum[(2 * at + 1 - use) ^ scalar_ref[1], part, :].astype(BF)
                        ref[1, at] = in_sum[(2 - 2 * use + at) ^ scalar_ref[1], part, :].astype(BF)

    if count:
        mine, theirs = mixed
        extra = [mine, mine, theirs, theirs, unfold]
        extra_specs = mixture_specs(rows, half, tile)
    else:
        extra, extra_specs = [], []
    return call(
        body,
        (rows // tile,),
        [scalar_block(), row_block(tile, width)]
        + extra_specs
        + [
            row_block(tile, width),
            row_block(tile, hidden),
            row_block(tile, hidden),
            row_block(tile, width),
            row_block(tile, 128),
            row_block(tile, width),
            row_block(tile, 128),
            layer_block(layer, width, hidden),
            layer_block(layer, hidden, width),
            layer_block(layer, 5, width),
            whole(width, width),
        ],
        [
            row_block(tile, width),
            row_block(tile, half),
            row_block(tile, half),
            whole(1, hidden),
            whole(8, width),
        ]
        + [whole(2, 2, half, width)] * 4,
        [
            like(rows, width, dtype=F32),
            like(rows, half),
            like(rows, half),
            like(1, hidden, dtype=F32),
            like(8, width, dtype=F32),
        ]
        + [like(2, 2, half, width)] * 4,
        8 * rows * width * (hidden + width),
        4 * width * hidden + 4 * rows * hidden + 14 * rows * width,
        "layer_backward",
        60,
        [pltpu.VMEM((squares, width, width), F32)] * 2,
    )(scalars, grad, *extra, low, act, slope, unit1, scale1, unit2, scale2, w1, w2, vec, spread)


def backward_last(layer, grad, kept, w1, w2, vec, spread):
    low, act, slope, unit1, scale1, unit2, scale2 = kept
    rows, width = grad.shape
    hidden = w1.shape[2]
    half = width // 2
    tile = min(ROWS, rows)
    chunk = min(CHUNK, hidden)
    factor = 1.0 / math.sqrt(width)

    def body(*refs):
        grad_ref = refs[0]
        slope_ref, unit1_ref, scale1_ref, unit2_ref, scale2_ref, w1_ref, w2_ref, vec_ref, spread_ref = refs[1:10]
        gh_ref, gb_ref, gp_ref, own_ref, other_ref, wide_ref, sums_ref = refs[10:]

        @pl.when(pl.program_id(0) == 0)
        def _():
            wide_ref[...] = jnp.zeros_like(wide_ref)
            sums_ref[...] = jnp.zeros_like(sums_ref)

        grad = grad_ref[...].astype(F32)
        mg, og = vec_ref[0, 1:2], vec_ref[0, 3:4]
        unit2 = unit2_ref[...].astype(F32)
        g_branch = standardize_back(grad * og, unit2, scale2_ref[:, :1])
        gb = g_branch.astype(BF)
        gb_ref[...] = gb
        total = g_branch
        for start in range(0, hidden, chunk):
            span = slice(start, start + chunk)
            g_act = contract(gb, w2_ref[0, span, :], 1, 1)
            gp = (g_act * slope_ref[:, span].astype(F32)).astype(BF)
            gp_ref[:, span] = gp
            wide_ref[:, span] += jnp.sum(gp.astype(F32), axis=0, keepdims=True)
            total = total + contract(gp, w1_ref[0, :, span], 1, 1)
        unit1 = unit1_ref[...].astype(F32)
        g_h = standardize_back(total * mg, unit1, scale1_ref[:, :1])
        gh_ref[...] = g_h
        for at, terms in enumerate((gb.astype(F32), total * unit1, total, grad * unit2, grad)):
            sums_ref[at : at + 1] += jnp.sum(terms, axis=0, keepdims=True)
        spectra = product(g_h.astype(BF), spread_ref[...]) * factor
        own_ref[...] = spectra[:, :half].astype(BF)
        other_ref[...] = spectra[:, half:].astype(BF)

    return call(
        body,
        (rows // tile,),
        [
            row_block(tile, width),
            row_block(tile, hidden),
            row_block(tile, width),
            row_block(tile, 128),
            row_block(tile, width),
            row_block(tile, 128),
            layer_block(layer, width, hidden),
            layer_block(layer, hidden, width),
            layer_block(layer, 5, width),
            whole(width, width),
        ],
        [
            row_block(tile, width),
            row_block(tile, width),
            row_block(tile, hidden),
            row_block(tile, half),
            row_block(tile, half),
            whole(1, hidden),
            whole(8, width),
        ],
        [
            like(rows, width, dtype=F32),
            like(rows, width),
            like(rows, hidden),
            like(rows, half),
            like(rows, half),
            like(1, hidden, dtype=F32),
            like(8, width, dtype=F32),
        ],
        4 * rows * width * (hidden + width),
        4 * width * hidden + 4 * rows * hidden + 14 * rows * width,
        "last_backward",
        58,
    )(grad, slope, unit1, scale1, unit2, scale2, w1, w2, vec, spread)


def grad_blocks(scalars, low, gp, act, gb):
    rows, width = low.shape
    half = width // 2

    def body(scalar_ref, act_ref, gb_ref, low_ref, gp_ref, *refs):
        outer = contract(act_ref[...], gb_ref[...], 0, 0).astype(BF)
        inner = contract(low_ref[...], gp_ref[...], 0, 0).astype(BF)

        def write(mine, theirs):
            mine[0, 0], mine[1, 0] = outer[part], inner[part]
            theirs[0, 0], theirs[1, 0] = outer[rest], inner[rest]

        for core in range(2):
            part, rest = slice(core * half, (core + 1) * half), slice((1 - core) * half, (2 - core) * half)

            @pl.when((scalar_ref[0] == core) & (pl.program_id(0) < 2))
            def _():
                write(refs[0], refs[2])

            @pl.when((scalar_ref[0] == core) & (pl.program_id(0) >= 2))
            def _():
                write(refs[1], refs[3])

    def out_square(i, s):
        return ((2 * i + 1 - i // 2) % 4) ^ s[1]

    def in_square(i, s):
        return ((i + 2) % 4) ^ s[1]

    sent = pl.BlockSpec((2, 1, half, width), lambda i, s: (0, jnp.minimum(i, 1), 0, 0))
    held = pl.BlockSpec((2, 1, half, width), lambda i, s: (0, jnp.maximum(i - 2, 0), 0, 0))
    return pl.pallas_call(
        body,
        grid_spec=pltpu.PrefetchScalarGridSpec(
            num_scalar_prefetch=1,
            grid=(4,),
            in_specs=[
                pl.BlockSpec((rows, width), lambda i, s: (0, out_square(i, s))),
                pl.BlockSpec((rows, width), lambda i, s: (0, 0)),
                pl.BlockSpec((rows, width), lambda i, s: (0, 0)),
                pl.BlockSpec((rows, width), lambda i, s: (0, in_square(i, s))),
            ],
            out_specs=[sent, held, sent, held],
        ),
        out_shape=[like(2, 2, half, width)] * 4,
        compiler_params=pltpu.CompilerParams(vmem_limit_bytes=58 << 20),
        cost_estimate=pl.CostEstimate(flops=16 * rows * width * width // COST, bytes_accessed=20 * rows * width // COST, transcendentals=0),
        name="grad_blocks",
    )(scalars, act, gb, low, gp)


def write_weights(scalars, far, sources, begun=None):
    _, slots, piece, width = sources[0][0][0].shape
    half = slots * piece
    flat = [array for pair in sources for source in pair for array in source]

    def body(s, *refs):
        in_ref, out_ref = refs[-2:]

        def write(target, source, top):
            for slot in range(slots):
                at = pl.multiple_of((s[2] + slots - slot) % slots * piece, piece)
                target[0, pl.ds(at + top, piece), :] = source[0, slot].astype(F32)

        for core in range(2):

            @pl.when(s[0] == core)
            def _():
                for at, top in ((0, core * half), (2, (1 - core) * half)):
                    write(out_ref, refs[4 * core + at], top)
                    write(in_ref, refs[4 * core + at + 1], top)

    def source(core):
        return pl.BlockSpec((1, slots, piece, width), lambda k, s: (jnp.where(s[0] == core, k, 0), 0, 0, 0))

    extra = [] if begun is None else list(begun)
    return pl.pallas_call(
        body,
        grid_spec=pltpu.PrefetchScalarGridSpec(
            num_scalar_prefetch=1,
            grid=(2,),
            in_specs=[source(0)] * 4 + [source(1)] * 4 + [pl.BlockSpec(memory_space=pl.ANY)] * len(extra),
            out_specs=[
                pl.BlockSpec((1, width, width), lambda k, s: (0, 0, (k + 2 * far) ^ s[1])),
                pl.BlockSpec((1, width, width), lambda k, s: (0, (2 * k + far) ^ s[1], 0)),
            ],
        ),
        out_shape=[like(1, width, 4 * width, dtype=F32), like(1, 4 * width, width, dtype=F32)],
        input_output_aliases={9: 0, 10: 1} if extra else {},
        compiler_params=pltpu.CompilerParams(vmem_limit_bytes=40 << 20),
        cost_estimate=pl.CostEstimate(flops=0, bytes_accessed=24 * width * width // COST, transcendentals=0),
        name="write_weights",
    )(scalars, *flat, *extra)


def finish(core, g_h, mixed, unfold):
    rows, width = g_h.shape
    half = width // 2
    tile = min(ROWS, rows)

    def body(g_ref, *refs):
        refs[-1][...] = (g_ref[...] + mixture_tile(*refs[:-1])).astype(BF)

    mine, theirs = mixed
    return call(
        body,
        (rows // tile,),
        [row_block(tile, width), scalar_block()] + mixture_specs(rows, half, tile),
        row_block(tile, width),
        like(rows, width),
        2 * rows * width * width,
        8 * rows * width,
        "finish",
        14,
    )(g_h, core, mine, mine, theirs, theirs, unfold)


def bit_pairs(count, bit):
    return [(i, i ^ (1 << bit)) for i in range(count)]


def added(left, right):
    return (left.astype(F32) + right.astype(F32)).astype(BF)


class Line:
    def __init__(self):
        self.last = None

    def __call__(self, step, *args):
        if self.last is not None:
            args, _ = lax.optimization_barrier((args, self.last))
        out = step(*args)
        self.last = min(jax.tree.leaves(out), key=lambda leaf: leaf.size)
        return out

    def after(self, value):
        return lax.optimization_barrier((value, self.last))[0]


class ChipSum:
    def __init__(self):
        self.count = lax.axis_size("dp")
        self.peers = lax.axis_size("seq")

    def across(self, bit, value):
        return lax.ppermute(value, "dp", bit_pairs(self.count, bit))

    def sent(self, mine, theirs):
        return (lambda a, b: [added(a[stream], b[stream]) for stream in range(2)]), (mine, theirs)

    def start_first(self, sent):
        self.first = [self.across(stream, sent[stream]) for stream in range(2)]

    def first_sums(self, mine, theirs):
        def step(a, b, *got):
            sums = [(a[m].astype(F32) + b[m].astype(F32) + got[m].astype(F32)).astype(BF) for m in range(2)]
            return [(part[1], part[0]) for part in sums]

        return step, (mine, theirs, *self.first)

    def start_second(self, sums):
        self.second = [(sums[stream][1], self.across(1 - stream, sums[stream][0])) for stream in range(2)]

    def second_sums(self):
        def step(z, *pairs):
            sums = [added(*pair) for pair in pairs]
            for bit in range(2, self.count.bit_length() - 1):
                sums = [added(part, self.across(bit, part)) for part in sums]
            both = jnp.stack(sums)
            both = both.reshape(2, self.peers, -1, both.shape[-1])
            return [lax.dynamic_index_in_dim(both, (z + d) % self.peers, 1, keepdims=False) for d in range(self.peers)]

        return step, (lax.axis_index("seq"), *self.second)

    def along(self, value, by):
        return lax.ppermute(value, "seq", [(i, (i + by) % self.peers) for i in range(self.peers)])

    def start_scatter(self, pieces):
        self.kept = pieces[0]
        self.got = [self.along(piece, d) for d, piece in enumerate(pieces) if d]

    def scattered(self):
        def step(kept, *got):
            return sum((g.astype(F32) for g in got), kept.astype(F32)).astype(BF)

        return step, (self.kept, *self.got)

    def start_gather(self, piece):
        self.kept = piece
        self.got = [self.along(piece, d) for d in range(1, self.peers)]

    def gathered(self):
        def step(*pieces):
            return [jnp.stack([piece[at] for piece in pieces]) for at in range(2)]

        return step, (self.kept, *self.got)

    def start_back(self, streams):
        self.own = streams
        self.near = [self.across(1 - stream, streams[stream]) for stream in range(2)]

    def paired(self):
        def step(a, b, c, d):
            return jnp.stack([a, b]), jnp.stack([c, d])

        return step, (self.own[0], self.near[0], self.own[1], self.near[1])

    def start_last(self, pairs):
        self.pairs = pairs
        self.far = [self.across(stream, pairs[stream]) for stream in range(2)]

def small_hops():
    hops = []
    for axis in ("pipe", "seq", "dp"):
        count = lax.axis_size(axis)
        hops += [(axis, bit_pairs(count, bit)) for bit in range(count.bit_length() - 1)]
    return hops


def on_device(
    inputs,
    cotangent,
    in_weight,
    in_bias,
    out_weight,
    out_bias,
    mix_gain,
    mix_shift,
    out_gain,
    out_shift,
):
    rows, width = inputs.shape[1:]
    hidden = in_weight.shape[2]
    peers = lax.axis_size("seq")
    blocks = peers // 2
    half = width // 2
    core = lax.axis_index("pipe")
    z = lax.axis_index("seq")
    first = core == 0
    low = z < blocks
    local = low == first
    block = jnp.minimum(z, peers - 1 - z)
    which = core.astype(jnp.int32).reshape(1)

    def place(member, is_low):
        return member if is_low else peers - 1 - member

    group_shifts = [
        [(place(b, side), place((b + d) % blocks, side)) for side in (True, False) for b in range(blocks)]
        for d in range(1, blocks)
    ]
    in_pairs = []
    out_pairs = []
    for i in range(peers):
        facing = peers - 1 - i
        source = peers + i if i < blocks else i
        in_pairs.append((source, facing if i < blocks else peers + facing))
        out_pairs.append((source, peers + facing if source < peers else facing))

    row_ids = lax.broadcasted_iota(jnp.int32, (rows, rows), 0)
    col_ids = lax.broadcasted_iota(jnp.int32, (rows, rows), 1)
    order = (col_ids == jnp.where(first, row_ids, (rows - row_ids) % rows)).astype(BF)

    def picked(items):
        return jnp.where(low, items[1], items[0]), jnp.where(low, items[0], items[1])

    def arranged(kept, moved):
        return product(order, jnp.where(local, kept, moved)).astype(BF)

    turned = z >= blocks
    back_order = (col_ids == jnp.where(turned, (rows - row_ids) % rows, row_ids)).astype(BF)

    def give_start(value):
        return value, lax.ppermute(value, ("pipe", "seq"), out_pairs)

    def give_pick(value, moved):
        return jnp.where(local, value, moved)

    def give_cut(block):
        return jnp.where(first, block[:, :half], block[:, half:]), jnp.where(first, block[:, half:], block[:, :half])

    def give_end(mine, beside):
        near = jnp.where(local, mine, beside)
        far = jnp.where(local, beside, mine)
        return jnp.stack(
            [product(back_order, part).astype(BF) for part in (jnp.where(low, near, far), jnp.where(low, far, near))]
        )

    sent, x = picked(inputs)
    x = arranged(x, lax.ppermute(sent, ("pipe", "seq"), in_pairs))
    vectors = jnp.concatenate([in_bias[0], out_bias[0], mix_gain[0], mix_shift[0], out_gain[0], out_shift[0]])
    other_vectors = swap_cores(vectors)
    vectors = jnp.where(first, jnp.stack([vectors, other_vectors]), jnp.stack([other_vectors, vectors]))
    b1 = vectors[:, :hidden].reshape(2, 1, hidden)
    vec = vectors[:, hidden:].reshape(2, 5, width)
    w1 = lax.all_gather(in_weight, "pipe", axis=0, tiled=True)
    w2 = lax.all_gather(out_weight, "pipe", axis=0, tiled=True)
    spread, unfold = feature_tables(width, core)
    cos, sin = token_tables(block, rows, blocks, rows * peers)
    factor = 1.0 / math.sqrt(rows * peers)

    line = Line()

    def fold(own, came):
        return line(lambda a, b: fold_spectra(which, a, b), own, came)

    def spread_out(folded):
        return [lax.ppermute(folded, "seq", pairs) for pairs in group_shifts]

    def part(folded):
        return line(lambda f: transform_part(cos, sin, 0, f), folded)

    def rest(begun, parts):
        return line(lambda a, *b: transform_rest(which, cos, sin, a, list(b), factor), begun, *parts)

    kept = []
    own, other = line(lambda v: spectra_call(which, v, spread), x)
    cot_sent, cot_kept = line.after(picked(cotangent))
    for layer in range(2):
        folded = fold(own, swap_cores(other))
        parts = spread_out(folded)
        begun = part(folded)
        if layer == 1:
            grad = line(arranged, cot_kept, cot_moved)
        mixed = rest(begun, parts)
        came = swap_cores(mixed)
        if layer == 0:
            cot_moved = lax.ppermute(line.after(cot_sent), ("pipe", "seq"), in_pairs)
        x, *saved = line(
            lambda v, m, l=layer: forward(which, l, v, m, unfold, w1, w2, b1, vec, spread, l == 0), x, (mixed, came)
        )
        kept.append(saved[:7])
        if layer == 0:
            own, other = saved[7:]

    index = lax.axis_index("dp") & 3
    scalars = jnp.stack([core, index]).astype(jnp.int32)

    def back(layer, grad, mixed):
        return line(
            lambda g, m, k: backward(scalars, layer, g, m, unfold, k, w1, w2, vec, spread), grad, mixed, kept[layer]
        )

    def run(work):
        return line(work[0], *work[1])

    def flat_small(wide, narrow):
        return jnp.concatenate([wide.reshape(-1), narrow[:5].reshape(-1)])

    late, early = ChipSum(), ChipSum()

    out_moved = give_start(x)
    grad, gb, gp, own, other, wide1, narrow1 = line(
        lambda g, k: backward_last(1, g, k, w1, w2, vec, spread), grad, kept[1]
    )

    came = swap_cores(other)
    folded = fold(own, came)

    parts = spread_out(line.after(folded))
    my_sent, my_kept1, other_sent, other_kept = line(grad_blocks, scalars, kept[1][0], gp, kept[1][1], gb)
    begun = part(folded)
    mixed = rest(begun, parts)

    came = swap_cores(mixed)
    got_sent = swap_cores(line.after(other_sent))
    add_sent, parts = early.sent(my_sent, got_sent)
    sent = line(lambda a, b, _: add_sent(a, b), *parts, came)
    got_kept1 = swap_cores(line.after(other_kept))

    early.start_first(line.after(sent))
    grad, own, other, wide0, narrow0, my_sent, my_kept, other_sent, other_kept = back(0, grad, (mixed, came))

    add_first, terms = early.first_sums(my_kept1, got_kept1)
    sums = line(lambda _, *v: add_first(*v), out_moved[1], *terms)

    got_sent = swap_cores(line.after(other_sent))
    came = swap_cores(line.after(other))
    early.start_second(line.after(sums))
    hops = iter(small_hops())
    small = line.after(jnp.stack([flat_small(wide0, narrow0), flat_small(wide1, narrow1)]))

    def start_hop():
        axis, pairs = next(hops)
        return lax.ppermute(line.after(small), axis, pairs)

    def end_hop(got):
        return line(lambda a, b: a + b, small, got)

    hop = start_hop()
    folded = fold(own, came)
    sent = run(late.sent(my_sent, got_sent))
    pieces = run(early.second_sums())
    small = end_hop(hop)

    late.start_first(line.after(sent))
    early.start_scatter(line.after(pieces))
    got_kept0 = swap_cores(line.after(other_kept))
    hop = start_hop()
    begun = part(folded)
    out_mine, out_theirs = line(lambda *v: give_cut(give_pick(*v)), *out_moved)
    piece = run(early.scattered())
    small = end_hop(hop)
    sums = run(late.first_sums(my_kept, got_kept0))

    late.start_second(line.after(sums))
    early.start_gather(line.after(piece))
    out_beside = swap_cores(line.after(out_theirs))
    pieces = run(late.second_sums())
    streams = run(early.gathered())

    late.start_scatter(line.after(pieces))
    early.start_back(line.after(streams))
    hop = start_hop()
    out = line(give_end, out_mine, out_beside)
    pairs = run(early.paired())

    early.start_last(line.after(pairs))
    piece = run(late.scattered())
    small = end_hop(hop)

    late.start_gather(line.after(piece))
    pairs_far1 = lax.ppermute(line.after(pairs), "pipe", [(0, 1)])
    streams = run(late.gathered())
    far1 = line.after(early.far)

    streams, far1 = lax.optimization_barrier((streams, far1))
    late.start_back(streams)
    parts = spread_out(line.after(folded))
    far1_far = lax.ppermute(line.after(far1), "pipe", [(0, 1)])
    pairs0 = run(late.paired())

    late.start_last(line.after(pairs0))
    pairs_far0 = lax.ppermute(line.after(pairs0), "pipe", [(1, 0)])
    mixed = rest(begun, parts)
    came = swap_cores(mixed)
    in_ready = line(lambda g, m: finish(which, g, m, unfold), grad, (mixed, came))
    in_moved = give_start(in_ready)
    scalars = jnp.stack([core, index, z]).astype(jnp.int32)
    begun = line(lambda *v: write_weights(scalars, 0, v), (pairs0, pairs_far0), (pairs, pairs_far1))
    far0 = line.after(late.far)

    far0_far = lax.ppermute(far0, "pipe", [(1, 0)])
    hop = start_hop()
    g_w1, g_w2 = line(lambda b, *v: write_weights(scalars, 1, v, b), begun, (far0, far0_far), (far1, far1_far))
    small = end_hop(hop)
    hop = start_hop()
    in_mine, in_theirs = line(lambda *v: give_cut(give_pick(*v)), *in_moved)
    in_beside = swap_cores(line.after(in_theirs))
    small = end_hop(hop)
    in_grad = line(give_end, in_mine, in_beside)
    for axis, hop in hops:
        small = line(lambda a, b: a + b, small, lax.ppermute(small, axis, hop))
    small = jnp.where(first, small[0], small[1])
    g_b1 = small[:hidden]
    g_b2, g_mg, g_ms, g_og, g_os = (small[hidden + i * width : hidden + (i + 1) * width] for i in range(5))
    return (
        out,
        in_grad,
        g_w1,
        g_b1[None],
        g_w2,
        g_b2[None],
        g_mg[None],
        g_ms[None],
        g_og[None],
        g_os[None],
    )


def solution(mesh):
    return jax.shard_map(
        on_device,
        mesh=mesh,
        in_specs=(
            P("dp", "seq", None),
            P("dp", "seq", None),
            P("pipe", None, None),
            P("pipe", None),
            P("pipe", None, None),
            P("pipe", None),
            P("pipe", None),
            P("pipe", None),
            P("pipe", None),
            P("pipe", None),
        ),
        out_specs=(
            P("dp", "seq", "pipe"),
            P("dp", "seq", "pipe"),
            P("pipe", None, None),
            P("pipe", None),
            P("pipe", None, None),
            P("pipe", None),
            P("pipe", None),
            P("pipe", None),
            P("pipe", None),
            P("pipe", None),
        ),
        check_vma=False,
    )
```
